32 devices in a mesh: dp: 8 (over z, y), fsdp: 4 (over x, core).
Axes of the slice: x: 2, y: 2, z: 4, core: 2. Of those that a mesh axis runs over, the one named last changes fastest.
Arguments:
- tokens: bfloat16 [12288, 1024], P(('dp', 'fsdp')), may hold values from -6 to 6
- cotangent: bfloat16 [12288, 1024], P(('dp', 'fsdp')), may hold values from -6 to 6
- lengths: int32 [32], P(('dp', 'fsdp')), may hold values from 128 to 384, as said below
- expert_ids: int32 [12288], P(('dp', 'fsdp')), may hold values from 0 to 1, as said below
- slot_ids: int32 [12288], P(('dp', 'fsdp')), may hold values from -1 to 111, as said below
- w_qkv: bfloat16 [1024, 3072], P(('dp', 'fsdp')), may hold values from -0.1875 to 0.1875
- w_out: bfloat16 [1024, 1024], P(('dp', 'fsdp')), may hold values from -3 to 3
- gain_one: bfloat16 [1024], P(('dp', 'fsdp')), may hold values from 0.5 to 1.5
- w_in: bfloat16 [1024, 4096], P(('dp', 'fsdp')), may hold values from -0.1875 to 0.1875
- w_down: bfloat16 [4096, 1024], P(('dp', 'fsdp')), may hold values from -0.09375 to 0.09375
- w_expert_in: bfloat16 [2, 1024, 4096], P(None, ('dp', 'fsdp')), may hold values from -0.1875 to 0.1875
- w_expert_out: bfloat16 [2, 4096, 1024], P(None, ('dp', 'fsdp')), may hold values from -0.09375 to 0.09375
- w_mix: bfloat16 [1024, 2], P(('dp', 'fsdp')), may hold values from -0.1875 to 0.1875
- gain_two: bfloat16 [1024], P(('dp', 'fsdp')), may hold values from 0.5 to 1.5
Outputs:
- block_out: bfloat16 [12288, 1024], P(('dp', 'fsdp'))
- grad_tokens: float32 [12288, 1024], P(('dp', 'fsdp'))
- grad_w_qkv: float32 [1024, 3072], P(('dp', 'fsdp'))
- grad_w_out: float32 [1024, 1024], P(('dp', 'fsdp'))
- grad_gain_one: float32 [1024], P(('dp', 'fsdp'))
- grad_w_in: float32 [1024, 4096], P(('dp', 'fsdp'))
- grad_w_down: float32 [4096, 1024], P(('dp', 'fsdp'))
- grad_w_expert_in: float32 [2, 1024, 4096], P(None, ('dp', 'fsdp'))
- grad_w_expert_out: float32 [2, 4096, 1024], P(None, ('dp', 'fsdp'))
- grad_w_mix: float32 [1024, 2], P(('dp', 'fsdp'))
- grad_gain_two: float32 [1024], P(('dp', 'fsdp'))
The draws below stay inside these ranges and needn't reach their ends.
Inputs may be any that keep to these rules, and one draw needn't show every extreme that they name: `lengths`: each sequence's real tokens; the other positions of its 384 slots are padding. `expert_ids`: each token's expert. `slot_ids`: among the real tokens of one device with the same expert, in order of position, the slots are 0, 1, 2 and so on; tokens whose count reaches 112 and padding tokens have -1.
All inputs are finite; a program needn't handle non-finite values.
Results may differ from the reference program's by a relative error of at most 0.012.
Values may be sent and summed in bfloat16 or wider, within the bound.
A program may use at most 384 MiB of HBM per device.

```python
import jax
import jax.numpy as jnp
from jax import lax

D = 1024
FF = 4096
HEAD_DIM = 64
EXPERTS = 2
TOK_DEV = 384
LEN_MIN = 128
CAP = 112
TOKENS = 12288


def routing_tables(key):
    devices = TOKENS // TOK_DEV
    lengths = jax.random.randint(jax.random.fold_in(key, 11), (devices,), LEN_MIN, TOK_DEV + 1)
    first = jax.random.randint(jax.random.fold_in(key, 12), (), 0, devices)
    offset = jax.random.randint(jax.random.fold_in(key, 13), (), 1, max(devices, 2))
    second = (first + offset) % devices
    lengths = lengths.at[first].set(TOK_DEV).at[second].set(LEN_MIN).astype(jnp.int32)
    positions = jnp.arange(TOK_DEV, dtype=jnp.int32)
    is_valid = positions[None, :] < lengths[:, None]
    busiest = jax.random.randint(jax.random.fold_in(key, 14), (devices,), 0, EXPERTS)
    scores = jax.random.randint(jax.random.fold_in(key, 15), (devices, TOK_DEV), 0, 1 << 20)
    scores = jnp.where(is_valid, scores, 1 << 21)
    ordering = jnp.argsort(scores, axis=1, stable=True)
    rank_within = jnp.argsort(ordering, axis=1, stable=True).astype(jnp.int32)
    random_expert = jax.random.randint(jax.random.fold_in(key, 16), (devices, TOK_DEV), 0, EXPERTS)
    experts = jnp.where(rank_within < LEN_MIN, busiest[:, None], random_expert).astype(jnp.int32)
    onehot = ((experts[:, :, None] == jnp.arange(EXPERTS, dtype=jnp.int32)) & is_valid[:, :, None]).astype(jnp.int32)
    before = jnp.cumsum(onehot, axis=1) - onehot
    slot_raw = jnp.take_along_axis(before, experts[:, :, None], axis=2)[:, :, 0]
    slot_table = jnp.where(is_valid & (slot_raw < CAP), slot_raw, -1).astype(jnp.int32)
    return (lengths, experts.reshape(-1), slot_table.reshape(-1))


def draw_lengths(key, part):
    return routing_tables(key)[0]


def draw_expert_ids(key, part):
    return routing_tables(key)[1]


def draw_slot_ids(key, part):
    return routing_tables(key)[2]


def level_of(stream_key, extent, cuts, smallest, top_value):
    gain, own = 1.0, jax.random.fold_in(stream_key, 6)
    for dim, shards_of in cuts:
        heights = jnp.exp(jax.random.uniform(jax.random.fold_in(own, dim), (shards_of,), jnp.float32, smallest / len(cuts), top_value / len(cuts)))
        gain = gain * jnp.repeat(heights, extent[dim] // shards_of).reshape([-1 if axis == dim else 1 for axis in range(len(extent))])
    return gain


def scatter_about(key, dims, spread, reach, pieces=(), kind=jnp.bfloat16):
    values = spread * jax.random.normal(key, dims, jnp.float32)
    if pieces:
        values = values * level_of(key, dims, pieces, -0.22, 0.18)
    return jnp.clip(values, -reach, reach).astype(kind)


def setup_inputs(seed: int = 0) -> dict:
    streams_of = jax.random.split(jax.random.key(seed), 15)
    tokens = scatter_about(streams_of[0], (TOKENS, D), 1.0, 6.0, ((0, 32),))
    cotangent = scatter_about(streams_of[1], (TOKENS, D), 1.0, 6.0, ((0, 32),))
    lengths = draw_lengths(jax.random.fold_in(streams_of[14], 71), 0)
    expert_ids = draw_expert_ids(jax.random.fold_in(streams_of[14], 71), 0)
    slot_ids = draw_slot_ids(jax.random.fold_in(streams_of[14], 71), 0)
    w_qkv = scatter_about(streams_of[5], (D, 3 * D), D ** -0.5, 0.1875, ((0, 32),))
    w_out = scatter_about(streams_of[6], (D, D), (D // 256) ** -0.5, 3.0, ((0, 32),))
    gain_one = jnp.clip(1.0 + 0.1 * jax.random.normal(streams_of[7], (D,), jnp.float32), 0.5, 1.5).astype(jnp.bfloat16)
    w_in = scatter_about(streams_of[8], (D, FF), D ** -0.5, 0.1875, ((0, 32),))
    w_down = scatter_about(streams_of[9], (FF, D), FF ** -0.5, 0.09375, ((0, 32),))
    w_expert_in = scatter_about(streams_of[10], (EXPERTS, D, FF), D ** -0.5, 0.1875, ((1, 32),))
    w_expert_out = scatter_about(streams_of[11], (EXPERTS, FF, D), FF ** -0.5, 0.09375, ((1, 32),))
    w_mix = scatter_about(streams_of[12], (D, 2), D ** -0.5, 0.1875, ((0, 32),))
    gain_two = jnp.clip(1.0 + 0.1 * jax.random.normal(streams_of[13], (D,), jnp.float32), 0.5, 1.5).astype(jnp.bfloat16)
    return {"tokens": tokens, "cotangent": cotangent, "lengths": lengths, "expert_ids": expert_ids, "slot_ids": slot_ids, "w_qkv": w_qkv, "w_out": w_out, "gain_one": gain_one, "w_in": w_in, "w_down": w_down, "w_expert_in": w_expert_in, "w_expert_out": w_expert_out, "w_mix": w_mix, "gain_two": gain_two}


@jax.custom_vjp
def low(v):
    return lax.optimization_barrier(v.astype(jnp.bfloat16)).astype(jnp.float32)

@jax.custom_vjp
def low_back(v):
    return v

def low_keep(v):
    return (low(v), None)

def low_pass(kept, grad):
    return (grad,)

def back_keep(v):
    return (v, None)

def back_low(kept, grad):
    return (low(grad),)
low.defvjp(low_keep, low_pass)
low_back.defvjp(back_keep, back_low)

def matmul_hi(left, right):
    return jnp.dot(left, right, precision=lax.Precision.HIGHEST, preferred_element_type=jnp.float32)

def layer_norm(values_in, gain_vec):
    average = lax.optimization_barrier(jnp.mean(values_in, axis=-1, keepdims=True))
    centred = values_in - average
    variance = lax.optimization_barrier(jnp.mean(centred * centred, axis=-1, keepdims=True))
    return centred * lax.rsqrt(variance + 1e-05) * gain_vec

def gelu_tanh(values_in):
    return jax.nn.gelu(values_in, approximate=True)

def sequence_forward(stream, seq_len, seq_expert, seq_slot, weights):
    w_qkv, w_out, gain_one, w_in, w_down, w_expert_in, w_expert_out, w_mix, gain_two = weights
    row_count, model_width = stream.shape
    positions = jnp.arange(row_count, dtype=jnp.int32)
    row_keep = (positions < seq_len).astype(jnp.float32)[:, None]
    allowed = (positions[None, :] <= positions[:, None]) & (positions[None, :] < seq_len)
    head_count = model_width // HEAD_DIM
    score_scale = HEAD_DIM ** (-0.5)
    normed_one = low(layer_norm(stream, gain_one))
    qkv_all = low(low_back(matmul_hi(normed_one, w_qkv)))

    def to_heads(block):
        return block.reshape(row_count, head_count, HEAD_DIM).transpose(1, 0, 2)
    queries = to_heads(qkv_all[:, :model_width])
    key_heads = to_heads(qkv_all[:, model_width:2 * model_width])
    value_heads = to_heads(qkv_all[:, 2 * model_width:])

    def head_forward(entries):
        query_h, key_h, value_h = entries
        scores = low_back(jnp.einsum('qd,kd->qk', query_h, key_h, precision=lax.Precision.HIGHEST) * score_scale)
        scores = jnp.where(allowed, scores, -1e+30)
        prob_low = low(jax.nn.softmax(scores, axis=-1))
        return jnp.einsum('qk,kd->qd', prob_low, value_h, precision=lax.Precision.HIGHEST)
    head_out = lax.map(jax.checkpoint(head_forward), (queries, key_heads, value_heads))
    attended = low(low_back(head_out.transpose(1, 0, 2).reshape(row_count, model_width)))
    stream_two = stream + low_back(matmul_hi(attended, w_out))
    normed_two = low(layer_norm(stream_two, gain_two))
    dense_up = low_back(matmul_hi(normed_two, w_in))
    dense_act = low(gelu_tanh(dense_up))
    dense_out = low_back(matmul_hi(dense_act, w_down))
    routed = seq_slot >= 0
    table_row = jnp.where(routed, seq_expert * CAP + seq_slot, 0).astype(jnp.int32)
    dispatch = ((table_row[None, :] == jnp.arange(EXPERTS * CAP, dtype=jnp.int32)[:, None]) & routed[None, :]).astype(jnp.float32)
    buffer = matmul_hi(dispatch, normed_two).reshape(EXPERTS, CAP, model_width)
    expert_up = low_back(jnp.einsum('ecd,edf->ecf', buffer, w_expert_in, precision=lax.Precision.HIGHEST))
    expert_act = low(gelu_tanh(expert_up))
    expert_y = jnp.einsum('ecf,efd->ecd', expert_act, w_expert_out, precision=lax.Precision.HIGHEST)
    expert_y = expert_y.reshape(EXPERTS * CAP, model_width)
    expert_mix = low_back(matmul_hi(dispatch.T, expert_y))
    mix_coeff = jax.nn.softmax(matmul_hi(normed_two, w_mix), axis=-1)
    branch = mix_coeff[:, 0:1] * dense_out + mix_coeff[:, 1:2] * expert_mix
    return (stream_two + branch) * row_keep

def reference(tokens, cotangent, lengths, expert_ids, slot_ids, w_qkv, w_out, gain_one, w_in, w_down, w_expert_in, w_expert_out, w_mix, gain_two):
    seq_count = TOKENS // TOK_DEV
    weights = tuple((w.astype(jnp.float32) for w in (w_qkv, w_out, gain_one, w_in, w_down, w_expert_in, w_expert_out, w_mix, gain_two)))
    stream = tokens.astype(jnp.float32).reshape(seq_count, TOK_DEV, D)
    seq_experts = expert_ids.reshape(seq_count, TOK_DEV)
    seq_slots = slot_ids.reshape(seq_count, TOK_DEV)

    def forward(stream_all, weight_all):

        def seq_step(carried, entries):
            seq_stream, seq_len, seq_expert, seq_slot = entries
            return (carried, sequence_forward(seq_stream, seq_len, seq_expert, seq_slot, weight_all))
        _, outputs = lax.scan(seq_step, jnp.zeros((), jnp.float32), (stream_all, lengths, seq_experts, seq_slots))
        return outputs
    block_out, pullback = jax.vjp(forward, stream, weights)
    grad_stream, grad_weights = pullback(cotangent.astype(jnp.float32).reshape(seq_count, TOK_DEV, D))
    return (block_out.reshape(TOKENS, D).astype(jnp.bfloat16), grad_stream.reshape(TOKENS, D), grad_weights[0], grad_weights[1], grad_weights[2], grad_weights[3], grad_weights[4], grad_weights[5], grad_weights[6], grad_weights[7], grad_weights[8])
```

```python
import jax
import jax.numpy as jnp
from jax import lax
from jax.experimental import pallas as pl
from jax.experimental.pallas import tpu as pltpu
from jax.sharding import PartitionSpec as P

HEAD_DIM = 64
EXPERTS = 2
CAP = 112


def layer_norm(values_in, gain_vec):
    average = jnp.mean(values_in, axis=-1, keepdims=True)
    centred = values_in - average
    variance = jnp.mean(centred * centred, axis=-1, keepdims=True)
    return centred * lax.rsqrt(variance + 1e-05) * gain_vec


def gelu_tanh(values_in):
    return jax.nn.gelu(values_in, approximate=True)


def gelu_back(values_in, grad_in):
    return jax.vjp(gelu_tanh, values_in)[1](grad_in)[0]


def head_scores(query_h, key_h, allowed, score_scale):
    scores = (
        jnp.einsum("qd,kd->qk", query_h, key_h, preferred_element_type=jnp.float32) * score_scale
    )
    return jnp.where(allowed, scores, -1e30)


def head_forward(entries, allowed, score_scale):
    query_h, key_h, value_h = entries
    scores = head_scores(query_h, key_h, allowed, score_scale)
    row_max = jnp.max(scores, axis=-1, keepdims=True)
    exp_scores = jnp.exp(scores - row_max)
    row_total = jnp.sum(exp_scores, axis=-1, keepdims=True)
    prob_low = (exp_scores / row_total).astype(jnp.bfloat16)
    head_out = jnp.dot(prob_low, value_h, preferred_element_type=jnp.float32)
    return (head_out, (row_max + jnp.log(row_total))[:, 0])


def head_backward(entries, allowed, score_scale):
    query_h, key_h, value_h, grad_head, log_total = entries
    scores = head_scores(query_h, key_h, allowed, score_scale)
    prob_full = jnp.where(allowed, jnp.exp(scores - log_total[:, None]), 0.0)
    prob_low = prob_full.astype(jnp.bfloat16)
    grad_value = jnp.einsum("qk,qd->kd", prob_low, grad_head, preferred_element_type=jnp.float32)
    grad_prob = jnp.einsum("qd,kd->qk", grad_head, value_h, preferred_element_type=jnp.float32)
    grad_score = prob_full * (grad_prob - jnp.sum(prob_full * grad_prob, axis=-1, keepdims=True))
    grad_score = grad_score.astype(jnp.bfloat16)
    grad_query = jnp.dot(grad_score, key_h, preferred_element_type=jnp.float32) * score_scale
    grad_key = (
        jnp.einsum("qk,qd->kd", grad_score, query_h, preferred_element_type=jnp.float32)
        * score_scale
    )
    return (grad_query, grad_key, grad_value)


def per_device(
    tokens,
    cotangent,
    lengths,
    expert_ids,
    slot_ids,
    w_qkv,
    w_out,
    gain_one,
    w_in,
    w_down,
    w_expert_in,
    w_expert_out,
    w_mix,
    gain_two,
):
    row_count, model_width = tokens.shape
    head_count = model_width // HEAD_DIM
    score_scale = HEAD_DIM ** (-0.5)
    full_qkv, full_out, full_gain_one = (
        lax.all_gather(w_qkv, ("dp", "fsdp"), axis=0, tiled=True),
        lax.all_gather(w_out, ("dp", "fsdp"), axis=0, tiled=True),
        lax.all_gather(gain_one, ("dp", "fsdp"), axis=0, tiled=True),
    )
    full_in, full_down, full_expert_in, full_expert_out, full_mix, full_gain_two = (
        lax.all_gather(w_in, ("dp", "fsdp"), axis=0, tiled=True),
        lax.all_gather(w_down, ("dp", "fsdp"), axis=0, tiled=True),
        lax.all_gather(w_expert_in, ("dp", "fsdp"), axis=1, tiled=True),
        lax.all_gather(w_expert_out, ("dp", "fsdp"), axis=1, tiled=True),
        lax.all_gather(w_mix, ("dp", "fsdp"), axis=0, tiled=True),
        lax.all_gather(gain_two, ("dp", "fsdp"), axis=0, tiled=True),
    )
    position = jnp.arange(row_count, dtype=jnp.int32)
    seq_len = lengths[0]
    row_keep = (position < seq_len).astype(jnp.float32)[:, None]
    allowed = (position[None, :] <= position[:, None]) & (position[None, :] < seq_len)

    def to_heads(block):
        return block.reshape(row_count, head_count, HEAD_DIM).transpose(1, 0, 2)

    def from_heads(block):
        return block.transpose(1, 0, 2).reshape(row_count, model_width)

    stream = tokens.astype(jnp.float32)
    gain_first = full_gain_one.astype(jnp.float32)
    normed_one = layer_norm(stream, gain_first).astype(jnp.bfloat16)
    qkv_all = jnp.dot(normed_one, full_qkv, preferred_element_type=jnp.float32).astype(jnp.bfloat16)
    queries = to_heads(qkv_all[:, :model_width])
    key_heads = to_heads(qkv_all[:, model_width : 2 * model_width])
    value_heads = to_heads(qkv_all[:, 2 * model_width :])
    head_out, log_total = lax.map(
        lambda entries: head_forward(entries, allowed, score_scale),
        (queries, key_heads, value_heads),
    )
    attended = from_heads(head_out).astype(jnp.bfloat16)
    stream_two = stream + jnp.dot(attended, full_out, preferred_element_type=jnp.float32)
    gain_second = full_gain_two.astype(jnp.float32)
    normed_two = layer_norm(stream_two, gain_second).astype(jnp.bfloat16)
    dense_up = jnp.dot(normed_two, full_in, preferred_element_type=jnp.float32)
    dense_act = gelu_tanh(dense_up).astype(jnp.bfloat16)
    dense_out = jnp.dot(dense_act, full_down, preferred_element_type=jnp.float32)
    routed = slot_ids >= 0
    table_row = jnp.where(routed, expert_ids * CAP + slot_ids, 0)
    slot_total = EXPERTS * CAP
    dispatch = (
        (table_row[None, :] == jnp.arange(slot_total, dtype=jnp.int32)[:, None]) & routed[None, :]
    ).astype(jnp.bfloat16)
    buffer = jnp.dot(dispatch, normed_two, preferred_element_type=jnp.float32).astype(jnp.bfloat16)
    buffer = buffer.reshape(EXPERTS, CAP, model_width)
    expert_up = jnp.einsum(
        "ecd,edf->ecf", buffer, full_expert_in, preferred_element_type=jnp.float32
    )
    expert_act = gelu_tanh(expert_up).astype(jnp.bfloat16)
    expert_y = jnp.einsum(
        "ecf,efd->ecd", expert_act, full_expert_out, preferred_element_type=jnp.float32
    )
    expert_y = expert_y.reshape(slot_total, model_width)
    expert_mix = jnp.where(routed[:, None], expert_y[table_row], 0.0)
    logits = jnp.dot(normed_two, full_mix, preferred_element_type=jnp.float32)
    mix_coeff = jax.nn.softmax(logits, axis=-1)
    branch = mix_coeff[:, 0:1] * dense_out + mix_coeff[:, 1:2] * expert_mix
    block_out = ((stream_two + branch) * row_keep).astype(jnp.bfloat16)
    grad_out = cotangent.astype(jnp.float32) * row_keep
    grad_dense = (mix_coeff[:, 0:1] * grad_out).astype(jnp.bfloat16)
    grad_expert = (mix_coeff[:, 1:2] * grad_out).astype(jnp.bfloat16)
    grad_coeff = jnp.stack(
        [jnp.sum(grad_out * dense_out, axis=-1), jnp.sum(grad_out * expert_mix, axis=-1)], axis=-1
    )
    grad_logits = jax.vjp(lambda values_in: jax.nn.softmax(values_in, axis=-1), logits)[1](
        grad_coeff
    )[0]
    full_in, full_down, full_expert_in, full_expert_out, full_mix, full_gain_two = (
        lax.all_gather(w_in, ("dp", "fsdp"), axis=0, tiled=True),
        lax.all_gather(w_down, ("dp", "fsdp"), axis=0, tiled=True),
        lax.all_gather(w_expert_in, ("dp", "fsdp"), axis=1, tiled=True),
        lax.all_gather(w_expert_out, ("dp", "fsdp"), axis=1, tiled=True),
        lax.all_gather(w_mix, ("dp", "fsdp"), axis=0, tiled=True),
        lax.all_gather(gain_two, ("dp", "fsdp"), axis=0, tiled=True),
    )
    gain_second = full_gain_two.astype(jnp.float32)
    grad_w_down = jnp.einsum("tf,td->fd", dense_act, grad_dense, preferred_element_type=jnp.float32)
    grad_dense_act = jnp.einsum(
        "td,fd->tf", grad_dense, full_down, preferred_element_type=jnp.float32
    )
    grad_dense_up = gelu_back(dense_up, grad_dense_act).astype(jnp.bfloat16)
    grad_w_in = jnp.einsum(
        "td,tf->df", normed_two, grad_dense_up, preferred_element_type=jnp.float32
    )
    grad_normed_two = jnp.einsum(
        "tf,df->td", grad_dense_up, full_in, preferred_element_type=jnp.float32
    )
    grad_y = jnp.dot(dispatch, grad_expert, preferred_element_type=jnp.float32).astype(jnp.bfloat16)
    grad_y = grad_y.reshape(EXPERTS, CAP, model_width)
    grad_expert_out_lead = jnp.einsum(
        "ecf,ecd->fed", expert_act, grad_y, preferred_element_type=jnp.float32
    )
    grad_expert_act = jnp.einsum(
        "ecd,efd->ecf", grad_y, full_expert_out, preferred_element_type=jnp.float32
    )
    grad_expert_up = gelu_back(expert_up, grad_expert_act).astype(jnp.bfloat16)
    grad_expert_in_lead = jnp.einsum(
        "ecd,ecf->def", buffer, grad_expert_up, preferred_element_type=jnp.float32
    )
    grad_buffer = jnp.einsum(
        "ecf,edf->ecd", grad_expert_up, full_expert_in, preferred_element_type=jnp.float32
    )
    grad_buffer = grad_buffer.reshape(slot_total, model_width)
    grad_normed_two = grad_normed_two + jnp.where(routed[:, None], grad_buffer[table_row], 0.0)
    mix_full = full_mix.astype(jnp.float32)
    normed_full = normed_two.astype(jnp.float32)
    grad_normed_two = grad_normed_two + jnp.dot(
        grad_logits, mix_full.T, precision=lax.Precision.HIGHEST
    )
    grad_w_mix = jnp.dot(normed_full.T, grad_logits, precision=lax.Precision.HIGHEST)
    _, pull_two = jax.vjp(layer_norm, stream_two, gain_second)
    grad_stream_ln, grad_gain_two = pull_two(grad_normed_two)
    grad_stream_two = grad_out + grad_stream_ln
    full_qkv, full_out, full_gain_one = (
        lax.all_gather(w_qkv, ("dp", "fsdp"), axis=0, tiled=True),
        lax.all_gather(w_out, ("dp", "fsdp"), axis=0, tiled=True),
        lax.all_gather(gain_one, ("dp", "fsdp"), axis=0, tiled=True),
    )
    gain_first = full_gain_one.astype(jnp.float32)
    grad_attn = grad_stream_two.astype(jnp.bfloat16)
    grad_w_out = jnp.einsum("td,te->de", attended, grad_attn, preferred_element_type=jnp.float32)
    grad_attended = jnp.einsum(
        "te,de->td", grad_attn, full_out, preferred_element_type=jnp.float32
    ).astype(jnp.bfloat16)
    grad_query, grad_key, grad_value = lax.map(
        lambda entries: head_backward(entries, allowed, score_scale),
        (queries, key_heads, value_heads, to_heads(grad_attended), log_total),
    )
    grad_qkv = jnp.concatenate(
        [from_heads(grad_query), from_heads(grad_key), from_heads(grad_value)], axis=1
    ).astype(jnp.bfloat16)
    grad_w_qkv = jnp.einsum("td,te->de", normed_one, grad_qkv, preferred_element_type=jnp.float32)
    grad_normed_one = jnp.einsum(
        "te,de->td", grad_qkv, full_qkv, preferred_element_type=jnp.float32
    )
    _, pull_one = jax.vjp(layer_norm, stream, gain_first)
    grad_stream_one, grad_gain_one = pull_one(grad_normed_one)
    grad_tokens = grad_stream_two + grad_stream_one
    (
        part_qkv,
        part_out,
        part_gain_one,
        part_in,
        part_down,
        lead_expert_in,
        lead_expert_out,
        part_mix,
        part_gain_two,
    ) = (
        lax.psum_scatter(grad_w_qkv, ("dp", "fsdp"), scatter_dimension=0, tiled=True),
        lax.psum_scatter(grad_w_out, ("dp", "fsdp"), scatter_dimension=0, tiled=True),
        lax.psum_scatter(grad_gain_one, ("dp", "fsdp"), scatter_dimension=0, tiled=True),
        lax.psum_scatter(grad_w_in, ("dp", "fsdp"), scatter_dimension=0, tiled=True),
        lax.psum_scatter(grad_w_down, ("dp", "fsdp"), scatter_dimension=0, tiled=True),
        lax.psum_scatter(grad_expert_in_lead, ("dp", "fsdp"), scatter_dimension=0, tiled=True),
        lax.psum_scatter(grad_expert_out_lead, ("dp", "fsdp"), scatter_dimension=0, tiled=True),
        lax.psum_scatter(grad_w_mix, ("dp", "fsdp"), scatter_dimension=0, tiled=True),
        lax.psum_scatter(grad_gain_two, ("dp", "fsdp"), scatter_dimension=0, tiled=True),
    )
    part_expert_in = lead_expert_in.transpose(1, 0, 2)
    part_expert_out = lead_expert_out.transpose(1, 0, 2)
    return (
        block_out,
        grad_tokens,
        part_qkv,
        part_out,
        part_gain_one,
        part_in,
        part_down,
        part_expert_in,
        part_expert_out,
        part_mix,
        part_gain_two,
    )


BF = jnp.bfloat16
F32 = jnp.float32
MESH = pl.DeviceIdType.MESH
ANY = pl.BlockSpec(memory_space=pl.ANY)
VM = pl.BlockSpec(memory_space=pltpu.VMEM)
SM = pl.BlockSpec(memory_space=pltpu.SMEM)
MIB = 1024 * 1024


def dot_nn(a, b):
    return lax.dot_general(a, b, (((1,), (0,)), ((), ())), preferred_element_type=F32)


def dot_nt(a, b):
    return lax.dot_general(a, b, (((1,), (1,)), ((), ())), preferred_element_type=F32)


def dot_tn(a, b):
    return lax.dot_general(a, b, (((0,), (0,)), ((), ())), preferred_element_type=F32)


class Place:
    def __init__(self):
        dp, fs = lax.axis_index("dp"), lax.axis_index("fsdp")
        z, y, x, c = dp // 2, dp % 2, fs // 2, fs % 2
        self.z, self.y, self.x, self.c = z, y, x, c
        self.own = (y, x, c)
        self.sib = (y, x, 1 - c)
        self.d1 = ((y + c) % 2, (x + 1 - c) % 2, c)
        self.d2 = ((y + 1 - c) % 2, (x + c) % 2, c)
        self.dd = (1 - y, 1 - x, c)
        self.zk = [z, z + 1 - 2 * (z % 2), (z + 2) % 4, 3 - z]
        self.t = self.rank(self.own)
        self.b = z * 8 + self.t

    @staticmethod
    def rank(p):
        return p[0] * 4 + p[1] * 2 + p[2]

    def flip(self, p):
        return (p[0], p[1], 1 - p[2])

    def dev(self, p, z=None):
        z = self.z if z is None else z
        return (z * 2 + p[0], p[1] * 2 + p[2])

    def plane_others(self):
        y, x, c = self.own
        return [
            ((y + k // 4) % 2, (x + (k // 2) % 2) % 2, (c + k % 2) % 2) for k in range(1, 8)
        ]


def rcopy(src, dst, send, recv, dev):
    return pltpu.make_async_remote_copy(
        src_ref=src, dst_ref=dst, send_sem=send, recv_sem=recv, device_id=dev, device_id_type=MESH
    )


def meet(devs):
    bar = pltpu.get_barrier_semaphore()
    for dev in devs:
        pl.semaphore_signal(bar, inc=1, device_id=dev, device_id_type=MESH)
    pl.semaphore_wait(bar, len(devs))


def norm_parts(v):
    mean = jnp.mean(v, axis=-1, keepdims=True)
    cen = v - mean
    var = jnp.mean(cen * cen, axis=-1, keepdims=True)
    r = lax.rsqrt(var + 1e-05)
    return cen * r, r


def row_of(extra, lane):
    pick = (lax.broadcasted_iota(jnp.int32, (8, 128), 1) == lane).astype(BF)
    return dot_nt(pick, extra)[0:1]


PW = 4224
EX = 3072
WO = 3200


def enter_kernel(
    len_ref, tok, pack, wia, wdn, gt,
    qkv, lse, att, s2, nt, n1, wmix, pack_all, wi_all, wd_all, g_all,
    pack_v, ps, pr, asend, arecv, fsend, fri, frd, gs, gr, lsem,
):
    P_ = Place()
    z, t, b = P_.z, P_.t, P_.b
    own, sib, d1, d2, dd = P_.own, P_.sib, P_.d1, P_.d2, P_.dd
    others = P_.plane_others()
    meet([P_.dev(p) for p in others] + [P_.dev(own, zz) for zz in P_.zk[1:]])
    sends = []

    def go(cp):
        cp.start()
        sends.append(cp)

    lc = pltpu.make_async_copy(pack, pack_v.at[b], lsem.at[0])
    lc.start()
    for k in range(1, 4):
        go(rcopy(pack, pack_v.at[b], ps.at[k - 1], pr.at[b], P_.dev(own, P_.zk[k])))
    go(rcopy(pack, pack_v.at[b], ps.at[3], pr.at[b], P_.dev(d1)))
    go(rcopy(pack, pack_v.at[b], ps.at[7], pr.at[b], P_.dev(d2)))
    go(rcopy(pack, pack_v.at[b], ps.at[15], pr.at[b], P_.dev(sib)))
    rows = pl.ds(pl.multiple_of(t * 32, 32), 32)
    lw = pltpu.make_async_copy(wia.at[t], wi_all.at[:, z, rows], lsem.at[1])
    lw.start()
    for i, p in enumerate(others):
        go(rcopy(wia.at[P_.rank(p)], wi_all.at[:, z, rows], asend.at[i], arecv.at[t], P_.dev(p)))
    ld = pltpu.make_async_copy(wdn, wd_all.at[:, z], lsem.at[2])
    ld.start()

    def landed(slot):
        rcopy(pack, pack_v.at[slot], ps.at[0], pr.at[slot], P_.dev(sib)).wait_recv()

    def fwd(slot, sem, p):
        go(rcopy(pack_v.at[slot], pack_v.at[slot], ps.at[sem], pr.at[slot], P_.dev(p)))

    def slot(k, p):
        return P_.zk[k] * 8 + P_.rank(p)

    for k in range(0, 6):
        if 1 <= k <= 3:
            s = slot(k, own)
            landed(s)
            fwd(s, 3 + k, d1)
            fwd(s, 7 + k, d2)
            fwd(s, 15 + k, sib)
        if k == 3:
            lw.wait()
            ld.wait()
            for p in others:
                rr = P_.rank(p)
                rq = pl.ds(pl.multiple_of(rr * 32, 32), 32)
                rcopy(
                    wia.at[0], wi_all.at[:, z, rq], asend.at[0], arecv.at[rr], P_.dev(sib)
                ).wait_recv()
            for kd in range(3):
                for j in range(1, 4):
                    zz = P_.dev(own, P_.zk[j])
                    i = kd * 6 + (j - 1) * 2
                    go(rcopy(wi_all.at[kd, z], wi_all.at[kd, z], fsend.at[i], fri.at[kd, z], zz))
                    go(rcopy(wdn.at[kd], wd_all.at[kd, z], fsend.at[i + 1], frd.at[kd, z], zz))
        if 1 <= k <= 4:
            s = slot(k - 1, d1)
            landed(s)
            fwd(s, 11 + k - 1, d2)
            fwd(s, 19 + k - 1, sib)
            s = slot(k - 1, d2)
            landed(s)
            fwd(s, 23 + k - 1, sib)
        if k >= 2:
            s = slot(k - 2, dd)
            landed(s)
            fwd(s, 27 + k - 2, sib)
    lg = pltpu.make_async_copy(gt, g_all.at[t], lsem.at[3])
    lg.start()
    for i, p in enumerate((d1, d2, sib)):
        go(rcopy(gt, g_all.at[t], gs.at[i], gr.at[t], P_.dev(p)))
    stream = tok[...].astype(F32)
    for k in range(4):
        for p in (own, d1, d2, dd):
            landed(slot(k, P_.flip(p)))
    lc.wait()
    keep_all = pltpu.make_async_copy(pack_v, pack_all, lsem.at[0])
    keep_all.start()

    extra = pack_v[:, :, EX : EX + 128].reshape(1024, 128)
    wmix[...] = extra
    n_one, _ = norm_parts(stream)
    n1[...] = (n_one * row_of(extra, 2)).astype(BF)

    def qkv_step(j, carry):
        cols = pl.ds(pl.multiple_of(j * 512, 512), 512)
        qkv[:, cols] = dot_nn(n1[...], pack_v[:, :, cols].reshape(1024, 512)).astype(BF)
        return carry

    lax.fori_loop(0, 6, qkv_step, 0)

    def g_landed(p):
        r = P_.rank(p)
        rcopy(gt, g_all.at[r], gs.at[0], gr.at[r], P_.dev(sib)).wait_recv()
        return r

    def g_fwd(r, i, p):
        go(rcopy(g_all.at[r], g_all.at[r], gs.at[i], gr.at[r], P_.dev(p)))

    r = g_landed(d1)
    g_fwd(r, 3, d2)
    g_fwd(r, 4, sib)

    allowed = masks(len_ref[0])
    lane = lax.broadcasted_iota(jnp.int32, (384, 128), 1)
    lse[...] = jnp.zeros_like(lse)

    def pair_step(p, carry):
        q2 = qkv[:, pl.ds(pl.multiple_of(p * 128, 128), 128)]
        k2 = qkv[:, pl.ds(pl.multiple_of(1024 + p * 128, 128), 128)]
        v2 = qkv[:, pl.ds(pl.multiple_of(2048 + p * 128, 128), 128)]
        outs = []
        for hh in range(2):
            qm = jnp.where(lane // 64 == hh, q2, jnp.zeros_like(q2))
            sc = jnp.where(allowed, dot_nt(qm, k2) * 0.125, -1e30)
            top = jnp.max(sc, axis=-1, keepdims=True)
            ex = jnp.exp(sc - top)
            tot = jnp.sum(ex, axis=-1, keepdims=True)
            outs.append(dot_nn((ex * (1.0 / tot)).astype(BF), v2))
            lse[...] = jnp.where(lane == 2 * p + hh, top + jnp.log(tot), lse[...])
        att[:, pl.ds(pl.multiple_of(p * 128, 128), 128)] = jnp.where(
            lane < 64, outs[0], outs[1]
        ).astype(BF)
        return carry

    lax.fori_loop(0, 8, pair_step, 0)
    r = g_landed(d2)
    g_fwd(r, 5, sib)
    for j in range(2):
        w = pack_v[:, :, WO + j * 512 : WO + (j + 1) * 512].reshape(1024, 512)
        s2[:, j * 512 : (j + 1) * 512] = stream[:, j * 512 : (j + 1) * 512] + dot_nn(att[...], w)
    n_two, _ = norm_parts(s2[...])
    nt[...] = (n_two * row_of(extra, 3)).astype(BF)
    r = g_landed(dd)
    g_fwd(r, 6, sib)
    for p in (own, d1, d2, dd):
        g_landed(P_.flip(p))
    for kd in range(3):
        for j in range(1, 4):
            zz = P_.zk[j]
            rcopy(wi_all.at[kd, zz], wi_all.at[kd, zz], fsend.at[0], fri.at[kd, zz], P_.dev(sib)).wait_recv()
            rcopy(wdn.at[kd], wd_all.at[kd, zz], fsend.at[0], frd.at[kd, zz], P_.dev(sib)).wait_recv()
    lg.wait()
    keep_all.wait()
    for cp in sends:
        cp.wait_send()


def masks(seq_len):
    row = lax.broadcasted_iota(jnp.int32, (384, 384), 0)
    col = lax.broadcasted_iota(jnp.int32, (384, 384), 1)
    return (col <= row) & (col < seq_len)


def run_enter(lengths, tok, pack, wia, wdn, gt):
    sd = jax.ShapeDtypeStruct
    return pl.pallas_call(
        enter_kernel,
        out_shape=(
            sd((384, 3072), BF), sd((384, 128), F32), sd((384, 1024), BF), sd((384, 1024), F32),
            sd((384, 1024), BF), sd((384, 1024), BF), sd((1024, 128), BF),
            sd((32, 32, PW), BF), sd((3, 4, 256, 512), BF), sd((3, 4, 128, 1024), BF),
            sd((8, 400, 1024), BF),
        ),
        in_specs=[SM, VM, ANY, ANY, ANY, ANY],
        out_specs=(VM,) * 7 + (ANY,) * 4,
        scratch_shapes=[
            pltpu.VMEM((32, 32, PW), BF),
            pltpu.SemaphoreType.DMA((31,)), pltpu.SemaphoreType.DMA((32,)),
            pltpu.SemaphoreType.DMA((7,)), pltpu.SemaphoreType.DMA((8,)),
            pltpu.SemaphoreType.DMA((18,)), pltpu.SemaphoreType.DMA((3, 4)),
            pltpu.SemaphoreType.DMA((3, 4)),
            pltpu.SemaphoreType.DMA((7,)), pltpu.SemaphoreType.DMA((8,)),
            pltpu.SemaphoreType.DMA((4,)),
        ],
        compiler_params=pltpu.CompilerParams(
            collective_id=0, has_side_effects=True, vmem_limit_bytes=48 * MIB
        ),
    )(lengths, tok, pack, wia, wdn, gt)


def mix_of(logits):
    delta = logits[:, 0:1] - logits[:, 1:2]
    return 1.0 / (1.0 + jnp.exp(-delta)), 1.0 / (1.0 + jnp.exp(delta))


def gelu_both(u):
    a, bb = 0.7978845608028654, 0.044715
    u2 = u * u
    th = jnp.tanh(a * u * (1.0 + bb * u2))
    half = 0.5 * (1.0 + th)
    return u * half, half + 0.5 * u * (1.0 - th * th) * a * (1.0 + 3.0 * bb * u2)


def ff_kernel(
    len_ref, nt_own, wmix, s2, g_all, wi_all, wd_all,
    block, gsum, gl_out, gdo, gx, r1, r2, rin, rdn,
    nt_all, gbuf, br, gn, xb, yb, logit, wi, wd, ai, ad, gin, gdn, tmp, gc, gcr, dots, tabs,
    ts, tr, gsem, wsem, fs_, fri, frd, s1s, s1r, s2s, s2r, cs, cr, xsd, xrv, lsem,
):
    P_ = Place()
    z, t = P_.z, P_.t
    own, sib, d1, d2, dd = P_.own, P_.sib, P_.d1, P_.d2, P_.dd
    others = P_.plane_others()
    meet([P_.dev(p) for p in others] + [P_.dev(own, zz) for zz in P_.zk[1:]])
    sends = []

    def go(cp):
        cp.start()
        sends.append(cp)

    ln = pltpu.make_async_copy(nt_own, nt_all.at[t], lsem.at[1])
    ln.start()
    for i, p in enumerate((d1, d2, sib)):
        go(rcopy(nt_own, nt_all.at[t], ts.at[i], tr.at[t], P_.dev(p)))
    def w_load(kd):
        return (
            pltpu.make_async_copy(wi_all.at[kd], wi.at[kd % 2], wsem.at[kd, 0]),
            pltpu.make_async_copy(wd_all.at[kd], wd.at[kd % 2], wsem.at[kd, 1]),
        )

    for kd in range(2):
        for cp in w_load(kd):
            cp.start()

    g_tab = pltpu.make_async_copy(g_all.at[:, 384:400], tabs, lsem.at[2])
    g_tab.start()
    s2_in = pltpu.make_async_copy(s2, gsum, lsem.at[3])
    s2_in.start()

    def w_landed(kd):
        for cp in w_load(kd):
            cp.wait()

    order = (own, sib, d1, P_.flip(d2), d2, P_.flip(d1), dd, P_.flip(dd))
    ranks = [P_.rank(p) for p in order]

    def seq_at(i):
        s = ranks[0]
        for k in range(1, 8):
            s = jnp.where(i == k, ranks[k], s)
        return s

    def g_copy(i):
        return pltpu.make_async_copy(g_all.at[seq_at(i)], gbuf.at[i % 2], gsem.at[i % 2])

    def ff(xv, gv, kd):
        wiv = wi[kd % 2].reshape(1024, 512)
        wdv = wd[kd % 2].reshape(512, 1024)
        act, dact = gelu_both(dot_nn(xv, wiv))
        act = act.astype(BF)
        gup = (dact * dot_nt(gv, wdv)).astype(BF)
        ad[...] += dot_tn(act, gv)
        ai[...] += dot_tn(xv, gup)
        return dot_nn(act, wdv), dot_nt(gup, wiv)

    lane = lax.broadcasted_iota(jnp.int32, (448, 128), 1)

    def clear():
        ad[...] = jnp.zeros_like(ad)
        ai[...] = jnp.zeros_like(ai)

    def ship(kd):
        gin[kd] = ai[...].astype(BF).reshape(4, 256, 512)
        gdn[kd] = ad[...].astype(BF).reshape(4, 128, 1024)
        for j in range(1, 4):
            zz = P_.zk[j]
            i = kd * 6 + (j - 1) * 2
            go(rcopy(gin.at[kd, zz], rin.at[kd, j - 1], fs_.at[i], fri.at[kd, j - 1], P_.dev(own, zz)))
            go(rcopy(gdn.at[kd, zz], rdn.at[kd, j - 1], fs_.at[i + 1], frd.at[kd, j - 1], P_.dev(own, zz)))

    def shares(tab, e):
        slot = lax.broadcasted_iota(jnp.int32, (112, 384), 0) + e * 112
        return (tab == slot.astype(F32)).astype(BF)

    fwds = {2: (d1, ((3, d2), (4, sib))), 4: (d2, ((5, sib),)), 6: (dd, ((6, sib),))}

    def fwd_copy(p, i, q):
        r = P_.rank(p)
        return rcopy(nt_all.at[r], nt_all.at[r], ts.at[i], tr.at[r], P_.dev(q))

    g_copy(0).start()
    clear()
    w_landed(0)
    ln.wait()

    def seq_step(i, carry):
        s = seq_at(i)

        @pl.when(i + 1 < 8)
        def _():
            g_copy(i + 1).start()

        @pl.when(i > 0)
        def _():
            rcopy(nt_own, nt_all.at[s], ts.at[0], tr.at[s], P_.dev(sib)).wait_recv()

        for k, (p, dests) in fwds.items():

            @pl.when(i == k)
            def _():
                for n, q in dests:
                    fwd_copy(p, n, q).start()

        g_copy(i).wait()
        xv = nt_all[s]
        gv = gbuf[i % 2, :384]
        tab = gbuf[i % 2, 384:400][0:1, :384].astype(F32)
        lg = dot_nn(xv, wmix[...])
        logit[s] = lg
        m0, m1 = mix_of(lg)
        gf = gv.astype(F32)
        out, gxv = ff(xv, (m0 * gf).astype(BF), 0)
        br[s] = (m0 * out).astype(BF)
        gn[s] = gxv.astype(BF)
        col = jnp.broadcast_to(jnp.sum(gf * out, axis=-1, keepdims=True), (384, 128))
        gc[s, 0:8] = jnp.transpose(col)[0:8]
        ge = (m1 * gf).astype(BF)
        for e in range(2):
            sh = shares(tab, e)
            xb[e, s] = dot_nn(sh, xv).astype(BF)
            yb[e, s] = dot_nn(sh, ge).astype(BF)
        return carry

    lax.fori_loop(0, 8, seq_step, 0)
    for k, (p, dests) in fwds.items():
        for n, q in dests:
            fwd_copy(p, n, q).wait_send()
    for cp in w_load(2):
        cp.start()
    ship(0)

    for e in range(2):
        clear()
        w_landed(1 + e)

        def ex_step(q, carry):
            four = pl.ds(q * 4, 4)
            gq = yb[e, four].reshape(448, 1024)
            yv, gb = ff(xb[e, four].reshape(448, 1024), gq, 1 + e)
            rs = jnp.sum(gq.astype(F32) * yv, axis=-1, keepdims=True)
            high = rs.astype(BF).astype(F32)
            dots[e, four] = (
                jnp.where(lane == 0, high, jnp.where(lane == 1, rs - high, 0.0))
                .astype(BF)
                .reshape(4, 112, 128)
            )
            xb[e, four] = yv.astype(BF).reshape(4, 112, 1024)
            yb[e, four] = gb.astype(BF).reshape(4, 112, 1024)
            return carry

        lax.fori_loop(0, 2, ex_step, 0)
        ship(1 + e)

    g_tab.wait()

    def mix_step(s, carry):
        tab = tabs[s][0:1, :384].astype(F32)
        _, m1 = mix_of(logit[s])
        s0, s1 = shares(tab, 0), shares(tab, 1)
        em = dot_tn(s0, xb[0, s]) + dot_tn(s1, xb[1, s])
        gb = dot_tn(s0, yb[0, s]) + dot_tn(s1, yb[1, s])
        q1 = dot_tn(s0, dots[0, s]) + dot_tn(s1, dots[1, s])
        gc[s, 8:16] = jnp.transpose(jnp.broadcast_to(q1[:, 0:1] + q1[:, 1:2], (384, 128)))[0:8]
        br[s] = (br[s].astype(F32) + m1 * em).astype(BF)
        gn[s] = (gn[s].astype(F32) + gb).astype(BF)
        return carry

    lax.fori_loop(0, 8, mix_step, 0)
    for i, p in enumerate(others):
        go(rcopy(gc.at[P_.rank(p)], gcr.at[t], cs.at[i], cr.at[t], P_.dev(p)))

    chips = (dd, d1, d2, own)
    both = (gn, br)
    for q in range(4):
        r = P_.rank(P_.flip(chips[q]))
        for w in range(2):
            i = w * 4 + q
            go(rcopy(both[w].at[r], r1.at[w, (0, 2, 1, 3)[q]], s1s.at[i], s1r.at[w, (0, 2, 1, 3)[q]], P_.dev(sib)))

    def add_in(w, r, src):
        cp = pltpu.make_async_copy(src, tmp, lsem.at[0])
        cp.start()
        cp.wait()
        both[w][r] = (both[w][r].astype(F32) + tmp[...].astype(F32)).astype(BF)

    def in1(w, q):
        rcopy(nt_own, r1.at[w, q], s1s.at[0], s1r.at[w, q], P_.dev(sib)).wait_recv()
        add_in(w, P_.rank(chips[q]), r1.at[w, q])

    def out2(w, q, k, p):
        src = both[w].at[P_.rank(chips[q])]
        go(rcopy(src, r2.at[w, k], s2s.at[w * 3 + k], s2r.at[w, k], P_.dev(p)))

    def in2(w, k, p):
        rcopy(nt_own, r2.at[w, k], s2s.at[0], s2r.at[w, k], P_.dev(sib)).wait_recv()
        add_in(w, P_.rank(p), r2.at[w, k])

    for w in range(2):
        in1(w, 0)
        out2(w, 0, 0, d2)
        in1(w, 2)
        out2(w, 2, 2, d2)
        in1(w, 1)
        in1(w, 3)
    for w in range(2):
        in2(w, 0, d1)
        out2(w, 1, 1, d1)
    for w in range(2):
        in2(w, 2, own)
        in2(w, 1, own)
    s2_in.wait()
    branch = br[t].astype(F32)
    keep = (lax.broadcasted_iota(jnp.int32, (384, 1), 0) < len_ref[0]).astype(F32)
    block[...] = ((gsum[...] + branch) * keep).astype(BF)
    gsum[...] = gn[t].astype(F32)
    for p in others:
        r = P_.rank(p)
        rcopy(gc.at[0], gcr.at[r], cs.at[0], cr.at[r], P_.dev(sib)).wait_recv()
    gcr[t] = gc[t]
    tot = jnp.sum(gcr[...], axis=0)
    gc0 = jnp.transpose(jnp.broadcast_to(tot[0:1], (128, 384)))
    q1 = jnp.transpose(jnp.broadcast_to(tot[8:9], (128, 384)))
    m0, m1 = mix_of(logit[t])
    gl_out[...] = m0 * (m1 * gc0 - q1)

    for kd in range(3):
        acc_i = gin[kd, z].astype(F32)
        acc_d = gdn[kd, z].astype(F32)
        for j in range(3):
            rcopy(gin.at[kd, 0], rin.at[kd, j], fs_.at[0], fri.at[kd, j], P_.dev(sib)).wait_recv()
            rcopy(gdn.at[kd, 0], rdn.at[kd, j], fs_.at[0], frd.at[kd, j], P_.dev(sib)).wait_recv()
            li = pltpu.make_async_copy(rin.at[kd, j], nt_all.at[j, 0:256, 0:512], lsem.at[0])
            lj = pltpu.make_async_copy(rdn.at[kd, j], nt_all.at[3, 0:128], lsem.at[1])
            li.start()
            lj.start()
            li.wait()
            lj.wait()
            acc_i += nt_all[j, 0:256, 0:512].astype(F32)
            acc_d += nt_all[3, 0:128].astype(F32)
        gin[kd, z] = acc_i.astype(BF)
        ad[kd * 128 : (kd + 1) * 128] = acc_d
    lgd = pltpu.make_async_copy(ad.at[0:384], gdo, lsem.at[0])
    lgd.start()

    def rows(p):
        return pl.ds(pl.multiple_of(P_.rank(p) * 32, 32), 32)

    lx = pltpu.make_async_copy(gin.at[:, z, rows(own)], gx.at[t], lsem.at[1])
    lx.start()
    for i, p in enumerate(others):
        go(rcopy(gin.at[:, z, rows(p)], gx.at[t], xsd.at[i], xrv.at[t], P_.dev(p)))
    for p in others:
        r = P_.rank(p)
        rcopy(gin.at[:, z, rows(own)], gx.at[r], xsd.at[0], xrv.at[r], P_.dev(sib)).wait_recv()
    lx.wait()
    lgd.wait()
    for cp in sends:
        cp.wait_send()


def run_ff(lengths, nt, wmix, s2, g_all, wi_all, wd_all):
    sd = jax.ShapeDtypeStruct
    dma = pltpu.SemaphoreType.DMA
    out = pl.pallas_call(
        ff_kernel,
        out_shape=(
            sd((384, 1024), BF), sd((384, 1024), F32), sd((384, 128), F32), sd((384, 1024), F32),
            sd((8, 3, 32, 512), BF), sd((2, 4, 384, 1024), BF), sd((2, 3, 384, 1024), BF),
            sd((3, 3, 256, 512), BF), sd((3, 3, 128, 1024), BF),
        ),
        in_specs=[SM, ANY, VM, ANY, ANY, ANY, ANY],
        out_specs=(VM,) * 3 + (ANY,) * 6,
        scratch_shapes=[
            pltpu.VMEM((8, 384, 1024), BF), pltpu.VMEM((2, 400, 1024), BF),
            pltpu.VMEM((8, 384, 1024), BF), pltpu.VMEM((8, 384, 1024), BF),
            pltpu.VMEM((2, 8, 112, 1024), BF), pltpu.VMEM((2, 8, 112, 1024), BF),
            pltpu.VMEM((8, 384, 128), F32),
            pltpu.VMEM((2, 4, 256, 512), BF), pltpu.VMEM((2, 4, 128, 1024), BF),
            pltpu.VMEM((1024, 512), F32), pltpu.VMEM((512, 1024), F32),
            pltpu.VMEM((3, 4, 256, 512), BF), pltpu.VMEM((3, 4, 128, 1024), BF),
            pltpu.VMEM((384, 1024), BF),
            pltpu.VMEM((8, 16, 384), F32), pltpu.VMEM((8, 16, 384), F32), pltpu.VMEM((2, 8, 112, 128), BF),
            pltpu.VMEM((8, 16, 1024), BF),
            dma((7,)), dma((8,)), dma((2,)), dma((3, 2)), dma((18,)), dma((3, 3)), dma((3, 3)),
            dma((8,)), dma((2, 4)), dma((6,)), dma((2, 3)), dma((7,)), dma((8,)),
            dma((7,)), dma((8,)), dma((4,)),
        ],
        compiler_params=pltpu.CompilerParams(
            collective_id=1, has_side_effects=True, vmem_limit_bytes=63 * MIB
        ),
    )(lengths, nt, wmix, s2, g_all, wi_all, wd_all)
    return out[:5]


def back_kernel(
    len_ref, tok, gt, s2, nt, n1, qkv, lse, att, gsum, gl, pack_all,
    gtok, gpack,
    pack_v, gq, gacc, gst, rs1, rs2, rs3, s1s, s1r, s2s, s2r, s3s, s3r, lsem,
):
    P_ = Place()
    z, t, b, c = P_.z, P_.t, P_.b, P_.c
    own, sib, d1, d2, dd = P_.own, P_.sib, P_.d1, P_.d2, P_.dd
    meet([P_.dev(p) for p in (d1, d2, sib)] + [P_.dev(own, zz) for zz in P_.zk[1:]])
    sends = []

    def go(cp):
        cp.start()
        sends.append(cp)

    lw = pltpu.make_async_copy(pack_all, pack_v, lsem.at[0])
    lw.start()
    lw.wait()
    extra = pack_v[:, :, EX : EX + 128].reshape(1024, 128)
    lane = lax.broadcasted_iota(jnp.int32, (384, 128), 1)
    glv = gl[...]
    gnt = gsum[...] + glv[:, 0:1] * (row_of(extra, 0) - row_of(extra, 1))
    two = jnp.where(lane == 0, glv, jnp.where(lane == 1, -glv, 0.0)).astype(BF)
    n_two, r_two = norm_parts(s2[...])
    gain_two_row = jnp.sum(gnt * n_two, axis=0, keepdims=True)

    def norm_back(gv, gain, n, r):
        tt = gv * gain
        return r * (tt - jnp.mean(tt, -1, keepdims=True) - n * jnp.mean(tt * n, -1, keepdims=True))

    gs2 = gt[0:384].astype(F32) + norm_back(gnt, row_of(extra, 3), n_two, r_two)
    gtok[...] = gs2
    ga = gs2.astype(BF)
    for j in range(2):
        cols = slice(j * 512, (j + 1) * 512)
        gst[:, :, WO + j * 512 : WO + (j + 1) * 512] = (
            dot_tn(att[...], ga[:, cols]).astype(BF).reshape(32, 32, 512)
        )
    gatt = dot_nt(ga[:, 0:512], pack_v[:, :, WO : WO + 512].reshape(1024, 512))
    gatt += dot_nt(ga[:, 512:1024], pack_v[:, :, WO + 512 : WO + 1024].reshape(1024, 512))
    gq[:, 0:1024] = gatt.astype(BF)
    allowed = masks(len_ref[0])

    def pair_step(p, carry):
        lo = pl.ds(pl.multiple_of(p * 128, 128), 128)
        mid = pl.ds(pl.multiple_of(1024 + p * 128, 128), 128)
        hi = pl.ds(pl.multiple_of(2048 + p * 128, 128), 128)
        q2, k2, v2, do = qkv[:, lo], qkv[:, mid], qkv[:, hi], gq[:, lo]
        dq = dk = dv = None
        for hh in range(2):
            mine = lane // 64 == hh
            zero = jnp.zeros_like(q2)
            qm, km, dm = (jnp.where(mine, v, zero) for v in (q2, k2, do))
            total = jnp.sum(jnp.where(lane == 2 * p + hh, lse[...], 0.0), axis=-1, keepdims=True)
            sc = dot_nt(qm, k2) * 0.125
            pf = jnp.where(allowed, jnp.exp(sc - total), 0.0)
            gp = dot_nt(dm, v2)
            ds = (pf * (gp - jnp.sum(pf * gp, axis=-1, keepdims=True))).astype(BF)
            terms = (dot_nn(ds, km), dot_tn(ds, qm), dot_tn(pf.astype(BF), dm))
            dq, dk, dv = terms if hh == 0 else (dq + terms[0], dk + terms[1], dv + terms[2])
        gq[:, lo] = (dq * 0.125).astype(BF)
        gq[:, mid] = (dk * 0.125).astype(BF)
        gq[:, hi] = dv.astype(BF)
        return carry

    lax.fori_loop(0, 8, pair_step, 0)

    def w_step(j, carry):
        cols = pl.ds(pl.multiple_of(j * 512, 512), 512)
        gcols = gq[:, cols]
        gst[:, :, cols] = dot_tn(n1[...], gcols).astype(BF).reshape(32, 32, 512)
        gacc[...] += dot_nt(gcols, pack_v[:, :, cols].reshape(1024, 512))
        return carry

    gacc[...] = jnp.zeros_like(gacc)
    lax.fori_loop(0, 6, w_step, 0)
    gn1 = gacc[...]
    n_one, r_one = norm_parts(tok[...].astype(F32))
    gain_one_row = jnp.sum(gn1 * n_one, axis=0, keepdims=True)
    gtok[...] += norm_back(gn1, row_of(extra, 2), n_one, r_one)
    rowi = lax.broadcasted_iota(jnp.int32, (8, 1024), 0)
    rows = jnp.where(rowi == 0, gain_one_row, jnp.where(rowi == 1, gain_two_row, 0.0)).astype(BF)
    sel = (
        lax.broadcasted_iota(jnp.int32, (8, 128), 1) == lax.broadcasted_iota(jnp.int32, (8, 128), 0) + 2
    ).astype(BF)
    gst[:, :, EX : EX + 128] = (
        (dot_tn(nt[...], two) + dot_tn(rows, sel)).astype(BF).reshape(32, 32, 128)
    )

    chips = (dd, d1, d2, own)
    swap = (0, 2, 1, 3)
    for q in range(4):
        for k in range(4):
            src = gst.at[P_.zk[k] * 8 + P_.rank(P_.flip(chips[q]))]
            i = swap[q] * 4 + k
            go(rcopy(src, rs1.at[i], s1s.at[i], s1r.at[i], P_.dev(sib)))

    def in1(q, k):
        i = q * 4 + k
        rcopy(gst.at[0], rs1.at[i], s1s.at[0], s1r.at[i], P_.dev(sib)).wait_recv()
        s = P_.zk[k] * 8 + P_.rank(chips[q])
        gst[s] = (gst[s].astype(F32) + rs1[i].astype(F32)).astype(BF)

    def out2(q, k, n, p):
        i = n * 4 + k
        go(rcopy(gst.at[P_.zk[k] * 8 + P_.rank(chips[q])], rs2.at[i], s2s.at[i], s2r.at[i], P_.dev(p)))

    def in2(n, k, p):
        i = n * 4 + k
        rcopy(gst.at[0], rs2.at[i], s2s.at[0], s2r.at[i], P_.dev(sib)).wait_recv()
        s = P_.zk[k] * 8 + P_.rank(p)
        gst[s] = (gst[s].astype(F32) + rs2[i].astype(F32)).astype(BF)

    for k in (3, 2, 1, 0):
        in1(0, k)
        out2(0, k, 0, d2)
        in1(2, k)
        out2(2, k, 2, d2)
    for k in (3, 2, 1, 0):
        in1(1, k)
        in1(3, k)
    for k in (3, 2, 1, 0):
        in2(0, k, d1)
        out2(1, k, 1, d1)
    for k in (3, 2, 1, 0):
        in2(2, k, own)
        in2(1, k, own)
        if k:
            zz = P_.zk[k]
            go(rcopy(gst.at[zz * 8 + t], rs3.at[k - 1], s3s.at[k - 1], s3r.at[k - 1], P_.dev(own, zz)))
    acc = gst[b].astype(F32)
    for k in (1, 2, 3):
        rcopy(gst.at[0], rs3.at[k - 1], s3s.at[0], s3r.at[k - 1], P_.dev(sib)).wait_recv()
        acc += rs3[k - 1].astype(F32)
    gpack[...] = acc
    for cp in sends:
        cp.wait_send()


def run_back(lengths, tok, gt, s2, nt, n1, qkv, lse, att, gsum, gl, pack_all):
    sd = jax.ShapeDtypeStruct
    dma = pltpu.SemaphoreType.DMA
    return pl.pallas_call(
        back_kernel,
        out_shape=(sd((384, 1024), F32), sd((32, PW), F32)),
        in_specs=[SM] + [VM] * 10 + [ANY],
        out_specs=(VM, VM),
        scratch_shapes=[
            pltpu.VMEM((32, 32, PW), BF), pltpu.VMEM((384, 3072), BF),
            pltpu.VMEM((384, 1024), F32), pltpu.VMEM((32, 32, PW), BF),
            pltpu.VMEM((16, 32, PW), BF), pltpu.VMEM((12, 32, PW), BF), pltpu.VMEM((3, 32, PW), BF),
            dma((16,)), dma((16,)), dma((12,)), dma((12,)), dma((3,)), dma((3,)), dma((1,)),
        ],
        compiler_params=pltpu.CompilerParams(
            collective_id=2, has_side_effects=True, vmem_limit_bytes=60 * MIB
        ),
    )(lengths, tok, gt, s2, nt, n1, qkv, lse, att, gsum, gl, pack_all)


def fused_device(
    tokens, cotangent, lengths, expert_ids, slot_ids, w_qkv, w_out, gain_one, w_in, w_down,
    w_expert_in, w_expert_out, w_mix, gain_two,
):
    keep = jnp.arange(384, dtype=jnp.int32) < lengths[0]
    table = jnp.where(slot_ids >= 0, expert_ids * CAP + slot_ids, -1).astype(BF)
    gt = jnp.concatenate(
        [
            jnp.where(keep[:, None], cotangent, jnp.zeros_like(cotangent)),
            jnp.pad(table[None, :], ((0, 15), (0, 640))),
        ],
        axis=0,
    )
    pack = jnp.concatenate(
        [
            w_qkv, w_mix, gain_one[:, None], gain_two[:, None],
            jnp.zeros((32, 124), BF), w_out,
        ],
        axis=1,
    )
    wia = jnp.concatenate([w_in[None], w_expert_in], axis=0)
    wia = wia.reshape(3, 32, 4, 8, 128).transpose(3, 0, 1, 2, 4).reshape(8, 3, 32, 512)
    wdn = jnp.concatenate([w_down[None], w_expert_out], axis=0)
    qkv, lse, att, s2, nt, n1, wmix, pack_all, wi_all, wd_all, g_all = run_enter(
        lengths, tokens, pack, wia, wdn, gt
    )
    block, gsum, gl, gdo, gx = run_ff(lengths, nt, wmix, s2, g_all, wi_all, wd_all)
    gtok, gpack = run_back(
        lengths, tokens, gt, s2, nt, n1, qkv, lse, att, gsum, gl, pack_all
    )
    gdo = gdo.reshape(3, 128, 1024)
    gwi = gx.reshape(8, 3, 32, 4, 128).transpose(1, 2, 3, 0, 4).reshape(3, 32, 4096).astype(F32)
    return (
        block, gtok, gpack[:, 0:3072], gpack[:, WO : WO + 1024], gpack[:, EX + 2],
        gwi[0], gdo[0], gwi[1:], gdo[1:], gpack[:, EX : EX + 2], gpack[:, EX + 3],
    )


def solution(mesh):
    placed = (
        P(("dp", "fsdp"), None),
        P(("dp", "fsdp"), None),
        P(("dp", "fsdp")),
        P(("dp", "fsdp")),
        P(("dp", "fsdp")),
        P(("dp", "fsdp"), None),
        P(("dp", "fsdp"), None),
        P(("dp", "fsdp")),
        P(("dp", "fsdp"), None),
        P(("dp", "fsdp"), None),
        P(None, ("dp", "fsdp"), None),
        P(None, ("dp", "fsdp"), None),
        P(("dp", "fsdp"), None),
        P(("dp", "fsdp")),
    )
    fused = (mesh.shape["dp"], mesh.shape["fsdp"]) == (8, 4)
    return jax.shard_map(
        fused_device if fused else per_device,
        mesh=mesh,
        in_specs=placed,
        out_specs=(
            P(("dp", "fsdp"), None),
            P(("dp", "fsdp"), None),
            P(("dp", "fsdp"), None),
            P(("dp", "fsdp"), None),
            P(("dp", "fsdp")),
            P(("dp", "fsdp"), None),
            P(("dp", "fsdp"), None),
            P(None, ("dp", "fsdp"), None),
            P(None, ("dp", "fsdp"), None),
            P(("dp", "fsdp"), None),
            P(("dp", "fsdp")),
        ),
        check_vma=False,
    )
```

```python
import jax
import jax.numpy as jnp
from jax import lax
from jax.experimental import pallas as pl
from jax.experimental.pallas import tpu as pltpu
from jax.sharding import PartitionSpec as P

HEAD_DIM = 64
EXPERTS = 2
CAP = 112


def layer_norm(values_in, gain_vec):
    average = jnp.mean(values_in, axis=-1, keepdims=True)
    centred = values_in - average
    variance = jnp.mean(centred * centred, axis=-1, keepdims=True)
    return centred * lax.rsqrt(variance + 1e-05) * gain_vec


def gelu_tanh(values_in):
    return jax.nn.gelu(values_in, approximate=True)


def gelu_back(values_in, grad_in):
    return jax.vjp(gelu_tanh, values_in)[1](grad_in)[0]


def head_scores(query_h, key_h, allowed, score_scale):
    scores = (
        jnp.einsum("qd,kd->qk", query_h, key_h, preferred_element_type=jnp.float32) * score_scale
    )
    return jnp.where(allowed, scores, -1e30)


def head_forward(entries, allowed, score_scale):
    query_h, key_h, value_h = entries
    scores = head_scores(query_h, key_h, allowed, score_scale)
    row_max = jnp.max(scores, axis=-1, keepdims=True)
    exp_scores = jnp.exp(scores - row_max)
    row_total = jnp.sum(exp_scores, axis=-1, keepdims=True)
    prob_low = (exp_scores / row_total).astype(jnp.bfloat16)
    head_out = jnp.dot(prob_low, value_h, preferred_element_type=jnp.float32)
    return (head_out, (row_max + jnp.log(row_total))[:, 0])


def head_backward(entries, allowed, score_scale):
    query_h, key_h, value_h, grad_head, log_total = entries
    scores = head_scores(query_h, key_h, allowed, score_scale)
    prob_full = jnp.where(allowed, jnp.exp(scores - log_total[:, None]), 0.0)
    prob_low = prob_full.astype(jnp.bfloat16)
    grad_value = jnp.einsum("qk,qd->kd", prob_low, grad_head, preferred_element_type=jnp.float32)
    grad_prob = jnp.einsum("qd,kd->qk", grad_head, value_h, preferred_element_type=jnp.float32)
    grad_score = prob_full * (grad_prob - jnp.sum(prob_full * grad_prob, axis=-1, keepdims=True))
    grad_score = grad_score.astype(jnp.bfloat16)
    grad_query = jnp.dot(grad_score, key_h, preferred_element_type=jnp.float32) * score_scale
    grad_key = (
        jnp.einsum("qk,qd->kd", grad_score, query_h, preferred_element_type=jnp.float32)
        * score_scale
    )
    return (grad_query, grad_key, grad_value)


def per_device(
    tokens,
    cotangent,
    lengths,
    expert_ids,
    slot_ids,
    w_qkv,
    w_out,
    gain_one,
    w_in,
    w_down,
    w_expert_in,
    w_expert_out,
    w_mix,
    gain_two,
):
    row_count, model_width = tokens.shape
    head_count = model_width // HEAD_DIM
    score_scale = HEAD_DIM ** (-0.5)
    full_qkv, full_out, full_gain_one = (
        lax.all_gather(w_qkv, ("dp", "fsdp"), axis=0, tiled=True),
        lax.all_gather(w_out, ("dp", "fsdp"), axis=0, tiled=True),
        lax.all_gather(gain_one, ("dp", "fsdp"), axis=0, tiled=True),
    )
    full_in, full_down, full_expert_in, full_expert_out, full_mix, full_gain_two = (
        lax.all_gather(w_in, ("dp", "fsdp"), axis=0, tiled=True),
        lax.all_gather(w_down, ("dp", "fsdp"), axis=0, tiled=True),
        lax.all_gather(w_expert_in, ("dp", "fsdp"), axis=1, tiled=True),
        lax.all_gather(w_expert_out, ("dp", "fsdp"), axis=1, tiled=True),
        lax.all_gather(w_mix, ("dp", "fsdp"), axis=0, tiled=True),
        lax.all_gather(gain_two, ("dp", "fsdp"), axis=0, tiled=True),
    )
    position = jnp.arange(row_count, dtype=jnp.int32)
    seq_len = lengths[0]
    row_keep = (position < seq_len).astype(jnp.float32)[:, None]
    allowed = (position[None, :] <= position[:, None]) & (position[None, :] < seq_len)

    def to_heads(block):
        return block.reshape(row_count, head_count, HEAD_DIM).transpose(1, 0, 2)

    def from_heads(block):
        return block.transpose(1, 0, 2).reshape(row_count, model_width)

    stream = tokens.astype(jnp.float32)
    gain_first = full_gain_one.astype(jnp.float32)
    normed_one = layer_norm(stream, gain_first).astype(jnp.bfloat16)
    qkv_all = jnp.dot(normed_one, full_qkv, preferred_element_type=jnp.float32).astype(jnp.bfloat16)
    queries = to_heads(qkv_all[:, :model_width])
    key_heads = to_heads(qkv_all[:, model_width : 2 * model_width])
    value_heads = to_heads(qkv_all[:, 2 * model_width :])
    head_out, log_total = lax.map(
        lambda entries: head_forward(entries, allowed, score_scale),
        (queries, key_heads, value_heads),
    )
    attended = from_heads(head_out).astype(jnp.bfloat16)
    stream_two = stream + jnp.dot(attended, full_out, preferred_element_type=jnp.float32)
    gain_second = full_gain_two.astype(jnp.float32)
    normed_two = layer_norm(stream_two, gain_second).astype(jnp.bfloat16)
    dense_up = jnp.dot(normed_two, full_in, preferred_element_type=jnp.float32)
    dense_act = gelu_tanh(dense_up).astype(jnp.bfloat16)
    dense_out = jnp.dot(dense_act, full_down, preferred_element_type=jnp.float32)
    routed = slot_ids >= 0
    table_row = jnp.where(routed, expert_ids * CAP + slot_ids, 0)
    slot_total = EXPERTS * CAP
    dispatch = (
        (table_row[None, :] == jnp.arange(slot_total, dtype=jnp.int32)[:, None]) & routed[None, :]
    ).astype(jnp.bfloat16)
    buffer = jnp.dot(dispatch, normed_two, preferred_element_type=jnp.float32).astype(jnp.bfloat16)
    buffer = buffer.reshape(EXPERTS, CAP, model_width)
    expert_up = jnp.einsum(
        "ecd,edf->ecf", buffer, full_expert_in, preferred_element_type=jnp.float32
    )
    expert_act = gelu_tanh(expert_up).astype(jnp.bfloat16)
    expert_y = jnp.einsum(
        "ecf,efd->ecd", expert_act, full_expert_out, preferred_element_type=jnp.float32
    )
    expert_y = expert_y.reshape(slot_total, model_width)
    expert_mix = jnp.where(routed[:, None], expert_y[table_row], 0.0)
    logits = jnp.dot(normed_two, full_mix, preferred_element_type=jnp.float32)
    mix_coeff = jax.nn.softmax(logits, axis=-1)
    branch = mix_coeff[:, 0:1] * dense_out + mix_coeff[:, 1:2] * expert_mix
    block_out = ((stream_two + branch) * row_keep).astype(jnp.bfloat16)
    grad_out = cotangent.astype(jnp.float32) * row_keep
    grad_dense = (mix_coeff[:, 0:1] * grad_out).astype(jnp.bfloat16)
    grad_expert = (mix_coeff[:, 1:2] * grad_out).astype(jnp.bfloat16)
    grad_coeff = jnp.stack(
        [jnp.sum(grad_out * dense_out, axis=-1), jnp.sum(grad_out * expert_mix, axis=-1)], axis=-1
    )
    grad_logits = jax.vjp(lambda values_in: jax.nn.softmax(values_in, axis=-1), logits)[1](
        grad_coeff
    )[0]
    full_in, full_down, full_expert_in, full_expert_out, full_mix, full_gain_two = (
        lax.all_gather(w_in, ("dp", "fsdp"), axis=0, tiled=True),
        lax.all_gather(w_down, ("dp", "fsdp"), axis=0, tiled=True),
        lax.all_gather(w_expert_in, ("dp", "fsdp"), axis=1, tiled=True),
        lax.all_gather(w_expert_out, ("dp", "fsdp"), axis=1, tiled=True),
        lax.all_gather(w_mix, ("dp", "fsdp"), axis=0, tiled=True),
        lax.all_gather(gain_two, ("dp", "fsdp"), axis=0, tiled=True),
    )
    gain_second = full_gain_two.astype(jnp.float32)
    grad_w_down = jnp.einsum("tf,td->fd", dense_act, grad_dense, preferred_element_type=jnp.float32)
    grad_dense_act = jnp.einsum(
        "td,fd->tf", grad_dense, full_down, preferred_element_type=jnp.float32
    )
    grad_dense_up = gelu_back(dense_up, grad_dense_act).astype(jnp.bfloat16)
    grad_w_in = jnp.einsum(
        "td,tf->df", normed_two, grad_dense_up, preferred_element_type=jnp.float32
    )
    grad_normed_two = jnp.einsum(
        "tf,df->td", grad_dense_up, full_in, preferred_element_type=jnp.float32
    )
    grad_y = jnp.dot(dispatch, grad_expert, preferred_element_type=jnp.float32).astype(jnp.bfloat16)
    grad_y = grad_y.reshape(EXPERTS, CAP, model_width)
    grad_expert_out_lead = jnp.einsum(
        "ecf,ecd->fed", expert_act, grad_y, preferred_element_type=jnp.float32
    )
    grad_expert_act = jnp.einsum(
        "ecd,efd->ecf", grad_y, full_expert_out, preferred_element_type=jnp.float32
    )
    grad_expert_up = gelu_back(expert_up, grad_expert_act).astype(jnp.bfloat16)
    grad_expert_in_lead = jnp.einsum(
        "ecd,ecf->def", buffer, grad_expert_up, preferred_element_type=jnp.float32
    )
    grad_buffer = jnp.einsum(
        "ecf,edf->ecd", grad_expert_up, full_expert_in, preferred_element_type=jnp.float32
    )
    grad_buffer = grad_buffer.reshape(slot_total, model_width)
    grad_normed_two = grad_normed_two + jnp.where(routed[:, None], grad_buffer[table_row], 0.0)
    mix_full = full_mix.astype(jnp.float32)
    normed_full = normed_two.astype(jnp.float32)
    grad_normed_two = grad_normed_two + jnp.dot(
        grad_logits, mix_full.T, precision=lax.Precision.HIGHEST
    )
    grad_w_mix = jnp.dot(normed_full.T, grad_logits, precision=lax.Precision.HIGHEST)
    _, pull_two = jax.vjp(layer_norm, stream_two, gain_second)
    grad_stream_ln, grad_gain_two = pull_two(grad_normed_two)
    grad_stream_two = grad_out + grad_stream_ln
    full_qkv, full_out, full_gain_one = (
        lax.all_gather(w_qkv, ("dp", "fsdp"), axis=0, tiled=True),
        lax.all_gather(w_out, ("dp", "fsdp"), axis=0, tiled=True),
        lax.all_gather(gain_one, ("dp", "fsdp"), axis=0, tiled=True),
    )
    gain_first = full_gain_one.astype(jnp.float32)
    grad_attn = grad_stream_two.astype(jnp.bfloat16)
    grad_w_out = jnp.einsum("td,te->de", attended, grad_attn, preferred_element_type=jnp.float32)
    grad_attended = jnp.einsum(
        "te,de->td", grad_attn, full_out, preferred_element_type=jnp.float32
    ).astype(jnp.bfloat16)
    grad_query, grad_key, grad_value = lax.map(
        lambda entries: head_backward(entries, allowed, score_scale),
        (queries, key_heads, value_heads, to_heads(grad_attended), log_total),
    )
    grad_qkv = jnp.concatenate(
        [from_heads(grad_query), from_heads(grad_key), from_heads(grad_value)], axis=1
    ).astype(jnp.bfloat16)
    grad_w_qkv = jnp.einsum("td,te->de", normed_one, grad_qkv, preferred_element_type=jnp.float32)
    grad_normed_one = jnp.einsum(
        "te,de->td", grad_qkv, full_qkv, preferred_element_type=jnp.float32
    )
    _, pull_one = jax.vjp(layer_norm, stream, gain_first)
    grad_stream_one, grad_gain_one = pull_one(grad_normed_one)
    grad_tokens = grad_stream_two + grad_stream_one
    (
        part_qkv,
        part_out,
        part_gain_one,
        part_in,
        part_down,
        lead_expert_in,
        lead_expert_out,
        part_mix,
        part_gain_two,
    ) = (
        lax.psum_scatter(grad_w_qkv, ("dp", "fsdp"), scatter_dimension=0, tiled=True),
        lax.psum_scatter(grad_w_out, ("dp", "fsdp"), scatter_dimension=0, tiled=True),
        lax.psum_scatter(grad_gain_one, ("dp", "fsdp"), scatter_dimension=0, tiled=True),
        lax.psum_scatter(grad_w_in, ("dp", "fsdp"), scatter_dimension=0, tiled=True),
        lax.psum_scatter(grad_w_down, ("dp", "fsdp"), scatter_dimension=0, tiled=True),
        lax.psum_scatter(grad_expert_in_lead, ("dp", "fsdp"), scatter_dimension=0, tiled=True),
        lax.psum_scatter(grad_expert_out_lead, ("dp", "fsdp"), scatter_dimension=0, tiled=True),
        lax.psum_scatter(grad_w_mix, ("dp", "fsdp"), scatter_dimension=0, tiled=True),
        lax.psum_scatter(grad_gain_two, ("dp", "fsdp"), scatter_dimension=0, tiled=True),
    )
    part_expert_in = lead_expert_in.transpose(1, 0, 2)
    part_expert_out = lead_expert_out.transpose(1, 0, 2)
    return (
        block_out,
        grad_tokens,
        part_qkv,
        part_out,
        part_gain_one,
        part_in,
        part_down,
        part_expert_in,
        part_expert_out,
        part_mix,
        part_gain_two,
    )


BF = jnp.bfloat16
F32 = jnp.float32
MESH = pl.DeviceIdType.MESH
ANY = pl.BlockSpec(memory_space=pl.ANY)
VM = pl.BlockSpec(memory_space=pltpu.VMEM)
SM = pl.BlockSpec(memory_space=pltpu.SMEM)
MIB = 1024 * 1024


def dot_nn(a, b):
    return lax.dot_general(a, b, (((1,), (0,)), ((), ())), preferred_element_type=F32)


def dot_nt(a, b):
    return lax.dot_general(a, b, (((1,), (1,)), ((), ())), preferred_element_type=F32)


def dot_tn(a, b):
    return lax.dot_general(a, b, (((0,), (0,)), ((), ())), preferred_element_type=F32)


class Place:
    def __init__(self):
        dp, fs = lax.axis_index("dp"), lax.axis_index("fsdp")
        z, y, x, c = dp // 2, dp % 2, fs // 2, fs % 2
        self.z, self.y, self.x, self.c = z, y, x, c
        self.own = (y, x, c)
        self.sib = (y, x, 1 - c)
        self.d1 = ((y + c) % 2, (x + 1 - c) % 2, c)
        self.d2 = ((y + 1 - c) % 2, (x + c) % 2, c)
        self.dd = (1 - y, 1 - x, c)
        self.zk = [z, z + 1 - 2 * (z % 2), (z + 2) % 4, 3 - z]
        self.t = self.rank(self.own)
        self.b = z * 8 + self.t

    @staticmethod
    def rank(p):
        return p[0] * 4 + p[1] * 2 + p[2]

    def flip(self, p):
        return (p[0], p[1], 1 - p[2])

    def dev(self, p, z=None):
        z = self.z if z is None else z
        return (z * 2 + p[0], p[1] * 2 + p[2])

    def plane_others(self):
        y, x, c = self.own
        return [
            ((y + k // 4) % 2, (x + (k // 2) % 2) % 2, (c + k % 2) % 2) for k in range(1, 8)
        ]


def rcopy(src, dst, send, recv, dev):
    return pltpu.make_async_remote_copy(
        src_ref=src, dst_ref=dst, send_sem=send, recv_sem=recv, device_id=dev, device_id_type=MESH
    )


def meet(devs):
    bar = pltpu.get_barrier_semaphore()
    for dev in devs:
        pl.semaphore_signal(bar, inc=1, device_id=dev, device_id_type=MESH)
    pl.semaphore_wait(bar, len(devs))


def norm_parts(v):
    mean = jnp.mean(v, axis=-1, keepdims=True)
    cen = v - mean
    var = jnp.mean(cen * cen, axis=-1, keepdims=True)
    r = lax.rsqrt(var + 1e-05)
    return cen * r, r


def row_of(extra, lane):
    pick = (lax.broadcasted_iota(jnp.int32, (8, 128), 1) == lane).astype(BF)
    return dot_nt(pick, extra)[0:1]


class ZSum:
    def __init__(self, P_, src, land, via, send, recv):
        self.P, self.src, self.land, self.via = P_, src, land, via
        self.send, self.recv = send, recv
        self.mid = (P_.z == 1) | (P_.z == 2)

    def copy(self, n, w, j):
        P_ = self.P
        to = P_.dev(P_.own, P_.zk[1 if j == 4 else j])
        block = self.src[w].at[n, P_.zk[3 if j == 4 else j]]
        dst = self.via[w].at[n] if j == 4 else self.land[w].at[n, j - 1]
        i = w * 4 + j - 1
        return rcopy(block, dst, self.send.at[n, i], self.recv.at[n, i], to)

    def ship(self, n):
        @pl.when(self.mid)
        def _():
            for j in (3, 1):
                for w in range(2):
                    self.copy(n, w, j).start()

        @pl.when(jnp.logical_not(self.mid))
        def _():
            for j in (4, 2, 1):
                for w in range(2):
                    self.copy(n, w, j).start()

    def transit(self, n):
        @pl.when(self.mid)
        def _():
            k2 = self.P.zk[2]
            for w in range(2):
                self.copy(n, w, 4).wait_recv()
                self.src[w][n, k2] = self.src[w][n, k2] + self.via[w][n]
                self.copy(n, w, 2).start()

    def arrived(self, n):
        for w in range(2):
            self.copy(n, w, 1).wait_recv()
            self.copy(n, w, 2).wait_recv()

        @pl.when(self.mid)
        def _():
            for w in range(2):
                self.copy(n, w, 3).wait_recv()

    def sent(self, n):
        for w in range(2):
            self.copy(n, w, 1).wait_send()
            self.copy(n, w, 2).wait_send()

        @pl.when(self.mid)
        def _():
            for w in range(2):
                self.copy(n, w, 3).wait_send()

        @pl.when(jnp.logical_not(self.mid))
        def _():
            for w in range(2):
                self.copy(n, w, 4).wait_send()


class ZGather:
    def __init__(self, P_, mine, full, send, recv):
        self.P, self.mine, self.full, self.send, self.recv = P_, mine, full, send, recv
        self.mid = (P_.z == 1) | (P_.z == 2)

    def copy(self, n, w, j):
        P_ = self.P
        zs = P_.zk[2] if j == 4 else P_.z
        block = self.full[w](n, zs) if j == 4 else self.mine[w](n)
        to = P_.dev(P_.own, P_.zk[1 if j == 4 else j])
        return rcopy(
            block, self.full[w](n, zs), self.send.at[n, w * 4 + j - 1], self.recv.at[n, w * 4 + zs], to
        )

    def landed(self, n, w, j):
        P_ = self.P
        zs = P_.zk[j]
        rcopy(
            self.mine[w](n), self.full[w](n, zs), self.send.at[n, 0], self.recv.at[n, w * 4 + zs],
            P_.dev(P_.sib),
        ).wait_recv()

    def ship(self, n):
        for w in range(2):
            self.copy(n, w, 2).start()

        @pl.when(self.mid)
        def _():
            for w in range(2):
                self.copy(n, w, 3).start()

        for w in range(2):
            self.copy(n, w, 1).start()

    def relay(self, n):
        for w in range(2):
            self.landed(n, w, 2)

        @pl.when(self.mid)
        def _():
            for w in range(2):
                self.copy(n, w, 4).start()

    def finish(self, n):
        for w in range(2):
            self.landed(n, w, 1)
            self.landed(n, w, 3)
            self.copy(n, w, 1).wait_send()
            self.copy(n, w, 2).wait_send()

        @pl.when(self.mid)
        def _():
            for w in range(2):
                self.copy(n, w, 3).wait_send()
                self.copy(n, w, 4).wait_send()


PW = 4224
EX = 3072
WO = 3200


def enter_kernel(
    len_ref, tok, pack, wia, wdn, gt,
    qkv, lse, att, s2, nt, n1, wmix, pack_all, wi_all, wd_all, g_all,
    pack_v, ps, pr, asend, arecv, fsend, frecv, gs, gr, lsem,
):
    P_ = Place()
    z, t, b = P_.z, P_.t, P_.b
    own, sib, d1, d2, dd = P_.own, P_.sib, P_.d1, P_.d2, P_.dd
    others = P_.plane_others()
    meet([P_.dev(p) for p in others] + [P_.dev(own, zz) for zz in P_.zk[1:]])
    sends = []

    def go(cp):
        cp.start()
        sends.append(cp)

    experts = ZGather(
        P_, (lambda n: wi_all.at[1 + n, z], lambda n: wd_all.at[1 + n, z]),
        (lambda n, zs: wi_all.at[1 + n, zs], lambda n, zs: wd_all.at[1 + n, zs]), fsend, frecv,
    )
    lc = pltpu.make_async_copy(pack, pack_v.at[b], lsem.at[0])
    lc.start()
    for k in range(1, 4):
        go(rcopy(pack, pack_v.at[b], ps.at[k - 1], pr.at[b], P_.dev(own, P_.zk[k])))
    go(rcopy(pack, pack_v.at[b], ps.at[3], pr.at[b], P_.dev(d1)))
    go(rcopy(pack, pack_v.at[b], ps.at[7], pr.at[b], P_.dev(d2)))
    go(rcopy(pack, pack_v.at[b], ps.at[15], pr.at[b], P_.dev(sib)))
    rows = pl.ds(pl.multiple_of(t * 32, 32), 32)
    lw = pltpu.make_async_copy(wia.at[t], wi_all.at[:, z, rows], lsem.at[1])
    lw.start()
    for i, p in enumerate(others):
        go(rcopy(wia.at[P_.rank(p)], wi_all.at[:, z, rows], asend.at[i], arecv.at[t], P_.dev(p)))
    ld = pltpu.make_async_copy(wdn, wd_all.at[:, z], lsem.at[2])
    ld.start()

    def landed(slot):
        rcopy(pack, pack_v.at[slot], ps.at[0], pr.at[slot], P_.dev(sib)).wait_recv()

    def fwd(slot, sem, p):
        go(rcopy(pack_v.at[slot], pack_v.at[slot], ps.at[sem], pr.at[slot], P_.dev(p)))

    def slot(k, p):
        return P_.zk[k] * 8 + P_.rank(p)

    for k in range(0, 6):
        if 1 <= k <= 3:
            s = slot(k, own)
            landed(s)
            fwd(s, 3 + k, d1)
            fwd(s, 7 + k, d2)
            fwd(s, 15 + k, sib)
        if k == 3:
            lw.wait()
            ld.wait()
            for p in others:
                rr = P_.rank(p)
                rq = pl.ds(pl.multiple_of(rr * 32, 32), 32)
                rcopy(
                    wia.at[0], wi_all.at[:, z, rq], asend.at[0], arecv.at[rr], P_.dev(sib)
                ).wait_recv()
            for e in range(2):
                experts.ship(e)
        if 1 <= k <= 4:
            s = slot(k - 1, d1)
            landed(s)
            fwd(s, 11 + k - 1, d2)
            fwd(s, 19 + k - 1, sib)
            s = slot(k - 1, d2)
            landed(s)
            fwd(s, 23 + k - 1, sib)
        if k >= 2:
            s = slot(k - 2, dd)
            landed(s)
            fwd(s, 27 + k - 2, sib)
    lg = pltpu.make_async_copy(gt, g_all.at[t], lsem.at[3])
    lg.start()
    for i, p in enumerate((d1, d2, sib)):
        go(rcopy(gt, g_all.at[t], gs.at[i], gr.at[t], P_.dev(p)))
    stream = tok[...].astype(F32)
    for k in range(4):
        for p in (own, d1, d2, dd):
            landed(slot(k, P_.flip(p)))
    lc.wait()
    keep_all = pltpu.make_async_copy(pack_v, pack_all, lsem.at[0])
    keep_all.start()

    extra = pack_v[:, :, EX : EX + 128].reshape(1024, 128)
    wmix[...] = extra
    n_one, _ = norm_parts(stream)
    n1[...] = (n_one * row_of(extra, 2)).astype(BF)

    def qkv_step(j, carry):
        cols = pl.ds(pl.multiple_of(j * 512, 512), 512)
        qkv[:, cols] = dot_nn(n1[...], pack_v[:, :, cols].reshape(1024, 512)).astype(BF)
        return carry

    lax.fori_loop(0, 6, qkv_step, 0)

    def g_landed(p):
        r = P_.rank(p)
        rcopy(gt, g_all.at[r], gs.at[0], gr.at[r], P_.dev(sib)).wait_recv()
        return r

    def g_fwd(r, i, p):
        go(rcopy(g_all.at[r], g_all.at[r], gs.at[i], gr.at[r], P_.dev(p)))

    r = g_landed(d1)
    g_fwd(r, 3, d2)
    g_fwd(r, 4, sib)

    allowed = masks(len_ref[0])
    lane = lax.broadcasted_iota(jnp.int32, (384, 128), 1)
    lse[...] = jnp.zeros_like(lse)

    def pair_step(p, carry):
        q2 = qkv[:, pl.ds(pl.multiple_of(p * 128, 128), 128)]
        k2 = qkv[:, pl.ds(pl.multiple_of(1024 + p * 128, 128), 128)]
        v2 = qkv[:, pl.ds(pl.multiple_of(2048 + p * 128, 128), 128)]
        outs = []
        for hh in range(2):
            qm = jnp.where(lane // 64 == hh, q2, jnp.zeros_like(q2))
            sc = jnp.where(allowed, dot_nt(qm, k2) * 0.125, -1e30)
            top = jnp.max(sc, axis=-1, keepdims=True)
            ex = jnp.exp(sc - top)
            tot = jnp.sum(ex, axis=-1, keepdims=True)
            outs.append(dot_nn((ex * (1.0 / tot)).astype(BF), v2))
            lse[...] = jnp.where(lane == 2 * p + hh, top + jnp.log(tot), lse[...])
        att[:, pl.ds(pl.multiple_of(p * 128, 128), 128)] = jnp.where(
            lane < 64, outs[0], outs[1]
        ).astype(BF)
        return carry

    lax.fori_loop(0, 8, pair_step, 0)
    r = g_landed(d2)
    g_fwd(r, 5, sib)
    experts.relay(0)
    for j in range(2):
        w = pack_v[:, :, WO + j * 512 : WO + (j + 1) * 512].reshape(1024, 512)
        s2[:, j * 512 : (j + 1) * 512] = stream[:, j * 512 : (j + 1) * 512] + dot_nn(att[...], w)
    n_two, _ = norm_parts(s2[...])
    nt[...] = (n_two * row_of(extra, 3)).astype(BF)
    r = g_landed(dd)
    g_fwd(r, 6, sib)
    for p in (own, d1, d2, dd):
        g_landed(P_.flip(p))
    experts.relay(1)
    for e in range(2):
        experts.finish(e)
    lg.wait()
    keep_all.wait()
    for cp in sends:
        cp.wait_send()


def masks(seq_len):
    row = lax.broadcasted_iota(jnp.int32, (384, 384), 0)
    col = lax.broadcasted_iota(jnp.int32, (384, 384), 1)
    return (col <= row) & (col < seq_len)


def run_enter(lengths, tok, pack, wia, wdn, gt):
    sd = jax.ShapeDtypeStruct
    return pl.pallas_call(
        enter_kernel,
        out_shape=(
            sd((384, 3072), BF), sd((384, 128), F32), sd((384, 1024), BF), sd((384, 1024), F32),
            sd((384, 1024), BF), sd((384, 1024), BF), sd((1024, 128), BF),
            sd((32, 32, PW), BF), sd((3, 4, 256, 512), BF), sd((3, 4, 128, 1024), BF),
            sd((8, 400, 1024), BF),
        ),
        in_specs=[SM, VM, ANY, ANY, ANY, ANY],
        out_specs=(VM,) * 7 + (ANY,) * 4,
        scratch_shapes=[
            pltpu.VMEM((32, 32, PW), BF),
            pltpu.SemaphoreType.DMA((31,)), pltpu.SemaphoreType.DMA((32,)),
            pltpu.SemaphoreType.DMA((7,)), pltpu.SemaphoreType.DMA((8,)),
            pltpu.SemaphoreType.DMA((2, 8)), pltpu.SemaphoreType.DMA((2, 8)),
            pltpu.SemaphoreType.DMA((7,)), pltpu.SemaphoreType.DMA((8,)),
            pltpu.SemaphoreType.DMA((4,)),
        ],
        compiler_params=pltpu.CompilerParams(
            collective_id=0, has_side_effects=True, vmem_limit_bytes=48 * MIB
        ),
    )(lengths, tok, pack, wia, wdn, gt)


def mix_of(logits):
    delta = logits[:, 0:1] - logits[:, 1:2]
    return 1.0 / (1.0 + jnp.exp(-delta)), 1.0 / (1.0 + jnp.exp(delta))


def gelu_both(u):
    a, bb = 0.7978845608028654, 0.044715
    u2 = u * u
    th = jnp.tanh(a * u * (1.0 + bb * u2))
    half = 0.5 * (1.0 + th)
    return u * half, half + 0.5 * u * (1.0 - th * th) * a * (1.0 + 3.0 * bb * u2)


def ff_kernel(
    len_ref, nt_own, wmix, s2, g_all, wi_all, wd_all,
    block, gsum, gl_out, gde, xe, dgi, dgd, r1, r2, rin, rdn, dwi, dwd,
    nt_all, gbuf, br, gn, xb, yb, wi, wd, ai, ad, gin, gdn, tri, trd, tmp, gc, gcr, dots,
    ts, tr, gsem, wsem, zas, zar, zss, zsr, s1s, s1r, s2s, s2r, cs, cr, lsem, tsem,
):
    P_ = Place()
    z, t = P_.z, P_.t
    own, sib, d1, d2, dd = P_.own, P_.sib, P_.d1, P_.d2, P_.dd
    others = P_.plane_others()
    meet([P_.dev(p) for p in others] + [P_.dev(own, zz) for zz in P_.zk[1:]])
    sends = []

    def go(cp):
        cp.start()
        sends.append(cp)

    ln = pltpu.make_async_copy(nt_own, nt_all.at[t], lsem.at[0])
    ln.start()
    for i, p in enumerate((d1, d2, sib)):
        go(rcopy(nt_own, nt_all.at[t], ts.at[i], tr.at[t], P_.dev(p)))
    dense = ZGather(
        P_, (lambda n: wi_all.at[0, z], lambda n: wd_all.at[0, z]),
        (lambda n, zs: dwi.at[zs], lambda n, zs: dwd.at[zs]), zas, zar,
    )
    dense.ship(0)
    l0 = pltpu.make_async_copy(wi_all.at[0, z], dwi.at[z], lsem.at[1])
    l1 = pltpu.make_async_copy(wd_all.at[0, z], dwd.at[z], lsem.at[2])
    l0.start()
    l1.start()
    s2_in = pltpu.make_async_copy(s2, gsum, lsem.at[3])
    s2_in.start()

    def w_load(e):
        return (
            pltpu.make_async_copy(wi_all.at[1 + e], wi.at[e], wsem.at[e, 0]),
            pltpu.make_async_copy(wd_all.at[1 + e], wd.at[e], wsem.at[e, 1]),
        )

    def dense_load():
        return (
            pltpu.make_async_copy(dwi, wi.at[0], wsem.at[0, 0]),
            pltpu.make_async_copy(dwd, wd.at[0], wsem.at[0, 1]),
        )

    for e in range(2):
        for cp in w_load(e):
            cp.start()
    zsum = ZSum(P_, (gin, gdn), (rin, rdn), (tri, trd), zss, zsr)

    order = (own, sib, d1, P_.flip(d2), d2, P_.flip(d1), dd, P_.flip(dd))
    ranks = [P_.rank(p) for p in order]

    def seq_at(i):
        s = ranks[0]
        for k in range(1, 8):
            s = jnp.where(i == k, ranks[k], s)
        return s

    def g_copy(i):
        return pltpu.make_async_copy(g_all.at[seq_at(i)], gbuf.at[i % 2], gsem.at[i % 2])

    def ff(xv, gv, k):
        wiv = wi[k].reshape(1024, 512)
        wdv = wd[k].reshape(512, 1024)
        act, dact = gelu_both(dot_nn(xv, wiv))
        act = act.astype(BF)
        gup = (dact * dot_nt(gv, wdv)).astype(BF)
        ad[k] += dot_tn(act, gv)
        ai[k] += dot_tn(xv, gup)
        return dot_nn(act, wdv), dot_nt(gup, wiv)

    lane = lax.broadcasted_iota(jnp.int32, (448, 128), 1)

    def shares(tab, e):
        slot = lax.broadcasted_iota(jnp.int32, (112, 384), 0) + e * 112
        return (tab == slot.astype(F32)).astype(BF)

    fwds = {2: (d1, ((3, d2), (4, sib))), 4: (d2, ((5, sib),)), 6: (dd, ((6, sib),))}

    def fwd_copy(p, i, q):
        r = P_.rank(p)
        return rcopy(nt_all.at[r], nt_all.at[r], ts.at[i], tr.at[r], P_.dev(q))

    g_copy(0).start()
    ai[...] = jnp.zeros_like(ai)
    ad[...] = jnp.zeros_like(ad)
    ln.wait()
    for e in range(2):
        for cp in w_load(e):
            cp.wait()

    def arrive(i, carry):
        s = seq_at(i)

        @pl.when(i + 1 < 8)
        def _():
            g_copy(i + 1).start()

        @pl.when(i > 0)
        def _():
            rcopy(nt_own, nt_all.at[s], ts.at[0], tr.at[s], P_.dev(sib)).wait_recv()

        for k, (p, dests) in fwds.items():

            @pl.when(i == k)
            def _():
                for n, q in dests:
                    fwd_copy(p, n, q).start()

        g_copy(i).wait()
        xv = nt_all[s]
        gv = gbuf[i % 2, :384]
        tab = gbuf[i % 2, 384:400][0:1, :384].astype(F32)
        _, m1 = mix_of(dot_nn(xv, wmix[...]))
        ge = (m1 * gv.astype(F32)).astype(BF)
        for e in range(2):
            sh = shares(tab, e)
            xb[e, i] = dot_nn(sh, xv).astype(BF)
            yb[e, i] = dot_nn(sh, ge).astype(BF)
        return carry

    def half(b, carry):
        lax.fori_loop(b * 4, b * 4 + 4, arrive, 0)

        @pl.when(b == 1)
        def _():
            dense.relay(0)

        def expert(e, carry):
            four = pl.ds(b * 4, 4)
            gq = yb[e, four].reshape(448, 1024)
            yv, gb = ff(xb[e, four].reshape(448, 1024), gq, e)
            rs = jnp.sum(gq.astype(F32) * yv, axis=-1, keepdims=True)
            high = rs.astype(BF).astype(F32)
            dots[e, four] = (
                jnp.where(lane == 0, high, jnp.where(lane == 1, rs - high, 0.0))
                .astype(BF)
                .reshape(4, 112, 128)
            )
            xb[e, four] = yv.astype(BF).reshape(4, 112, 1024)
            yb[e, four] = gb.astype(BF).reshape(4, 112, 1024)

            @pl.when(b == 1)
            def _():
                gin[e] = ai[e].astype(BF).reshape(4, 256, 512)
                gdn[e] = ad[e].astype(BF).reshape(4, 128, 1024)
                zsum.ship(e)

            return carry

        lax.fori_loop(0, 2, expert, 0)
        return carry

    lax.fori_loop(0, 2, half, 0)
    g_copy(7).start()
    l0.wait()
    l1.wait()
    dense.finish(0)
    for cp in dense_load():
        cp.start()
    ai[0] = jnp.zeros_like(ai[0])
    ad[0] = jnp.zeros_like(ad[0])
    for cp in dense_load():
        cp.wait()

    chips = (dd, d1, d2, own)
    both = (gn, br)

    def give1(q, w):
        r = P_.rank(P_.flip(chips[q]))
        k = (0, 2, 1, 3)[q]
        return rcopy(both[w].at[r], r1.at[w, k], s1s.at[w, k], s1r.at[w, k], P_.dev(sib))

    def load1(q, w, start):
        cp = pltpu.make_async_copy(r1.at[w, q], tmp.at[w], tsem.at[w])
        if start:
            rcopy(nt_own, r1.at[w, q], s1s.at[0, 0], s1r.at[w, q], P_.dev(sib)).wait_recv()
            cp.start()
        else:
            cp.wait()
            add_tmp(w, P_.rank(chips[q]))

    def load2(k, p, w, start):
        cp = pltpu.make_async_copy(r2.at[w, k], tmp.at[w], tsem.at[w])
        if start:
            rcopy(nt_own, r2.at[w, k], s2s.at[0, 0], s2r.at[w, k], P_.dev(sib)).wait_recv()
            cp.start()
        else:
            cp.wait()
            add_tmp(w, P_.rank(p))

    def add_tmp(w, r):
        both[w][r] = both[w][r] + tmp[w]

    def give2(q, k, p, w):
        src = both[w].at[P_.rank(chips[q])]
        return rcopy(src, r2.at[w, k], s2s.at[w, k], s2r.at[w, k], P_.dev(p))

    def dense_step(k, carry):
        i = 7 - k
        s = seq_at(i)

        @pl.when(i > 0)
        def _():
            g_copy(i - 1).start()

        g_copy(i).wait()
        xv = nt_all[s]
        gf = gbuf[i % 2, :384].astype(F32)
        tab = gbuf[i % 2, 384:400][0:1, :384].astype(F32)
        m0, m1 = mix_of(dot_nn(xv, wmix[...]))
        out, gxv = ff(xv, (m0 * gf).astype(BF), 0)
        col = jnp.broadcast_to(jnp.sum(gf * out, axis=-1, keepdims=True), (384, 128))
        gc[s, 0:8] = jnp.transpose(col)[0:8]
        s0, s1 = shares(tab, 0), shares(tab, 1)
        q1 = dot_tn(s0, dots[0, i]) + dot_tn(s1, dots[1, i])
        gc[s, 8:16] = jnp.transpose(jnp.broadcast_to(q1[:, 0:1] + q1[:, 1:2], (384, 128)))[0:8]
        br[s] = (m0 * out + m1 * (dot_tn(s0, xb[0, i]) + dot_tn(s1, xb[1, i]))).astype(BF)
        gn[s] = (gxv + dot_tn(s0, yb[0, i]) + dot_tn(s1, yb[1, i])).astype(BF)

        for step, q in ((0, 0), (2, 1), (4, 2), (6, 3)):

            @pl.when(k == step)
            def _():
                for w in range(2):
                    give1(q, w).start()

        @pl.when(k == 1)
        def _():
            for w in range(2):
                load1(0, w, True)

        @pl.when(k == 2)
        def _():
            for w in range(2):
                load1(0, w, False)
                give2(0, 0, d2, w).start()
            zsum.transit(0)

        @pl.when(k == 3)
        def _():
            for w in range(2):
                load1(2, w, True)

        @pl.when(k == 4)
        def _():
            for w in range(2):
                load1(2, w, False)
                give2(2, 2, d2, w).start()

        @pl.when(k == 5)
        def _():
            for w in range(2):
                load1(1, w, True)
            zsum.transit(1)

        @pl.when(k == 6)
        def _():
            for w in range(2):
                load1(1, w, False)
                load2(0, d1, w, True)

        return carry

    lax.fori_loop(0, 8, dense_step, 0)
    for w in range(2):
        load2(0, d1, w, False)
        give2(1, 1, d1, w).start()
        load1(3, w, True)
    for i, p in enumerate(others):
        go(rcopy(gc.at[P_.rank(p)], gcr.at[t], cs.at[i], cr.at[t], P_.dev(p)))
    o0 = pltpu.make_async_copy(ai.at[0], dgi, lsem.at[0])
    o1 = pltpu.make_async_copy(ad.at[0], dgd, lsem.at[1])
    o0.start()
    o1.start()
    for w in range(2):
        load1(3, w, False)
        load2(2, own, w, True)
    for w in range(2):
        load2(2, own, w, False)
    for w in range(2):
        load2(1, own, w, True)
        load2(1, own, w, False)
    s2_in.wait()
    branch = br[t].astype(F32)
    keep = (lax.broadcasted_iota(jnp.int32, (384, 1), 0) < len_ref[0]).astype(F32)
    block[...] = ((gsum[...] + branch) * keep).astype(BF)
    gsum[...] = gn[t].astype(F32)
    for p in others:
        r = P_.rank(p)
        rcopy(gc.at[0], gcr.at[r], cs.at[0], cr.at[r], P_.dev(sib)).wait_recv()
    gcr[t] = gc[t]
    tot = jnp.sum(gcr[...], axis=0)
    gc0 = jnp.transpose(jnp.broadcast_to(tot[0:1], (128, 384)))
    q1 = jnp.transpose(jnp.broadcast_to(tot[8:9], (128, 384)))
    m0, m1 = mix_of(dot_nn(nt_all[t], wmix[...]))
    gl_out[...] = m0 * (m1 * gc0 - q1)

    for k, (p, dests) in fwds.items():
        for n, q in dests:
            fwd_copy(p, n, q).wait_send()
    mids = zsum.mid

    def third(e):
        return (
            pltpu.make_async_copy(rin.at[e, 2], nt_all.at[2, 0:256, 0:512], lsem.at[4]),
            pltpu.make_async_copy(rdn.at[e, 2], nt_all.at[3, 0:128], lsem.at[5]),
        )

    for e in range(2):
        zsum.arrived(e)
        loads = (
            (rin.at[e, 0], nt_all.at[0, 0:256, 0:512]), (rin.at[e, 1], nt_all.at[0, 0:256, 512:1024]),
            (rdn.at[e, 0], nt_all.at[1, 0:128]), (rdn.at[e, 1], nt_all.at[1, 128:256]),
        )
        loads = [pltpu.make_async_copy(u, v, lsem.at[6 + n]) for n, (u, v) in enumerate(loads)]

        @pl.when(mids)
        def _():
            for cp in third(e):
                cp.start()

        for cp in loads:
            cp.start()
        for cp in loads:
            cp.wait()
        two = nt_all[0, 0:256]
        ai[1, 0:256] = gin[e, z].astype(F32) + two[:, 0:512].astype(F32) + two[:, 512:1024].astype(F32)
        at = slice(e * 128, (e + 1) * 128)
        ad[1, at] = gdn[e, z].astype(F32) + nt_all[1, 0:128].astype(F32) + nt_all[1, 128:256].astype(F32)

        @pl.when(mids)
        def _():
            for cp in third(e):
                cp.wait()
            ai[1, 0:256] += nt_all[2, 0:256, 0:512].astype(F32)
            ad[1, at] += nt_all[3, 0:128].astype(F32)

        gin[e, z] = ai[1, 0:256].astype(BF)
    o2 = pltpu.make_async_copy(gin.at[:, z], xe, lsem.at[2])
    o3 = pltpu.make_async_copy(ad.at[1, 0:256], gde, lsem.at[3])
    o2.start()
    o3.start()
    for w in range(2):
        for q in range(4):
            give1(q, w).wait_send()
        give2(0, 0, d2, w).wait_send()
        give2(1, 1, d1, w).wait_send()
        give2(2, 2, d2, w).wait_send()
    for e in range(2):
        zsum.sent(e)
    for cp in (o0, o1, o2, o3):
        cp.wait()
    for cp in sends:
        cp.wait_send()


def run_ff(lengths, nt, wmix, s2, g_all, wi_all, wd_all):
    sd = jax.ShapeDtypeStruct
    dma = pltpu.SemaphoreType.DMA
    out = pl.pallas_call(
        ff_kernel,
        out_shape=(
            sd((384, 1024), BF), sd((384, 1024), F32), sd((384, 128), F32),
            sd((256, 1024), F32), sd((2, 256, 512), BF), sd((1024, 512), F32), sd((512, 1024), F32),
            sd((2, 4, 384, 1024), BF), sd((2, 3, 384, 1024), BF),
            sd((2, 3, 256, 512), BF), sd((2, 3, 128, 1024), BF),
            sd((4, 256, 512), BF), sd((4, 128, 1024), BF),
        ),
        in_specs=[SM, ANY, VM, ANY, ANY, ANY, ANY],
        out_specs=(VM,) * 3 + (ANY,) * 10,
        scratch_shapes=[
            pltpu.VMEM((8, 384, 1024), BF), pltpu.VMEM((2, 400, 1024), BF),
            pltpu.VMEM((8, 384, 1024), BF), pltpu.VMEM((8, 384, 1024), BF),
            pltpu.VMEM((2, 8, 112, 1024), BF), pltpu.VMEM((2, 8, 112, 1024), BF),
            pltpu.VMEM((2, 4, 256, 512), BF), pltpu.VMEM((2, 4, 128, 1024), BF),
            pltpu.VMEM((2, 1024, 512), F32), pltpu.VMEM((2, 512, 1024), F32),
            pltpu.VMEM((2, 4, 256, 512), BF), pltpu.VMEM((2, 4, 128, 1024), BF),
            pltpu.VMEM((2, 256, 512), BF), pltpu.VMEM((2, 128, 1024), BF),
            pltpu.VMEM((2, 384, 1024), BF),
            pltpu.VMEM((8, 16, 384), F32), pltpu.VMEM((8, 16, 384), F32), pltpu.VMEM((2, 8, 112, 128), BF),
            dma((7,)), dma((8,)), dma((2,)), dma((2, 2)), dma((1, 8)), dma((1, 8)), dma((2, 8)), dma((2, 8)),
            dma((2, 4)), dma((2, 4)), dma((2, 3)), dma((2, 3)), dma((7,)), dma((8,)), dma((10,)), dma((2,)),
        ],
        compiler_params=pltpu.CompilerParams(
            collective_id=1, has_side_effects=True, vmem_limit_bytes=63 * MIB
        ),
    )(lengths, nt, wmix, s2, g_all, wi_all, wd_all)
    return out[:7]


class RowSum:
    swap = (0, 2, 1, 3)

    def __init__(self, P_, g, r1, r2, r3, sems):
        self.P, self.g, self.r1, self.r2, self.r3 = P_, g, r1, r2, r3
        self.s1s, self.s1r, self.s2s, self.s2r, self.s3s, self.s3r = sems
        self.chips = (P_.dd, P_.d1, P_.d2, P_.own)

    def rank(self, q):
        return self.P.rank(self.chips[q])

    def copy1(self, n, q):
        k = self.swap[q]
        src = self.g.at[n, self.P.rank(self.P.flip(self.chips[q]))]
        return rcopy(src, self.r1.at[n, k], self.s1s.at[n, k], self.s1r.at[n, k], self.P.dev(self.P.sib))

    def copy2(self, n, q, k, p):
        src = self.g.at[n, self.rank(q)]
        return rcopy(src, self.r2.at[n, k], self.s2s.at[n, k], self.s2r.at[n, k], self.P.dev(p))

    def copy3(self, n, k):
        P_ = self.P
        return rcopy(
            self.g.at[n, P_.t, P_.zk[k]], self.r3.at[n, k - 1], self.s3s.at[n, k - 1],
            self.s3r.at[n, k - 1], P_.dev(P_.own, P_.zk[k]),
        )

    def in1(self, n, q):
        rcopy(
            self.g.at[n, 0], self.r1.at[n, q], self.s1s.at[n, 0], self.s1r.at[n, q], self.P.dev(self.P.sib)
        ).wait_recv()
        r = self.rank(q)
        self.g[n, r] = self.g[n, r] + self.r1[n, q]

    def in2(self, n, k, q):
        rcopy(
            self.g.at[n, 0], self.r2.at[n, k], self.s2s.at[n, 0], self.s2r.at[n, k], self.P.dev(self.P.sib)
        ).wait_recv()
        r = self.rank(q)
        self.g[n, r] = self.g[n, r] + self.r2[n, k]

    def step1(self, n):
        for q in (0, 1, 2, 3):
            self.copy1(n, q).start()

    def step2(self, n):
        P_ = self.P
        self.in1(n, 0)
        self.copy2(n, 0, 0, P_.d2).start()
        self.in1(n, 2)
        self.copy2(n, 2, 2, P_.d2).start()
        self.in1(n, 1)

    def step3(self, n):
        self.in2(n, 0, 1)
        self.copy2(n, 1, 1, self.P.d1).start()
        self.in1(n, 3)

    def step4(self, n):
        self.in2(n, 2, 3)
        self.in2(n, 1, 3)
        for k in (3, 2, 1):
            self.copy3(n, k).start()

    def step5(self, n):
        P_ = self.P
        for k in (1, 2, 3):
            rcopy(
                self.g.at[n, 0, 0], self.r3.at[n, k - 1], self.s3s.at[n, 0], self.s3r.at[n, k - 1],
                P_.dev(P_.sib),
            ).wait_recv()
        total = self.g[n, P_.t, P_.z].astype(F32)
        for k in range(3):
            total += self.r3[n, k].astype(F32)
        return total

    def sent(self, n):
        P_ = self.P
        for q in range(4):
            self.copy1(n, q).wait_send()
        self.copy2(n, 0, 0, P_.d2).wait_send()
        self.copy2(n, 2, 2, P_.d2).wait_send()
        self.copy2(n, 1, 1, P_.d1).wait_send()
        for k in (1, 2, 3):
            self.copy3(n, k).wait_send()


def back_kernel(
    len_ref, tok, gt, s2, nt, n1, qkv, lse, att, gsum, gl, pack_all, dgi, dgd, xe,
    gtok, gqkv, gwo, gex, gdd, gx,
    pack_v, gq, gacc, n1t, ga_, gb_, gc_, ra1, ra2, ra3, rb1, rb2, rb3, rc1, rc2, rc3,
    di, dj, gin, gdn, rin, rdn, tri, trd, *sems,
):
    P_ = Place()
    z, t = P_.z, P_.t
    own, sib, d1, d2, dd = P_.own, P_.sib, P_.d1, P_.d2, P_.dd
    others = P_.plane_others()
    zss, zsr, xs, xr, lsem = sems[18:]
    sum_a = RowSum(P_, ga_, ra1, ra2, ra3, sems[0:6])
    sum_b = RowSum(P_, gb_, rb1, rb2, rb3, sems[6:12])
    sum_c = RowSum(P_, gc_, rc1, rc2, rc3, sems[12:18])
    lw = pltpu.make_async_copy(pack_all, pack_v, lsem.at[0])
    li = pltpu.make_async_copy(dgi, di, lsem.at[1])
    lj = pltpu.make_async_copy(dgd, dj, lsem.at[2])
    li.start()
    lj.start()
    lw.start()
    meet([P_.dev(p) for p in others] + [P_.dev(own, zz) for zz in P_.zk[1:]])
    sends = []

    def go(cp):
        cp.start()
        sends.append(cp)

    def rows(p):
        return pl.ds(pl.multiple_of(P_.rank(p) * 32, 32), 32)

    zsum = ZSum(P_, (gin, gdn), (rin, rdn), (tri, trd), zss, zsr)
    li.wait()
    lj.wait()
    gin[0] = di[...].astype(BF).reshape(4, 256, 512)
    gdn[0] = dj[...].astype(BF).reshape(4, 128, 1024)
    zsum.ship(0)
    le = pltpu.make_async_copy(xe.at[:, rows(own)], gx.at[t, 1:3], lsem.at[3])
    le.start()
    for i, p in enumerate(others):
        go(rcopy(xe.at[:, rows(p)], gx.at[t, 1:3], xs.at[i], xr.at[t, 0], P_.dev(p)))

    lw.wait()
    extra = pack_v[:, :, EX : EX + 128].reshape(1024, 128)
    lane = lax.broadcasted_iota(jnp.int32, (384, 128), 1)
    glv = gl[...]
    gnt = gsum[...] + glv[:, 0:1] * (row_of(extra, 0) - row_of(extra, 1))
    two = jnp.where(lane == 0, glv, jnp.where(lane == 1, -glv, 0.0)).astype(BF)
    n_two, r_two = norm_parts(s2[...])
    gain_two_row = jnp.sum(gnt * n_two, axis=0, keepdims=True)

    def norm_back(gv, gain, n, r):
        tt = gv * gain
        return r * (tt - jnp.mean(tt, -1, keepdims=True) - n * jnp.mean(tt * n, -1, keepdims=True))

    gs2 = gt[0:384].astype(F32) + norm_back(gnt, row_of(extra, 3), n_two, r_two)
    gtok[...] = gs2
    ga = gs2.astype(BF)

    def put(ref, n, cols, val):
        low = val.astype(BF)
        for zz in range(4):
            ref[n, :, zz, :, cols] = low[zz * 256 : (zz + 1) * 256].reshape(8, 32, low.shape[1])

    for j in range(2):
        cols = slice(j * 512, (j + 1) * 512)
        put(ga_, 0, cols, dot_tn(att[...], ga[:, cols]))
    sum_a.step1(0)
    gatt = dot_nt(ga[:, 0:512], pack_v[:, :, WO : WO + 512].reshape(1024, 512))
    gatt += dot_nt(ga[:, 512:1024], pack_v[:, :, WO + 512 : WO + 1024].reshape(1024, 512))
    gq[:, 0:1024] = gatt.astype(BF)
    n1t[...] = jnp.transpose(n1[...])
    gacc[...] = jnp.zeros_like(gacc)
    allowed = masks(len_ref[0])
    sum_a.step2(0)

    def pair_step(p, carry):
        lo = pl.ds(pl.multiple_of(p * 128, 128), 128)
        mid = pl.ds(pl.multiple_of(1024 + p * 128, 128), 128)
        hi = pl.ds(pl.multiple_of(2048 + p * 128, 128), 128)
        q2, k2, v2, do = qkv[:, lo], qkv[:, mid], qkv[:, hi], gq[:, lo]
        dq = dk = dv = None
        for hh in range(2):
            mine = lane // 64 == hh
            zero = jnp.zeros_like(q2)
            qm, km, dm = (jnp.where(mine, v, zero) for v in (q2, k2, do))
            total = jnp.sum(jnp.where(lane == 2 * p + hh, lse[...], 0.0), axis=-1, keepdims=True)
            sc = dot_nt(qm, k2) * 0.125
            pf = jnp.where(allowed, jnp.exp(sc - total), 0.0)
            gp = dot_nt(dm, v2)
            ds = (pf * (gp - jnp.sum(pf * gp, axis=-1, keepdims=True))).astype(BF)
            terms = (dot_nn(ds, km), dot_tn(ds, qm), dot_tn(pf.astype(BF), dm))
            dq, dk, dv = terms if hh == 0 else (dq + terms[0], dk + terms[1], dv + terms[2])
        gq[:, lo] = (dq * 0.125).astype(BF)
        gq[:, mid] = (dk * 0.125).astype(BF)
        gq[:, hi] = dv.astype(BF)
        return carry

    def chunk_step(j, carry):
        lax.fori_loop(2 * j, 2 * j + 2, pair_step, 0)
        for seg in range(3):
            cols = pl.ds(pl.multiple_of(seg * 1024 + j * 256, 256), 256)
            gcols = gq[:, cols]
            put(gb_, j, slice(seg * 256, (seg + 1) * 256), dot_nn(n1t[...], gcols))
            gacc[...] += dot_nt(gcols, pack_v[:, :, cols].reshape(1024, 256))
        sum_b.step1(j)

        @pl.when(j == 0)
        def _():
            zsum.transit(0)
            sum_a.step3(0)

        @pl.when(j == 1)
        def _():
            sum_a.step4(0)

        @pl.when(j >= 1)
        def _():
            sum_b.step2(j - 1)

        @pl.when(j >= 2)
        def _():
            sum_b.step3(j - 2)

        @pl.when(j >= 3)
        def _():
            sum_b.step4(j - 3)

        return carry

    lax.fori_loop(0, 4, chunk_step, 0)
    gn1 = gacc[...]
    n_one, r_one = norm_parts(tok[...].astype(F32))
    gain_one_row = jnp.sum(gn1 * n_one, axis=0, keepdims=True)
    rowi = lax.broadcasted_iota(jnp.int32, (8, 1024), 0)
    rws = jnp.where(rowi == 0, gain_one_row, jnp.where(rowi == 1, gain_two_row, 0.0)).astype(BF)
    sel = (
        lax.broadcasted_iota(jnp.int32, (8, 128), 1) == lax.broadcasted_iota(jnp.int32, (8, 128), 0) + 2
    ).astype(BF)
    put(gc_, 0, slice(0, 128), dot_tn(nt[...], two) + dot_tn(rws, sel))
    sum_c.step1(0)
    sum_b.step2(3)
    sum_b.step3(2)
    sum_c.step2(0)
    gtok[...] += norm_back(gn1, row_of(extra, 2), n_one, r_one)
    sum_b.step3(3)
    sum_b.step4(1)
    sum_c.step3(0)

    zsum.arrived(0)
    di[0:256] = gin[0, z].astype(F32) + rin[0, 0].astype(F32) + rin[0, 1].astype(F32)
    gdd[...] = gdn[0, z].astype(F32) + rdn[0, 0].astype(F32) + rdn[0, 1].astype(F32)

    @pl.when(zsum.mid)
    def _():
        di[0:256] += rin[0, 2].astype(F32)
        gdd[...] += rdn[0, 2].astype(F32)

    gin[0, z] = di[0:256].astype(BF)
    lx = pltpu.make_async_copy(gin.at[:, z, rows(own)], gx.at[t, 0:1], lsem.at[4])
    lx.start()
    for i, p in enumerate(others):
        go(rcopy(gin.at[:, z, rows(p)], gx.at[t, 0:1], xs.at[7 + i], xr.at[t, 1], P_.dev(p)))

    sum_b.step4(2)
    sum_b.step4(3)
    sum_c.step4(0)
    gwo[...] = sum_a.step5(0)
    for j in range(4):
        total = sum_b.step5(j)
        for seg in range(3):
            at = seg * 1024 + j * 256
            gqkv[:, at : at + 256] = total[:, seg * 256 : (seg + 1) * 256]
    gex[...] = sum_c.step5(0)
    for p in others:
        r = P_.rank(p)
        rcopy(xe.at[:, rows(own)], gx.at[r, 1:3], xs.at[0], xr.at[r, 0], P_.dev(sib)).wait_recv()
        rcopy(gin.at[:, 0, rows(own)], gx.at[r, 0:1], xs.at[0], xr.at[r, 1], P_.dev(sib)).wait_recv()
    le.wait()
    lx.wait()
    zsum.sent(0)
    sum_a.sent(0)
    for j in range(4):
        sum_b.sent(j)
    sum_c.sent(0)
    for cp in sends:
        cp.wait_send()


def run_back(lengths, tok, gt, s2, nt, n1, qkv, lse, att, gsum, gl, pack_all, dgi, dgd, xe):
    sd = jax.ShapeDtypeStruct
    dma = pltpu.SemaphoreType.DMA
    sizes = ((1, 1024), (4, 768), (1, 128))
    blocks = [pltpu.VMEM((n, 8, 4, 32, w), BF) for n, w in sizes]
    for n, w in sizes:
        blocks += [
            pltpu.VMEM((n, 4, 4, 32, w), BF), pltpu.VMEM((n, 3, 4, 32, w), BF), pltpu.VMEM((n, 3, 32, w), BF),
        ]
    sems = []
    for n, _ in sizes:
        sems += [dma((n, 4)), dma((n, 4)), dma((n, 3)), dma((n, 3)), dma((n, 3)), dma((n, 3))]
    return pl.pallas_call(
        back_kernel,
        out_shape=(
            sd((384, 1024), F32), sd((32, 3072), F32), sd((32, 1024), F32), sd((32, 128), F32),
            sd((128, 1024), F32), sd((8, 3, 32, 512), BF),
        ),
        in_specs=[SM] + [VM] * 10 + [ANY] * 4,
        out_specs=(VM,) * 5 + (ANY,),
        scratch_shapes=[
            pltpu.VMEM((32, 32, PW), BF), pltpu.VMEM((384, 3072), BF), pltpu.VMEM((384, 1024), F32),
            pltpu.VMEM((1024, 384), BF), *blocks,
            pltpu.VMEM((1024, 512), F32), pltpu.VMEM((512, 1024), F32),
            pltpu.VMEM((1, 4, 256, 512), BF), pltpu.VMEM((1, 4, 128, 1024), BF),
            pltpu.VMEM((1, 3, 256, 512), BF), pltpu.VMEM((1, 3, 128, 1024), BF),
            pltpu.VMEM((1, 256, 512), BF), pltpu.VMEM((1, 128, 1024), BF),
            *sems, dma((1, 8)), dma((1, 8)), dma((14,)), dma((8, 2)), dma((5,)),
        ],
        compiler_params=pltpu.CompilerParams(
            collective_id=2, has_side_effects=True, vmem_limit_bytes=63 * MIB
        ),
    )(lengths, tok, gt, s2, nt, n1, qkv, lse, att, gsum, gl, pack_all, dgi, dgd, xe)


def fused_device(
    tokens, cotangent, lengths, expert_ids, slot_ids, w_qkv, w_out, gain_one, w_in, w_down,
    w_expert_in, w_expert_out, w_mix, gain_two,
):
    keep = jnp.arange(384, dtype=jnp.int32) < lengths[0]
    table = jnp.where(slot_ids >= 0, expert_ids * CAP + slot_ids, -1).astype(BF)
    gt = jnp.concatenate(
        [
            jnp.where(keep[:, None], cotangent, jnp.zeros_like(cotangent)),
            jnp.pad(table[None, :], ((0, 15), (0, 640))),
        ],
        axis=0,
    )
    pack = jnp.concatenate(
        [
            w_qkv, w_mix, gain_one[:, None], gain_two[:, None],
            jnp.zeros((32, 124), BF), w_out,
        ],
        axis=1,
    )
    wia = jnp.concatenate([w_in[None], w_expert_in], axis=0)
    wia = wia.reshape(3, 32, 4, 8, 128).transpose(3, 0, 1, 2, 4).reshape(8, 3, 32, 512)
    wdn = jnp.concatenate([w_down[None], w_expert_out], axis=0)
    qkv, lse, att, s2, nt, n1, wmix, pack_all, wi_all, wd_all, g_all = run_enter(
        lengths, tokens, pack, wia, wdn, gt
    )
    block, gsum, gl, gde, xe, dgi, dgd = run_ff(lengths, nt, wmix, s2, g_all, wi_all, wd_all)
    gtok, gqkv, gwo, gex, gdd, gx = run_back(
        lengths, tokens, gt, s2, nt, n1, qkv, lse, att, gsum, gl, pack_all, dgi, dgd, xe
    )
    gwi = gx.reshape(8, 3, 32, 4, 128).transpose(1, 2, 3, 0, 4).reshape(3, 32, 4096).astype(F32)
    return (
        block, gtok, gqkv, gwo, gex[:, 2], gwi[0], gdd, gwi[1:], gde.reshape(2, 128, 1024),
        gex[:, 0:2], gex[:, 3],
    )


def solution(mesh):
    placed = (
        P(("dp", "fsdp"), None),
        P(("dp", "fsdp"), None),
        P(("dp", "fsdp")),
        P(("dp", "fsdp")),
        P(("dp", "fsdp")),
        P(("dp", "fsdp"), None),
        P(("dp", "fsdp"), None),
        P(("dp", "fsdp")),
        P(("dp", "fsdp"), None),
        P(("dp", "fsdp"), None),
        P(None, ("dp", "fsdp"), None),
        P(None, ("dp", "fsdp"), None),
        P(("dp", "fsdp"), None),
        P(("dp", "fsdp")),
    )
    fused = (mesh.shape["dp"], mesh.shape["fsdp"]) == (8, 4)
    return jax.shard_map(
        fused_device if fused else per_device,
        mesh=mesh,
        in_specs=placed,
        out_specs=(
            P(("dp", "fsdp"), None),
            P(("dp", "fsdp"), None),
            P(("dp", "fsdp"), None),
            P(("dp", "fsdp"), None),
            P(("dp", "fsdp")),
            P(("dp", "fsdp"), None),
            P(("dp", "fsdp"), None),
            P(None, ("dp", "fsdp"), None),
            P(None, ("dp", "fsdp"), None),
            P(("dp", "fsdp"), None),
            P(("dp", "fsdp")),
        ),
        check_vma=False,
    )
```

```python
import jax
import jax.numpy as jnp
from jax import lax
from jax.experimental import pallas as pl
from jax.experimental.pallas import tpu as pltpu
from jax.sharding import PartitionSpec as P

HEAD_DIM = 64
EXPERTS = 2
CAP = 112


def layer_norm(values_in, gain_vec):
    average = jnp.mean(values_in, axis=-1, keepdims=True)
    centred = values_in - average
    variance = jnp.mean(centred * centred, axis=-1, keepdims=True)
    return centred * lax.rsqrt(variance + 1e-05) * gain_vec


def gelu_tanh(values_in):
    return jax.nn.gelu(values_in, approximate=True)


def gelu_back(values_in, grad_in):
    return jax.vjp(gelu_tanh, values_in)[1](grad_in)[0]


def head_scores(query_h, key_h, allowed, score_scale):
    scores = (
        jnp.einsum("qd,kd->qk", query_h, key_h, preferred_element_type=jnp.float32) * score_scale
    )
    return jnp.where(allowed, scores, -1e30)


def head_forward(entries, allowed, score_scale):
    query_h, key_h, value_h = entries
    scores = head_scores(query_h, key_h, allowed, score_scale)
    row_max = jnp.max(scores, axis=-1, keepdims=True)
    exp_scores = jnp.exp(scores - row_max)
    row_total = jnp.sum(exp_scores, axis=-1, keepdims=True)
    prob_low = (exp_scores / row_total).astype(jnp.bfloat16)
    head_out = jnp.dot(prob_low, value_h, preferred_element_type=jnp.float32)
    return (head_out, (row_max + jnp.log(row_total))[:, 0])


def head_backward(entries, allowed, score_scale):
    query_h, key_h, value_h, grad_head, log_total = entries
    scores = head_scores(query_h, key_h, allowed, score_scale)
    prob_full = jnp.where(allowed, jnp.exp(scores - log_total[:, None]), 0.0)
    prob_low = prob_full.astype(jnp.bfloat16)
    grad_value = jnp.einsum("qk,qd->kd", prob_low, grad_head, preferred_element_type=jnp.float32)
    grad_prob = jnp.einsum("qd,kd->qk", grad_head, value_h, preferred_element_type=jnp.float32)
    grad_score = prob_full * (grad_prob - jnp.sum(prob_full * grad_prob, axis=-1, keepdims=True))
    grad_score = grad_score.astype(jnp.bfloat16)
    grad_query = jnp.dot(grad_score, key_h, preferred_element_type=jnp.float32) * score_scale
    grad_key = (
        jnp.einsum("qk,qd->kd", grad_score, query_h, preferred_element_type=jnp.float32)
        * score_scale
    )
    return (grad_query, grad_key, grad_value)


def per_device(
    tokens,
    cotangent,
    lengths,
    expert_ids,
    slot_ids,
    w_qkv,
    w_out,
    gain_one,
    w_in,
    w_down,
    w_expert_in,
    w_expert_out,
    w_mix,
    gain_two,
):
    row_count, model_width = tokens.shape
    head_count = model_width // HEAD_DIM
    score_scale = HEAD_DIM ** (-0.5)
    full_qkv, full_out, full_gain_one = (
        lax.all_gather(w_qkv, ("dp", "fsdp"), axis=0, tiled=True),
        lax.all_gather(w_out, ("dp", "fsdp"), axis=0, tiled=True),
        lax.all_gather(gain_one, ("dp", "fsdp"), axis=0, tiled=True),
    )
    full_in, full_down, full_expert_in, full_expert_out, full_mix, full_gain_two = (
        lax.all_gather(w_in, ("dp", "fsdp"), axis=0, tiled=True),
        lax.all_gather(w_down, ("dp", "fsdp"), axis=0, tiled=True),
        lax.all_gather(w_expert_in, ("dp", "fsdp"), axis=1, tiled=True),
        lax.all_gather(w_expert_out, ("dp", "fsdp"), axis=1, tiled=True),
        lax.all_gather(w_mix, ("dp", "fsdp"), axis=0, tiled=True),
        lax.all_gather(gain_two, ("dp", "fsdp"), axis=0, tiled=True),
    )
    position = jnp.arange(row_count, dtype=jnp.int32)
    seq_len = lengths[0]
    row_keep = (position < seq_len).astype(jnp.float32)[:, None]
    allowed = (position[None, :] <= position[:, None]) & (position[None, :] < seq_len)

    def to_heads(block):
        return block.reshape(row_count, head_count, HEAD_DIM).transpose(1, 0, 2)

    def from_heads(block):
        return block.transpose(1, 0, 2).reshape(row_count, model_width)

    stream = tokens.astype(jnp.float32)
    gain_first = full_gain_one.astype(jnp.float32)
    normed_one = layer_norm(stream, gain_first).astype(jnp.bfloat16)
    qkv_all = jnp.dot(normed_one, full_qkv, preferred_element_type=jnp.float32).astype(jnp.bfloat16)
    queries = to_heads(qkv_all[:, :model_width])
    key_heads = to_heads(qkv_all[:, model_width : 2 * model_width])
    value_heads = to_heads(qkv_all[:, 2 * model_width :])
    head_out, log_total = lax.map(
        lambda entries: head_forward(entries, allowed, score_scale),
        (queries, key_heads, value_heads),
    )
    attended = from_heads(head_out).astype(jnp.bfloat16)
    stream_two = stream + jnp.dot(attended, full_out, preferred_element_type=jnp.float32)
    gain_second = full_gain_two.astype(jnp.float32)
    normed_two = layer_norm(stream_two, gain_second).astype(jnp.bfloat16)
    dense_up = jnp.dot(normed_two, full_in, preferred_element_type=jnp.float32)
    dense_act = gelu_tanh(dense_up).astype(jnp.bfloat16)
    dense_out = jnp.dot(dense_act, full_down, preferred_element_type=jnp.float32)
    routed = slot_ids >= 0
    table_row = jnp.where(routed, expert_ids * CAP + slot_ids, 0)
    slot_total = EXPERTS * CAP
    dispatch = (
        (table_row[None, :] == jnp.arange(slot_total, dtype=jnp.int32)[:, None]) & routed[None, :]
    ).astype(jnp.bfloat16)
    buffer = jnp.dot(dispatch, normed_two, preferred_element_type=jnp.float32).astype(jnp.bfloat16)
    buffer = buffer.reshape(EXPERTS, CAP, model_width)
    expert_up = jnp.einsum(
        "ecd,edf->ecf", buffer, full_expert_in, preferred_element_type=jnp.float32
    )
    expert_act = gelu_tanh(expert_up).astype(jnp.bfloat16)
    expert_y = jnp.einsum(
        "ecf,efd->ecd", expert_act, full_expert_out, preferred_element_type=jnp.float32
    )
    expert_y = expert_y.reshape(slot_total, model_width)
    expert_mix = jnp.where(routed[:, None], expert_y[table_row], 0.0)
    logits = jnp.dot(normed_two, full_mix, preferred_element_type=jnp.float32)
    mix_coeff = jax.nn.softmax(logits, axis=-1)
    branch = mix_coeff[:, 0:1] * dense_out + mix_coeff[:, 1:2] * expert_mix
    block_out = ((stream_two + branch) * row_keep).astype(jnp.bfloat16)
    grad_out = cotangent.astype(jnp.float32) * row_keep
    grad_dense = (mix_coeff[:, 0:1] * grad_out).astype(jnp.bfloat16)
    grad_expert = (mix_coeff[:, 1:2] * grad_out).astype(jnp.bfloat16)
    grad_coeff = jnp.stack(
        [jnp.sum(grad_out * dense_out, axis=-1), jnp.sum(grad_out * expert_mix, axis=-1)], axis=-1
    )
    grad_logits = jax.vjp(lambda values_in: jax.nn.softmax(values_in, axis=-1), logits)[1](
        grad_coeff
    )[0]
    full_in, full_down, full_expert_in, full_expert_out, full_mix, full_gain_two = (
        lax.all_gather(w_in, ("dp", "fsdp"), axis=0, tiled=True),
        lax.all_gather(w_down, ("dp", "fsdp"), axis=0, tiled=True),
        lax.all_gather(w_expert_in, ("dp", "fsdp"), axis=1, tiled=True),
        lax.all_gather(w_expert_out, ("dp", "fsdp"), axis=1, tiled=True),
        lax.all_gather(w_mix, ("dp", "fsdp"), axis=0, tiled=True),
        lax.all_gather(gain_two, ("dp", "fsdp"), axis=0, tiled=True),
    )
    gain_second = full_gain_two.astype(jnp.float32)
    grad_w_down = jnp.einsum("tf,td->fd", dense_act, grad_dense, preferred_element_type=jnp.float32)
    grad_dense_act = jnp.einsum(
        "td,fd->tf", grad_dense, full_down, preferred_element_type=jnp.float32
    )
    grad_dense_up = gelu_back(dense_up, grad_dense_act).astype(jnp.bfloat16)
    grad_w_in = jnp.einsum(
        "td,tf->df", normed_two, grad_dense_up, preferred_element_type=jnp.float32
    )
    grad_normed_two = jnp.einsum(
        "tf,df->td", grad_dense_up, full_in, preferred_element_type=jnp.float32
    )
    grad_y = jnp.dot(dispatch, grad_expert, preferred_element_type=jnp.float32).astype(jnp.bfloat16)
    grad_y = grad_y.reshape(EXPERTS, CAP, model_width)
    grad_expert_out_lead = jnp.einsum(
        "ecf,ecd->fed", expert_act, grad_y, preferred_element_type=jnp.float32
    )
    grad_expert_act = jnp.einsum(
        "ecd,efd->ecf", grad_y, full_expert_out, preferred_element_type=jnp.float32
    )
    grad_expert_up = gelu_back(expert_up, grad_expert_act).astype(jnp.bfloat16)
    grad_expert_in_lead = jnp.einsum(
        "ecd,ecf->def", buffer, grad_expert_up, preferred_element_type=jnp.float32
    )
    grad_buffer = jnp.einsum(
        "ecf,edf->ecd", grad_expert_up, full_expert_in, preferred_element_type=jnp.float32
    )
    grad_buffer = grad_buffer.reshape(slot_total, model_width)
    grad_normed_two = grad_normed_two + jnp.where(routed[:, None], grad_buffer[table_row], 0.0)
    mix_full = full_mix.astype(jnp.float32)
    normed_full = normed_two.astype(jnp.float32)
    grad_normed_two = grad_normed_two + jnp.dot(
        grad_logits, mix_full.T, precision=lax.Precision.HIGHEST
    )
    grad_w_mix = jnp.dot(normed_full.T, grad_logits, precision=lax.Precision.HIGHEST)
    _, pull_two = jax.vjp(layer_norm, stream_two, gain_second)
    grad_stream_ln, grad_gain_two = pull_two(grad_normed_two)
    grad_stream_two = grad_out + grad_stream_ln
    full_qkv, full_out, full_gain_one = (
        lax.all_gather(w_qkv, ("dp", "fsdp"), axis=0, tiled=True),
        lax.all_gather(w_out, ("dp", "fsdp"), axis=0, tiled=True),
        lax.all_gather(gain_one, ("dp", "fsdp"), axis=0, tiled=True),
    )
    gain_first = full_gain_one.astype(jnp.float32)
    grad_attn = grad_stream_two.astype(jnp.bfloat16)
    grad_w_out = jnp.einsum("td,te->de", attended, grad_attn, preferred_element_type=jnp.float32)
    grad_attended = jnp.einsum(
        "te,de->td", grad_attn, full_out, preferred_element_type=jnp.float32
    ).astype(jnp.bfloat16)
    grad_query, grad_key, grad_value = lax.map(
        lambda entries: head_backward(entries, allowed, score_scale),
        (queries, key_heads, value_heads, to_heads(grad_attended), log_total),
    )
    grad_qkv = jnp.concatenate(
        [from_heads(grad_query), from_heads(grad_key), from_heads(grad_value)], axis=1
    ).astype(jnp.bfloat16)
    grad_w_qkv = jnp.einsum("td,te->de", normed_one, grad_qkv, preferred_element_type=jnp.float32)
    grad_normed_one = jnp.einsum(
        "te,de->td", grad_qkv, full_qkv, preferred_element_type=jnp.float32
    )
    _, pull_one = jax.vjp(layer_norm, stream, gain_first)
    grad_stream_one, grad_gain_one = pull_one(grad_normed_one)
    grad_tokens = grad_stream_two + grad_stream_one
    (
        part_qkv,
        part_out,
        part_gain_one,
        part_in,
        part_down,
        lead_expert_in,
        lead_expert_out,
        part_mix,
        part_gain_two,
    ) = (
        lax.psum_scatter(grad_w_qkv, ("dp", "fsdp"), scatter_dimension=0, tiled=True),
        lax.psum_scatter(grad_w_out, ("dp", "fsdp"), scatter_dimension=0, tiled=True),
        lax.psum_scatter(grad_gain_one, ("dp", "fsdp"), scatter_dimension=0, tiled=True),
        lax.psum_scatter(grad_w_in, ("dp", "fsdp"), scatter_dimension=0, tiled=True),
        lax.psum_scatter(grad_w_down, ("dp", "fsdp"), scatter_dimension=0, tiled=True),
        lax.psum_scatter(grad_expert_in_lead, ("dp", "fsdp"), scatter_dimension=0, tiled=True),
        lax.psum_scatter(grad_expert_out_lead, ("dp", "fsdp"), scatter_dimension=0, tiled=True),
        lax.psum_scatter(grad_w_mix, ("dp", "fsdp"), scatter_dimension=0, tiled=True),
        lax.psum_scatter(grad_gain_two, ("dp", "fsdp"), scatter_dimension=0, tiled=True),
    )
    part_expert_in = lead_expert_in.transpose(1, 0, 2)
    part_expert_out = lead_expert_out.transpose(1, 0, 2)
    return (
        block_out,
        grad_tokens,
        part_qkv,
        part_out,
        part_gain_one,
        part_in,
        part_down,
        part_expert_in,
        part_expert_out,
        part_mix,
        part_gain_two,
    )


BF = jnp.bfloat16
F32 = jnp.float32
MESH = pl.DeviceIdType.MESH
ANY = pl.BlockSpec(memory_space=pl.ANY)
VM = pl.BlockSpec(memory_space=pltpu.VMEM)
SM = pl.BlockSpec(memory_space=pltpu.SMEM)
MIB = 1024 * 1024


def dot_nn(a, b):
    return lax.dot_general(a, b, (((1,), (0,)), ((), ())), preferred_element_type=F32)


def dot_nt(a, b):
    return lax.dot_general(a, b, (((1,), (1,)), ((), ())), preferred_element_type=F32)


def dot_tn(a, b):
    return lax.dot_general(a, b, (((0,), (0,)), ((), ())), preferred_element_type=F32)


class Place:
    def __init__(self):
        dp, fs = lax.axis_index("dp"), lax.axis_index("fsdp")
        z, y, x, c = dp // 2, dp % 2, fs // 2, fs % 2
        self.z, self.y, self.x, self.c = z, y, x, c
        self.own = (y, x, c)
        self.sib = (y, x, 1 - c)
        self.d1 = ((y + c) % 2, (x + 1 - c) % 2, c)
        self.d2 = ((y + 1 - c) % 2, (x + c) % 2, c)
        self.dd = (1 - y, 1 - x, c)
        self.zk = [z, z + 1 - 2 * (z % 2), (z + 2) % 4, 3 - z]
        self.t = self.rank(self.own)
        self.b = z * 8 + self.t

    @staticmethod
    def rank(p):
        return p[0] * 4 + p[1] * 2 + p[2]

    def flip(self, p):
        return (p[0], p[1], 1 - p[2])

    def dev(self, p, z=None):
        z = self.z if z is None else z
        return (z * 2 + p[0], p[1] * 2 + p[2])

    def plane_others(self):
        y, x, c = self.own
        return [
            ((y + k // 4) % 2, (x + (k // 2) % 2) % 2, (c + k % 2) % 2) for k in range(1, 8)
        ]


def rcopy(src, dst, send, recv, dev):
    return pltpu.make_async_remote_copy(
        src_ref=src, dst_ref=dst, send_sem=send, recv_sem=recv, device_id=dev, device_id_type=MESH
    )


def meet(devs):
    bar = pltpu.get_barrier_semaphore()
    for dev in devs:
        pl.semaphore_signal(bar, inc=1, device_id=dev, device_id_type=MESH)
    pl.semaphore_wait(bar, len(devs))


def norm_parts(v):
    mean = jnp.mean(v, axis=-1, keepdims=True)
    cen = v - mean
    var = jnp.mean(cen * cen, axis=-1, keepdims=True)
    r = lax.rsqrt(var + 1e-05)
    return cen * r, r


def row_of(extra, lane):
    pick = (lax.broadcasted_iota(jnp.int32, (8, 128), 1) == lane).astype(BF)
    return dot_nt(pick, extra)[0:1]


class ZSum:
    def __init__(self, P_, src, land, via, send, recv):
        self.P, self.src, self.land, self.via = P_, src, land, via
        self.send, self.recv = send, recv
        self.mid = (P_.z == 1) | (P_.z == 2)

    def copy(self, n, w, j):
        P_ = self.P
        to = P_.dev(P_.own, P_.zk[1 if j == 4 else j])
        block = self.src[w].at[n, P_.zk[3 if j == 4 else j]]
        dst = self.via[w].at[n] if j == 4 else self.land[w].at[n, j - 1]
        i = w * 4 + j - 1
        return rcopy(block, dst, self.send.at[n, i], self.recv.at[n, i], to)

    def ship(self, n):
        @pl.when(self.mid)
        def _():
            for j in (3, 1):
                for w in range(2):
                    self.copy(n, w, j).start()

        @pl.when(jnp.logical_not(self.mid))
        def _():
            for j in (4, 2, 1):
                for w in range(2):
                    self.copy(n, w, j).start()

    def transit(self, n):
        @pl.when(self.mid)
        def _():
            k2 = self.P.zk[2]
            for w in range(2):
                self.copy(n, w, 4).wait_recv()
                self.src[w][n, k2] = self.src[w][n, k2] + self.via[w][n]
                self.copy(n, w, 2).start()

    def arrived(self, n):
        for w in range(2):
            self.copy(n, w, 1).wait_recv()
            self.copy(n, w, 2).wait_recv()

        @pl.when(self.mid)
        def _():
            for w in range(2):
                self.copy(n, w, 3).wait_recv()

    def sent(self, n):
        for w in range(2):
            self.copy(n, w, 1).wait_send()
            self.copy(n, w, 2).wait_send()

        @pl.when(self.mid)
        def _():
            for w in range(2):
                self.copy(n, w, 3).wait_send()

        @pl.when(jnp.logical_not(self.mid))
        def _():
            for w in range(2):
                self.copy(n, w, 4).wait_send()


class ZGather:
    def __init__(self, P_, mine, full, send, recv):
        self.P, self.mine, self.full, self.send, self.recv = P_, mine, full, send, recv
        self.mid = (P_.z == 1) | (P_.z == 2)
        self.all = range(len(mine))

    def copy(self, w, j):
        P_ = self.P
        zs = P_.zk[2] if j == 4 else P_.z
        block = self.full[w](zs) if j == 4 else self.mine[w]
        to = P_.dev(P_.own, P_.zk[1 if j == 4 else j])
        return rcopy(block, self.full[w](zs), self.send.at[w * 4 + j - 1], self.recv.at[w * 4 + zs], to)

    def landed(self, w, j):
        P_ = self.P
        zs = P_.zk[j]
        rcopy(
            self.mine[w], self.full[w](zs), self.send.at[0], self.recv.at[w * 4 + zs], P_.dev(P_.sib)
        ).wait_recv()

    def ship(self):
        for w in self.all:
            self.copy(w, 2).start()

        @pl.when(self.mid)
        def _():
            for w in self.all:
                self.copy(w, 3).start()

        for w in self.all:
            self.copy(w, 1).start()

    def relay(self):
        for w in self.all:
            self.landed(w, 2)

        @pl.when(self.mid)
        def _():
            for w in self.all:
                self.copy(w, 4).start()

    def finish(self):
        for w in self.all:
            self.landed(w, 1)
            self.landed(w, 3)
            self.copy(w, 1).wait_send()
            self.copy(w, 2).wait_send()

        @pl.when(self.mid)
        def _():
            for w in self.all:
                self.copy(w, 3).wait_send()
                self.copy(w, 4).wait_send()


PW = 4224
EX = 3072
WO = 3200


def enter_kernel(
    len_ref, tok, cot, tab, w_qkv, w_out, small, w_in, w_ein, w_down, w_eout,
    qkv_o, lse_o, att_o, s2_o, n1_o, wmix_o, pack_all, wi_all, wd_all, g_all, nt_all,
    pack_v, wia, gt, qkv, lse, att, s2, nt, n1,
    pz, ps, pr, asend, arecv, fsend, frecv, gs, gr, ts, tr, lsem, osem,
):
    P_ = Place()
    z, t, b = P_.z, P_.t, P_.b
    own, sib, d1, d2, dd = P_.own, P_.sib, P_.d1, P_.d2, P_.dd
    others = P_.plane_others()
    pack = pack_v.at[b]
    pack_v[b, :, 0:3072] = w_qkv[...]
    pack_v[b, :, EX : EX + 128] = small[...]
    pack_v[b, :, WO : WO + 1024] = w_out[...]
    meet([P_.dev(p) for p in others] + [P_.dev(own, zz) for zz in P_.zk[1:]])
    sends = []
    keeps = []

    def go(cp):
        cp.start()
        sends.append(cp)

    def store(src, dst):
        cp = pltpu.make_async_copy(src, dst, osem.at[len(keeps)])
        cp.start()
        keeps.append(cp)

    def gather(n, mine, full):
        return ZGather(P_, (mine,), (full,), fsend.at[n], frecv.at[n])

    out_a = gather(0, w_eout.at[0], lambda zs: wd_all.at[1, zs])
    out_b = gather(1, w_eout.at[1], lambda zs: wd_all.at[2, zs])
    in_a = gather(2, wi_all.at[1, z], lambda zs: wi_all.at[1, zs])
    in_b = gather(3, wi_all.at[2, z], lambda zs: wi_all.at[2, zs])
    out_d = gather(4, w_down, lambda zs: wd_all.at[0, zs])
    mid = in_a.mid

    def z_copy(k, s, to):
        return rcopy(pack_v.at[s], pack_v.at[s], pz.at[k - 1], pr.at[s], P_.dev(own, P_.zk[to]))

    z_copy(2, b, 2).start()

    @pl.when(mid)
    def _():
        z_copy(3, b, 3).start()

    z_copy(1, b, 1).start()
    go(rcopy(pack, pack, ps.at[3], pr.at[b], P_.dev(d1)))
    go(rcopy(pack, pack, ps.at[7], pr.at[b], P_.dev(d2)))
    go(rcopy(pack, pack, ps.at[15], pr.at[b], P_.dev(sib)))
    out_a.ship()
    for r in range(8):
        for zz in range(4):
            at = slice((zz * 8 + r) * 128, (zz * 8 + r + 1) * 128)
            to = slice(zz * 128, (zz + 1) * 128)
            wia[r, 0, :, to] = w_in[:, at]
            wia[r, 1:3, :, to] = w_ein[:, :, at]
    rows = pl.ds(pl.multiple_of(t * 32, 32), 32)
    lw = pltpu.make_async_copy(wia.at[t], wi_all.at[:, z, rows], lsem.at[1])
    lw.start()
    for i, p in enumerate(others):
        go(rcopy(wia.at[P_.rank(p)], wi_all.at[:, z, rows], asend.at[i], arecv.at[t], P_.dev(p)))
    store(w_down, wd_all.at[0, z])
    store(w_eout, wd_all.at[1:3, z])
    keep = lax.broadcasted_iota(jnp.int32, (384, 1), 0) < len_ref[0]
    gt[0:384] = jnp.where(keep, cot[...], jnp.zeros_like(cot[...]))
    gt[384:400] = jnp.zeros((16, 1024), BF)
    gt[384:385, 0:384] = tab[...].astype(BF)

    def landed(slot):
        rcopy(pack, pack_v.at[slot], ps.at[0], pr.at[slot], P_.dev(sib)).wait_recv()

    def fwd(slot, sem, p):
        go(rcopy(pack_v.at[slot], pack_v.at[slot], ps.at[sem], pr.at[slot], P_.dev(p)))

    def slot(k, p):
        return P_.zk[k] * 8 + P_.rank(p)

    for k in range(0, 6):
        if k == 2:
            out_b.ship()
        if 1 <= k <= 3:
            s = slot(k, own)
            landed(s)
            if k == 2:

                @pl.when(mid)
                def _():
                    z_copy(4, s, 1).start()

            fwd(s, 3 + k, d1)
            fwd(s, 7 + k, d2)
            fwd(s, 15 + k, sib)
        if k == 3:
            lw.wait()
            for p in others:
                rr = P_.rank(p)
                rq = pl.ds(pl.multiple_of(rr * 32, 32), 32)
                rcopy(
                    wia.at[0], wi_all.at[:, z, rq], asend.at[0], arecv.at[rr], P_.dev(sib)
                ).wait_recv()
            out_a.relay()
            in_a.ship()
        if k == 4:
            store(gt, g_all.at[t])
            for i, p in enumerate((d1, d2, sib)):
                go(rcopy(gt, g_all.at[t], gs.at[i], gr.at[t], P_.dev(p)))
        if 1 <= k <= 4:
            s = slot(k - 1, d1)
            landed(s)
            fwd(s, 11 + k - 1, d2)
            fwd(s, 19 + k - 1, sib)
            s = slot(k - 1, d2)
            landed(s)
            fwd(s, 23 + k - 1, sib)
        if k >= 2:
            s = slot(k - 2, dd)
            landed(s)
            fwd(s, 27 + k - 2, sib)
    out_b.relay()
    in_b.ship()
    stream = tok[...].astype(F32)
    for k in range(4):
        for p in (own, d1, d2, dd):
            landed(slot(k, P_.flip(p)))
    store(pack_v, pack_all)
    store(pack_v.at[:, :, EX : EX + 128], wmix_o)

    extra = pack_v[:, :, EX : EX + 128].reshape(1024, 128)
    n_one, _ = norm_parts(stream)
    n1[...] = (n_one * row_of(extra, 2)).astype(BF)
    store(n1, n1_o)

    def qkv_step(j, carry):
        cols = pl.ds(pl.multiple_of(j * 512, 512), 512)
        qkv[:, cols] = dot_nn(n1[...], pack_v[:, :, cols].reshape(1024, 512)).astype(BF)
        return carry

    lax.fori_loop(0, 6, qkv_step, 0)
    store(qkv, qkv_o)

    def plane(src_own, full, send, recv):
        def landed_at(p):
            r = P_.rank(p)
            rcopy(src_own, full.at[r], send.at[0], recv.at[r], P_.dev(sib)).wait_recv()
            return r

        def pass_on(p, *dests):
            r = landed_at(p)
            for i, q in dests:
                go(rcopy(full.at[r], full.at[r], send.at[i], recv.at[r], P_.dev(q)))

        return landed_at, pass_on

    g_landed, g_pass = plane(gt, g_all, gs, gr)
    n_landed, n_pass = plane(nt, nt_all, ts, tr)
    g_pass(d1, (3, d2), (4, sib))

    allowed = masks(len_ref[0])
    lane = lax.broadcasted_iota(jnp.int32, (384, 128), 1)
    lse[...] = jnp.zeros_like(lse)

    def pair_step(p, carry):
        q2 = qkv[:, pl.ds(pl.multiple_of(p * 128, 128), 128)]
        k2 = qkv[:, pl.ds(pl.multiple_of(1024 + p * 128, 128), 128)]
        v2 = qkv[:, pl.ds(pl.multiple_of(2048 + p * 128, 128), 128)]
        outs = []
        for hh in range(2):
            qm = jnp.where(lane // 64 == hh, q2, jnp.zeros_like(q2))
            sc = jnp.where(allowed, dot_nt(qm, k2) * 0.125, -1e30)
            top = jnp.max(sc, axis=-1, keepdims=True)
            ex = jnp.exp(sc - top)
            tot = jnp.sum(ex, axis=-1, keepdims=True)
            outs.append(dot_nn((ex * (1.0 / tot)).astype(BF), v2))
            lse[...] = jnp.where(lane == 2 * p + hh, top + jnp.log(tot), lse[...])
        att[:, pl.ds(pl.multiple_of(p * 128, 128), 128)] = jnp.where(
            lane < 64, outs[0], outs[1]
        ).astype(BF)

        @pl.when(p == 4)
        def _():
            in_a.relay()
            out_d.ship()

        return carry

    lax.fori_loop(0, 8, pair_step, 0)
    store(lse, lse_o)
    store(att, att_o)
    for j in range(2):
        w = pack_v[:, :, WO + j * 512 : WO + (j + 1) * 512].reshape(1024, 512)
        s2[:, j * 512 : (j + 1) * 512] = stream[:, j * 512 : (j + 1) * 512] + dot_nn(att[...], w)
    store(s2, s2_o)
    n_two, _ = norm_parts(s2[...])
    nt[...] = (n_two * row_of(extra, 3)).astype(BF)
    store(nt, nt_all.at[t])
    for i, p in enumerate((d1, d2, sib)):
        go(rcopy(nt, nt_all.at[t], ts.at[i], tr.at[t], P_.dev(p)))
    g_pass(d2, (5, sib))
    g_pass(dd, (6, sib))
    in_b.relay()
    n_pass(d1, (3, d2), (4, sib))
    n_pass(d2, (5, sib))
    out_d.relay()
    n_pass(dd, (6, sib))
    for p in (own, d1, d2, dd):
        g_landed(P_.flip(p))
    for p in (own, d2, d1, dd):
        n_landed(P_.flip(p))
    for part in (out_a, out_b, in_a, in_b, out_d):
        part.finish()
    z_copy(1, b, 1).wait_send()
    z_copy(2, b, 2).wait_send()

    @pl.when(mid)
    def _():
        z_copy(3, b, 3).wait_send()
        z_copy(4, b, 1).wait_send()

    for cp in keeps:
        cp.wait()
    for cp in sends:
        cp.wait_send()


def masks(seq_len):
    row = lax.broadcasted_iota(jnp.int32, (384, 384), 0)
    col = lax.broadcasted_iota(jnp.int32, (384, 384), 1)
    return (col <= row) & (col < seq_len)


def run_enter(*args):
    sd = jax.ShapeDtypeStruct
    dma = pltpu.SemaphoreType.DMA
    return pl.pallas_call(
        enter_kernel,
        out_shape=(
            sd((384, 3072), BF), sd((384, 128), F32), sd((384, 1024), BF), sd((384, 1024), F32),
            sd((384, 1024), BF), sd((32, 32, 128), BF),
            sd((32, 32, PW), BF), sd((3, 4, 256, 512), BF), sd((3, 4, 128, 1024), BF),
            sd((8, 400, 1024), BF), sd((8, 384, 1024), BF),
        ),
        in_specs=[SM] + [VM] * 10,
        out_specs=(ANY,) * 11,
        scratch_shapes=[
            pltpu.VMEM((32, 32, PW), BF), pltpu.VMEM((8, 3, 32, 512), BF), pltpu.VMEM((400, 1024), BF),
            pltpu.VMEM((384, 3072), BF), pltpu.VMEM((384, 128), F32), pltpu.VMEM((384, 1024), BF),
            pltpu.VMEM((384, 1024), F32), pltpu.VMEM((384, 1024), BF), pltpu.VMEM((384, 1024), BF),
            dma((4,)), dma((31,)), dma((32,)), dma((7,)), dma((8,)), dma((5, 4)), dma((5, 4)),
            dma((7,)), dma((8,)), dma((7,)), dma((8,)), dma((4,)), dma((12,)),
        ],
        compiler_params=pltpu.CompilerParams(
            collective_id=0, has_side_effects=True, vmem_limit_bytes=63 * MIB
        ),
    )(*args)


def mix_of(delta):
    return 1.0 / (1.0 + jnp.exp(-delta)), 1.0 / (1.0 + jnp.exp(delta))


def gelu_both(u):
    a, bb = 0.7978845608028654, 0.044715
    u2 = u * u
    th = jnp.tanh(a * u * (1.0 + bb * u2))
    half = 0.5 * (1.0 + th)
    return u * half, half + 0.5 * u * (1.0 - th * th) * a * (1.0 + 3.0 * bb * u2)


def ff_kernel(
    len_ref, nt_hbm, wmix, s2, g_all, wi_all, wd_all,
    block, gsum, gl_out, gde, xe, dgi, dgd, r1, r2, rin, rdn, dwi,
    nt_all, gbuf, br, gn, xb, yb, wi, wd, ai, ad, gin, gdn, tri, trd, tmp, gc, gcr, dots, gaps,
    tr, gsem, wsem, dsem, zas, zar, zss, zsr, s1s, s1r, s2s, s2r, cs, cr, lsem, tsem,
):
    P_ = Place()
    z, t = P_.z, P_.t
    own, sib, d1, d2, dd = P_.own, P_.sib, P_.d1, P_.d2, P_.dd
    others = P_.plane_others()
    meet([P_.dev(p) for p in others] + [P_.dev(own, zz) for zz in P_.zk[1:]])
    sends = []

    def go(cp):
        cp.start()
        sends.append(cp)

    dense = ZGather(
        P_, (wi_all.at[0, z],), (lambda zs: dwi.at[zs],), zas, zar
    )
    dense.ship()
    s2_in = pltpu.make_async_copy(s2, gsum, lsem.at[3])
    s2_in.start()

    expert_load = (
        pltpu.make_async_copy(wi_all.at[1], wi.at[0], wsem.at[0, 0]),
        pltpu.make_async_copy(wd_all.at[1], wd.at[0], wsem.at[0, 1]),
        pltpu.make_async_copy(wi_all.at[2], wi.at[1], wsem.at[1, 0]),
        pltpu.make_async_copy(wd_all.at[2], wd.at[1], wsem.at[1, 1]),
    )
    for cp in expert_load:
        cp.start()

    def dense_load():
        copies = [pltpu.make_async_copy(wd_all.at[0], wd.at[0], dsem.at[4])]
        for k in range(4):
            zz = P_.zk[k]
            src = wi_all.at[0, z] if k == 0 else dwi.at[zz]
            copies.append(pltpu.make_async_copy(src, wi.at[0, zz], dsem.at[k]))
        return copies

    zsum = ZSum(P_, (gin, gdn), (rin, rdn), (tri, trd), zss, zsr)

    order = (own, sib, d1, P_.flip(d2), d2, P_.flip(d1), dd, P_.flip(dd))
    ranks = [P_.rank(p) for p in order]

    def seq_at(i):
        s = ranks[0]
        for k in range(1, 8):
            s = jnp.where(i == k, ranks[k], s)
        return s

    def g_copy(i):
        return pltpu.make_async_copy(g_all.at[seq_at(i)], gbuf.at[i % 2], gsem.at[i % 2])

    def ff(xv, gv, k):
        wiv = wi[k].reshape(1024, 512)
        wdv = wd[k].reshape(512, 1024)
        act, dact = gelu_both(dot_nn(xv, wiv))
        act = act.astype(BF)
        gup = (dact * dot_nt(gv, wdv)).astype(BF)
        ad[k] += dot_tn(act, gv)
        ai[k] += dot_tn(xv, gup)
        return dot_nn(act, wdv), dot_nt(gup, wiv)

    lane = lax.broadcasted_iota(jnp.int32, (448, 128), 1)

    def shares(tab):
        slot = lax.broadcasted_iota(jnp.int32, (224, 384), 0)
        return (tab == slot.astype(F32)).astype(BF)

    def n_copy(s):
        return pltpu.make_async_copy(nt_hbm.at[s], nt_all.at[s], tr.at[s])

    for s in ranks:
        n_copy(s).start()
    g_copy(0).start()
    ai[...] = jnp.zeros_like(ai)
    ad[...] = jnp.zeros_like(ad)
    for cp in expert_load:
        cp.wait()

    def arrive(i, carry):
        s = seq_at(i)

        @pl.when(i + 1 < 8)
        def _():
            g_copy(i + 1).start()

        n_copy(s).wait()
        g_copy(i).wait()
        xv = nt_all[s]
        gv = gbuf[i % 2, :384]
        tab = gbuf[i % 2, 384:400][0:1, :384].astype(F32)
        lg = dot_nn(xv, wmix[...])
        gap = lg[:, 0:1] - lg[:, 1:2]
        gaps[i] = jnp.transpose(jnp.broadcast_to(gap, (384, 128)))[0:8]
        _, m1 = mix_of(gap)
        ge = (m1 * gv.astype(F32)).astype(BF)
        sh = shares(tab)
        xb[i] = dot_nn(sh, xv).astype(BF).reshape(2, 112, 1024)
        yb[i] = dot_nn(sh, ge).astype(BF).reshape(2, 112, 1024)
        return carry

    def expert(b, e):
        four = pl.ds(b * 4, 4)
        gq = yb[four, e].reshape(448, 1024)
        yv, gb = ff(xb[four, e].reshape(448, 1024), gq, e)
        rs = jnp.sum(gq.astype(F32) * yv, axis=-1, keepdims=True)
        high = rs.astype(BF).astype(F32)
        dots[four, e] = (
            jnp.where(lane == 0, high, jnp.where(lane == 1, rs - high, 0.0))
            .astype(BF)
            .reshape(4, 112, 128)
        )
        xb[four, e] = yv.astype(BF).reshape(4, 112, 1024)
        yb[four, e] = gb.astype(BF).reshape(4, 112, 1024)

    def stage(e):
        gin[e] = ai[e].astype(BF).reshape(4, 256, 512)
        gdn[e] = ad[e].astype(BF).reshape(4, 128, 1024)
        zsum.ship(e)

    def half(b, carry):
        lax.fori_loop(b * 4, b * 4 + 4, arrive, 0)
        expert(b, 0)
        return carry

    def half_two(b, carry):
        expert(b, 1)
        return carry

    lax.fori_loop(0, 2, half, 0)
    stage(0)
    dense.relay()
    lax.fori_loop(0, 2, half_two, 0)
    stage(1)
    g_copy(7).start()
    dense.finish()
    for cp in dense_load():
        cp.start()
    ai[0] = jnp.zeros_like(ai[0])
    ad[0] = jnp.zeros_like(ad[0])
    for cp in dense_load():
        cp.wait()

    chips = (dd, d1, d2, own)
    both = (gn, br)

    def give1(q, w):
        r = P_.rank(P_.flip(chips[q]))
        k = (0, 2, 1, 3)[q]
        return rcopy(both[w].at[r], r1.at[w, k], s1s.at[w, k], s1r.at[w, k], P_.dev(sib))

    def load1(q, w, start):
        cp = pltpu.make_async_copy(r1.at[w, q], tmp.at[w], tsem.at[w])
        if start:
            rcopy(tmp.at[0], r1.at[w, q], s1s.at[0, 0], s1r.at[w, q], P_.dev(sib)).wait_recv()
            cp.start()
        else:
            cp.wait()
            add_tmp(w, P_.rank(chips[q]))

    def load2(k, p, w, start):
        cp = pltpu.make_async_copy(r2.at[w, k], tmp.at[w], tsem.at[w])
        if start:
            rcopy(tmp.at[0], r2.at[w, k], s2s.at[0, 0], s2r.at[w, k], P_.dev(sib)).wait_recv()
            cp.start()
        else:
            cp.wait()
            add_tmp(w, P_.rank(p))

    def add_tmp(w, r):
        both[w][r] = both[w][r] + tmp[w]

    def give2(q, k, p, w):
        src = both[w].at[P_.rank(chips[q])]
        return rcopy(src, r2.at[w, k], s2s.at[w, k], s2r.at[w, k], P_.dev(p))

    def at_step(step, k, fn):
        @pl.when(step == k)
        def _():
            for w in range(2):
                fn(w)

    def dense_step(k, carry):
        i = 7 - k
        s = seq_at(i)

        @pl.when(i > 0)
        def _():
            g_copy(i - 1).start()

        g_copy(i).wait()
        xv = nt_all[s]
        gf = gbuf[i % 2, :384].astype(F32)
        tab = gbuf[i % 2, 384:400][0:1, :384].astype(F32)
        gap = jnp.transpose(jnp.broadcast_to(gaps[i][0:1], (128, 384)))[:, 0:1]
        m0, m1 = mix_of(gap)
        out, gxv = ff(xv, (m0 * gf).astype(BF), 0)
        at_step(k, 1, lambda w: load1(0, w, True))
        at_step(k, 3, lambda w: load1(2, w, True))
        at_step(k, 5, lambda w: load1(1, w, True))
        at_step(k, 7, lambda w: load1(3, w, True))
        col = jnp.broadcast_to(jnp.sum(gf * out, axis=-1, keepdims=True), (384, 128))
        gc[s, 0:8] = jnp.transpose(col)[0:8]
        sh = shares(tab)
        q1 = dot_tn(sh, dots[i].reshape(224, 128))
        gc[s, 8:16] = jnp.transpose(jnp.broadcast_to(q1[:, 0:1] + q1[:, 1:2], (384, 128)))[0:8]
        gn[s] = (gxv + dot_tn(sh, yb[i].reshape(224, 1024))).astype(BF)
        br[s] = (m0 * out + m1 * dot_tn(sh, xb[i].reshape(224, 1024))).astype(BF)

        for q in range(4):
            at_step(k, 2 * q, lambda w, q=q: give1(q, w).start())

        def pass_on(q, n, p):
            def fn(w):
                load1(q, w, False)
                give2(q, n, p, w).start()

            return fn

        at_step(k, 1, pass_on(0, 0, d2))
        at_step(k, 3, pass_on(2, 2, d2))
        at_step(k, 5, lambda w: load1(1, w, False))
        at_step(k, 5, lambda w: load2(0, d1, w, True))

        def turn(w):
            load2(0, d1, w, False)
            give2(1, 1, d1, w).start()

        at_step(k, 5, turn)
        at_step(k, 7, lambda w: load1(3, w, False))

        @pl.when(k == 2)
        def _():
            zsum.transit(0)

        @pl.when(k == 5)
        def _():
            zsum.transit(1)

        return carry

    lax.fori_loop(0, 8, dense_step, 0)
    for i, p in enumerate(others):
        go(rcopy(gc.at[P_.rank(p)], gcr.at[t], cs.at[i], cr.at[t], P_.dev(p)))
    o0 = pltpu.make_async_copy(ai.at[0], dgi, lsem.at[0])
    o1 = pltpu.make_async_copy(ad.at[0], dgd, lsem.at[1])
    o0.start()
    o1.start()
    for w in range(2):
        load2(2, own, w, True)
    for w in range(2):
        load2(2, own, w, False)
    for w in range(2):
        load2(1, own, w, True)
        load2(1, own, w, False)
    s2_in.wait()
    branch = br[t].astype(F32)
    keep = (lax.broadcasted_iota(jnp.int32, (384, 1), 0) < len_ref[0]).astype(F32)
    block[...] = ((gsum[...] + branch) * keep).astype(BF)
    gsum[...] = gn[t].astype(F32)
    for p in others:
        r = P_.rank(p)
        rcopy(gc.at[0], gcr.at[r], cs.at[0], cr.at[r], P_.dev(sib)).wait_recv()
    gcr[t] = gc[t]
    tot = jnp.sum(gcr[...], axis=0)
    gc0 = jnp.transpose(jnp.broadcast_to(tot[0:1], (128, 384)))
    q1 = jnp.transpose(jnp.broadcast_to(tot[8:9], (128, 384)))
    m0, m1 = mix_of(jnp.transpose(jnp.broadcast_to(gaps[0][0:1], (128, 384))))
    gl_out[...] = m0 * (m1 * gc0 - q1)

    mids = zsum.mid

    def third(e):
        return (
            pltpu.make_async_copy(rin.at[e, 2], nt_all.at[2, 0:256, 0:512], lsem.at[4]),
            pltpu.make_async_copy(rdn.at[e, 2], nt_all.at[3, 0:128], lsem.at[5]),
        )

    for e in range(2):
        zsum.arrived(e)
        loads = (
            (rin.at[e, 0], nt_all.at[0, 0:256, 0:512]), (rin.at[e, 1], nt_all.at[0, 0:256, 512:1024]),
            (rdn.at[e, 0], nt_all.at[1, 0:128]), (rdn.at[e, 1], nt_all.at[1, 128:256]),
        )
        loads = [pltpu.make_async_copy(u, v, lsem.at[6 + n]) for n, (u, v) in enumerate(loads)]

        @pl.when(mids)
        def _():
            for cp in third(e):
                cp.start()

        for cp in loads:
            cp.start()
        for cp in loads:
            cp.wait()
        two = nt_all[0, 0:256]
        ai[1, 0:256] = gin[e, z].astype(F32) + two[:, 0:512].astype(F32) + two[:, 512:1024].astype(F32)
        at = slice(e * 128, (e + 1) * 128)
        ad[1, at] = gdn[e, z].astype(F32) + nt_all[1, 0:128].astype(F32) + nt_all[1, 128:256].astype(F32)

        @pl.when(mids)
        def _():
            for cp in third(e):
                cp.wait()
            ai[1, 0:256] += nt_all[2, 0:256, 0:512].astype(F32)
            ad[1, at] += nt_all[3, 0:128].astype(F32)

        gin[e, z] = ai[1, 0:256].astype(BF)
    o2 = pltpu.make_async_copy(gin.at[:, z], xe, lsem.at[2])
    o3 = pltpu.make_async_copy(ad.at[1, 0:256], gde, lsem.at[3])
    o2.start()
    o3.start()
    for w in range(2):
        for q in range(4):
            give1(q, w).wait_send()
        give2(0, 0, d2, w).wait_send()
        give2(1, 1, d1, w).wait_send()
        give2(2, 2, d2, w).wait_send()
    for e in range(2):
        zsum.sent(e)
    for cp in (o0, o1, o2, o3):
        cp.wait()
    for cp in sends:
        cp.wait_send()


def run_ff(lengths, nt, wmix, s2, g_all, wi_all, wd_all):
    sd = jax.ShapeDtypeStruct
    dma = pltpu.SemaphoreType.DMA
    out = pl.pallas_call(
        ff_kernel,
        out_shape=(
            sd((384, 1024), BF), sd((384, 1024), F32), sd((384, 128), F32),
            sd((256, 1024), F32), sd((2, 256, 512), BF), sd((1024, 512), F32), sd((512, 1024), F32),
            sd((2, 4, 384, 1024), BF), sd((2, 3, 384, 1024), BF),
            sd((2, 3, 256, 512), BF), sd((2, 3, 128, 1024), BF),
            sd((4, 256, 512), BF),
        ),
        in_specs=[SM, ANY, VM, ANY, ANY, ANY, ANY],
        out_specs=(VM,) * 3 + (ANY,) * 9,
        scratch_shapes=[
            pltpu.VMEM((8, 384, 1024), BF), pltpu.VMEM((2, 400, 1024), BF),
            pltpu.VMEM((8, 384, 1024), BF), pltpu.VMEM((8, 384, 1024), BF),
            pltpu.VMEM((8, 2, 112, 1024), BF), pltpu.VMEM((8, 2, 112, 1024), BF),
            pltpu.VMEM((2, 4, 256, 512), BF), pltpu.VMEM((2, 4, 128, 1024), BF),
            pltpu.VMEM((2, 1024, 512), F32), pltpu.VMEM((2, 512, 1024), F32),
            pltpu.VMEM((2, 4, 256, 512), BF), pltpu.VMEM((2, 4, 128, 1024), BF),
            pltpu.VMEM((2, 256, 512), BF), pltpu.VMEM((2, 128, 1024), BF),
            pltpu.VMEM((2, 384, 1024), BF),
            pltpu.VMEM((8, 16, 384), F32), pltpu.VMEM((8, 16, 384), F32), pltpu.VMEM((8, 2, 112, 128), BF),
            pltpu.VMEM((8, 8, 384), F32),
            dma((8,)), dma((2,)), dma((2, 2)), dma((5,)), dma((4,)), dma((4,)), dma((2, 8)), dma((2, 8)),
            dma((2, 4)), dma((2, 4)), dma((2, 3)), dma((2, 3)), dma((7,)), dma((8,)), dma((10,)), dma((2,)),
        ],
        compiler_params=pltpu.CompilerParams(
            collective_id=1, has_side_effects=True, vmem_limit_bytes=63 * MIB
        ),
    )(lengths, nt, wmix, s2, g_all, wi_all, wd_all)
    return out[:7]


class RowSum:
    swap = (0, 2, 1, 3)

    def __init__(self, P_, g, r1, r2, r3, sems):
        self.P, self.g, self.r1, self.r2, self.r3 = P_, g, r1, r2, r3
        self.s1s, self.s1r, self.s2s, self.s2r, self.s3s, self.s3r = sems
        self.chips = (P_.dd, P_.d1, P_.d2, P_.own)

    def rank(self, q):
        return self.P.rank(self.chips[q])

    def copy1(self, n, q):
        k = self.swap[q]
        src = self.g.at[n, self.P.rank(self.P.flip(self.chips[q]))]
        return rcopy(src, self.r1.at[n, k], self.s1s.at[n, k], self.s1r.at[n, k], self.P.dev(self.P.sib))

    def copy2(self, n, q, k, p):
        src = self.g.at[n, self.rank(q)]
        return rcopy(src, self.r2.at[n, k], self.s2s.at[n, k], self.s2r.at[n, k], self.P.dev(p))

    def copy3(self, n, k):
        P_ = self.P
        return rcopy(
            self.g.at[n, P_.t, P_.zk[k]], self.r3.at[n, k - 1], self.s3s.at[n, k - 1],
            self.s3r.at[n, k - 1], P_.dev(P_.own, P_.zk[k]),
        )

    def in1(self, n, q):
        rcopy(
            self.g.at[n, 0], self.r1.at[n, q], self.s1s.at[n, 0], self.s1r.at[n, q], self.P.dev(self.P.sib)
        ).wait_recv()
        r = self.rank(q)
        self.g[n, r] = self.g[n, r] + self.r1[n, q]

    def in2(self, n, k, q):
        rcopy(
            self.g.at[n, 0], self.r2.at[n, k], self.s2s.at[n, 0], self.s2r.at[n, k], self.P.dev(self.P.sib)
        ).wait_recv()
        r = self.rank(q)
        self.g[n, r] = self.g[n, r] + self.r2[n, k]

    def step1(self, n):
        for q in (0, 1, 2, 3):
            self.copy1(n, q).start()

    def step2(self, n):
        P_ = self.P
        self.in1(n, 0)
        self.copy2(n, 0, 0, P_.d2).start()
        self.in1(n, 2)
        self.copy2(n, 2, 2, P_.d2).start()
        self.in1(n, 1)

    def step3(self, n):
        self.in2(n, 0, 1)
        self.copy2(n, 1, 1, self.P.d1).start()
        self.in1(n, 3)

    def step4(self, n):
        self.in2(n, 2, 3)
        self.in2(n, 1, 3)
        for k in (3, 2, 1):
            self.copy3(n, k).start()

    def step5(self, n):
        P_ = self.P
        for k in (1, 2, 3):
            rcopy(
                self.g.at[n, 0, 0], self.r3.at[n, k - 1], self.s3s.at[n, 0], self.s3r.at[n, k - 1],
                P_.dev(P_.sib),
            ).wait_recv()
        total = self.g[n, P_.t, P_.z].astype(F32)
        for k in range(3):
            total += self.r3[n, k].astype(F32)
        return total

    def sent(self, n):
        P_ = self.P
        for q in range(4):
            self.copy1(n, q).wait_send()
        self.copy2(n, 0, 0, P_.d2).wait_send()
        self.copy2(n, 2, 2, P_.d2).wait_send()
        self.copy2(n, 1, 1, P_.d1).wait_send()
        for k in (1, 2, 3):
            self.copy3(n, k).wait_send()


def back_kernel(
    len_ref, tok, s2, n1, qkv, lse, att, gsum, gl, g_all, nt_all, pack_all, dgi, dgd, xe,
    gtok, gqkv, gwo, gex, gdd, gwi, gwe,
    gx, gt, nt,
    pack_v, gq, gacc, n1t, ga_, gb_, gc_, ra1, ra2, ra3, rb1, rb2, rb3, rc1, rc2, rc3,
    di, dj, gin, gdn, rin, rdn, tri, trd, *sems,
):
    P_ = Place()
    z, t = P_.z, P_.t
    own, sib, d1, d2, dd = P_.own, P_.sib, P_.d1, P_.d2, P_.dd
    others = P_.plane_others()
    zss, zsr, xs, xr, lsem = sems[18:]
    sum_a = RowSum(P_, ga_, ra1, ra2, ra3, sems[0:6])
    sum_b = RowSum(P_, gb_, rb1, rb2, rb3, sems[6:12])
    sum_c = RowSum(P_, gc_, rc1, rc2, rc3, sems[12:18])
    lw = pltpu.make_async_copy(pack_all, pack_v, lsem.at[0])
    li = pltpu.make_async_copy(dgi, di, lsem.at[1])
    lj = pltpu.make_async_copy(dgd, dj, lsem.at[2])
    li.start()
    lj.start()
    lw.start()
    own_in = (
        pltpu.make_async_copy(g_all.at[t], gt, lsem.at[5]),
        pltpu.make_async_copy(nt_all.at[t], nt, lsem.at[6]),
    )
    for cp in own_in:
        cp.start()
    meet([P_.dev(p) for p in others] + [P_.dev(own, zz) for zz in P_.zk[1:]])
    sends = []

    def go(cp):
        cp.start()
        sends.append(cp)

    def rows(p):
        return pl.ds(pl.multiple_of(P_.rank(p) * 32, 32), 32)

    zsum = ZSum(P_, (gin, gdn), (rin, rdn), (tri, trd), zss, zsr)
    li.wait()
    lj.wait()
    gin[0] = di[...].astype(BF).reshape(4, 256, 512)
    gdn[0] = dj[...].astype(BF).reshape(4, 128, 1024)
    zsum.ship(0)
    le = pltpu.make_async_copy(xe.at[:, rows(own)], gx.at[t, 1:3], lsem.at[3])
    le.start()
    for i, p in enumerate(others):
        go(rcopy(xe.at[:, rows(p)], gx.at[t, 1:3], xs.at[i], xr.at[t, 0], P_.dev(p)))

    lw.wait()
    for cp in own_in:
        cp.wait()
    extra = pack_v[:, :, EX : EX + 128].reshape(1024, 128)
    lane = lax.broadcasted_iota(jnp.int32, (384, 128), 1)
    glv = gl[...]
    gnt = gsum[...] + glv[:, 0:1] * (row_of(extra, 0) - row_of(extra, 1))
    two = jnp.where(lane == 0, glv, jnp.where(lane == 1, -glv, 0.0)).astype(BF)
    n_two, r_two = norm_parts(s2[...])
    gain_two_row = jnp.sum(gnt * n_two, axis=0, keepdims=True)

    def norm_back(gv, gain, n, r):
        tt = gv * gain
        return r * (tt - jnp.mean(tt, -1, keepdims=True) - n * jnp.mean(tt * n, -1, keepdims=True))

    gs2 = gt[0:384].astype(F32) + norm_back(gnt, row_of(extra, 3), n_two, r_two)
    gtok[...] = gs2
    ga = gs2.astype(BF)

    def put(ref, n, cols, val):
        low = val.astype(BF)
        for zz in range(4):
            ref[n, :, zz, :, cols] = low[zz * 256 : (zz + 1) * 256].reshape(8, 32, low.shape[1])

    for j in range(2):
        cols = slice(j * 512, (j + 1) * 512)
        put(ga_, 0, cols, dot_tn(att[...], ga[:, cols]))
    sum_a.step1(0)
    gatt = dot_nt(ga[:, 0:512], pack_v[:, :, WO : WO + 512].reshape(1024, 512))
    gatt += dot_nt(ga[:, 512:1024], pack_v[:, :, WO + 512 : WO + 1024].reshape(1024, 512))
    gq[:, 0:1024] = gatt.astype(BF)
    n1t[...] = jnp.transpose(n1[...])
    gacc[...] = jnp.zeros_like(gacc)
    allowed = masks(len_ref[0])
    sum_a.step2(0)

    def pair_step(p, carry):
        lo = pl.ds(pl.multiple_of(p * 128, 128), 128)
        mid = pl.ds(pl.multiple_of(1024 + p * 128, 128), 128)
        hi = pl.ds(pl.multiple_of(2048 + p * 128, 128), 128)
        q2, k2, v2, do = qkv[:, lo], qkv[:, mid], qkv[:, hi], gq[:, lo]
        dq = dk = dv = None
        for hh in range(2):
            mine = lane // 64 == hh
            zero = jnp.zeros_like(q2)
            qm, km, dm = (jnp.where(mine, v, zero) for v in (q2, k2, do))
            total = jnp.sum(jnp.where(lane == 2 * p + hh, lse[...], 0.0), axis=-1, keepdims=True)
            sc = dot_nt(qm, k2) * 0.125
            pf = jnp.where(allowed, jnp.exp(sc - total), 0.0)
            gp = dot_nt(dm, v2)
            ds = (pf * (gp - jnp.sum(pf * gp, axis=-1, keepdims=True))).astype(BF)
            terms = (dot_nn(ds, km), dot_tn(ds, qm), dot_tn(pf.astype(BF), dm))
            dq, dk, dv = terms if hh == 0 else (dq + terms[0], dk + terms[1], dv + terms[2])
        gq[:, lo] = (dq * 0.125).astype(BF)
        gq[:, mid] = (dk * 0.125).astype(BF)
        gq[:, hi] = dv.astype(BF)
        return carry

    def chunk_step(j, carry):
        lax.fori_loop(2 * j, 2 * j + 2, pair_step, 0)
        for seg in range(3):
            cols = pl.ds(pl.multiple_of(seg * 1024 + j * 256, 256), 256)
            gcols = gq[:, cols]
            put(gb_, j, slice(seg * 256, (seg + 1) * 256), dot_nn(n1t[...], gcols))
            gacc[...] += dot_nt(gcols, pack_v[:, :, cols].reshape(1024, 256))
        sum_b.step1(j)

        @pl.when(j == 0)
        def _():
            zsum.transit(0)
            sum_a.step3(0)

        @pl.when(j == 1)
        def _():
            sum_a.step4(0)

        @pl.when(j >= 1)
        def _():
            sum_b.step2(j - 1)

        @pl.when(j >= 2)
        def _():
            sum_b.step3(j - 2)

        @pl.when(j >= 3)
        def _():
            sum_b.step4(j - 3)

        return carry

    lax.fori_loop(0, 4, chunk_step, 0)
    gn1 = gacc[...]
    n_one, r_one = norm_parts(tok[...].astype(F32))
    gain_one_row = jnp.sum(gn1 * n_one, axis=0, keepdims=True)
    rowi = lax.broadcasted_iota(jnp.int32, (8, 1024), 0)
    rws = jnp.where(rowi == 0, gain_one_row, jnp.where(rowi == 1, gain_two_row, 0.0)).astype(BF)
    sel = (
        lax.broadcasted_iota(jnp.int32, (8, 128), 1) == lax.broadcasted_iota(jnp.int32, (8, 128), 0) + 2
    ).astype(BF)
    put(gc_, 0, slice(0, 128), dot_tn(nt[...], two) + dot_tn(rws, sel))
    sum_c.step1(0)
    sum_b.step2(3)
    sum_b.step3(2)
    sum_c.step2(0)
    gtok[...] += norm_back(gn1, row_of(extra, 2), n_one, r_one)
    sum_b.step3(3)
    sum_b.step4(1)
    sum_c.step3(0)

    zsum.arrived(0)
    di[0:256] = gin[0, z].astype(F32) + rin[0, 0].astype(F32) + rin[0, 1].astype(F32)
    gdd[...] = gdn[0, z].astype(F32) + rdn[0, 0].astype(F32) + rdn[0, 1].astype(F32)

    @pl.when(zsum.mid)
    def _():
        di[0:256] += rin[0, 2].astype(F32)
        gdd[...] += rdn[0, 2].astype(F32)

    gin[0, z] = di[0:256].astype(BF)
    lx = pltpu.make_async_copy(gin.at[:, z, rows(own)], gx.at[t, 0:1], lsem.at[4])
    lx.start()
    for i, p in enumerate(others):
        go(rcopy(gin.at[:, z, rows(p)], gx.at[t, 0:1], xs.at[7 + i], xr.at[t, 1], P_.dev(p)))

    sum_b.step4(2)
    sum_b.step4(3)
    sum_c.step4(0)
    gwo[...] = sum_a.step5(0)
    for j in range(4):
        total = sum_b.step5(j)
        for seg in range(3):
            at = seg * 1024 + j * 256
            gqkv[:, at : at + 256] = total[:, seg * 256 : (seg + 1) * 256]
    gex[...] = sum_c.step5(0)
    for p in others:
        r = P_.rank(p)
        rcopy(xe.at[:, rows(own)], gx.at[r, 1:3], xs.at[0], xr.at[r, 0], P_.dev(sib)).wait_recv()
        rcopy(gin.at[:, 0, rows(own)], gx.at[r, 0:1], xs.at[0], xr.at[r, 1], P_.dev(sib)).wait_recv()
    le.wait()
    lx.wait()
    for r in range(8):
        for zz in range(4):
            to = slice((zz * 8 + r) * 128, (zz * 8 + r + 1) * 128)
            at = slice(zz * 128, (zz + 1) * 128)
            gwi[:, to] = gx[r, 0, :, at].astype(F32)
            gwe[:, :, to] = gx[r, 1:3, :, at].astype(F32)
    zsum.sent(0)
    sum_a.sent(0)
    for j in range(4):
        sum_b.sent(j)
    sum_c.sent(0)
    for cp in sends:
        cp.wait_send()


def run_back(*args):
    sd = jax.ShapeDtypeStruct
    dma = pltpu.SemaphoreType.DMA
    sizes = ((1, 1024), (4, 768), (1, 128))
    blocks = [pltpu.VMEM((n, 8, 4, 32, w), BF) for n, w in sizes]
    for n, w in sizes:
        blocks += [
            pltpu.VMEM((n, 4, 4, 32, w), BF), pltpu.VMEM((n, 3, 4, 32, w), BF), pltpu.VMEM((n, 3, 32, w), BF),
        ]
    sems = []
    for n, _ in sizes:
        sems += [dma((n, 4)), dma((n, 4)), dma((n, 3)), dma((n, 3)), dma((n, 3)), dma((n, 3))]
    return pl.pallas_call(
        back_kernel,
        out_shape=(
            sd((384, 1024), F32), sd((32, 3072), F32), sd((32, 1024), F32), sd((32, 128), F32),
            sd((128, 1024), F32), sd((32, 4096), F32), sd((2, 32, 4096), F32),
        ),
        in_specs=[SM] + [VM] * 8 + [ANY] * 6,
        out_specs=(VM,) * 7,
        scratch_shapes=[
            pltpu.VMEM((8, 3, 32, 512), BF), pltpu.VMEM((400, 1024), BF), pltpu.VMEM((384, 1024), BF),
            pltpu.VMEM((32, 32, PW), BF), pltpu.VMEM((384, 3072), BF), pltpu.VMEM((384, 1024), F32),
            pltpu.VMEM((1024, 384), BF), *blocks,
            pltpu.VMEM((1024, 512), F32), pltpu.VMEM((512, 1024), F32),
            pltpu.VMEM((1, 4, 256, 512), BF), pltpu.VMEM((1, 4, 128, 1024), BF),
            pltpu.VMEM((1, 3, 256, 512), BF), pltpu.VMEM((1, 3, 128, 1024), BF),
            pltpu.VMEM((1, 256, 512), BF), pltpu.VMEM((1, 128, 1024), BF),
            *sems, dma((1, 8)), dma((1, 8)), dma((14,)), dma((8, 2)), dma((7,)),
        ],
        compiler_params=pltpu.CompilerParams(
            collective_id=2, has_side_effects=True, vmem_limit_bytes=63 * MIB
        ),
    )(*args)


def fused_device(
    tokens, cotangent, lengths, expert_ids, slot_ids, w_qkv, w_out, gain_one, w_in, w_down,
    w_expert_in, w_expert_out, w_mix, gain_two,
):
    table = jnp.where(slot_ids >= 0, expert_ids * CAP + slot_ids, -1).astype(F32)
    lane = jnp.arange(128, dtype=jnp.int32)[None, :]
    small = jnp.zeros((32, 128), BF)
    for k, col in enumerate((w_mix[:, 0], w_mix[:, 1], gain_one, gain_two)):
        small = jnp.where(lane == k, col[:, None], small)
    qkv, lse, att, s2, n1, wmix, pack_all, wi_all, wd_all, g_all, nt_all = run_enter(
        lengths, tokens, cotangent, table.reshape(1, 384),
        w_qkv, w_out, small, w_in, w_expert_in, w_down, w_expert_out,
    )
    block, gsum, gl, gde, xe, dgi, dgd = run_ff(
        lengths, nt_all, wmix.reshape(1024, 128), s2, g_all, wi_all, wd_all
    )
    gtok, gqkv, gwo, gex, gdd, gwi, gwe = run_back(
        lengths, tokens, s2, n1, qkv, lse, att, gsum, gl, g_all, nt_all, pack_all, dgi, dgd, xe
    )
    return (
        block, gtok, gqkv, gwo, gex[:, 2], gwi, gdd, gwe, gde.reshape(2, 128, 1024), gex[:, 0:2], gex[:, 3],
    )


def solution(mesh):
    placed = (
        P(("dp", "fsdp"), None),
        P(("dp", "fsdp"), None),
        P(("dp", "fsdp")),
        P(("dp", "fsdp")),
        P(("dp", "fsdp")),
        P(("dp", "fsdp"), None),
        P(("dp", "fsdp"), None),
        P(("dp", "fsdp")),
        P(("dp", "fsdp"), None),
        P(("dp", "fsdp"), None),
        P(None, ("dp", "fsdp"), None),
        P(None, ("dp", "fsdp"), None),
        P(("dp", "fsdp"), None),
        P(("dp", "fsdp")),
    )
    fused = (mesh.shape["dp"], mesh.shape["fsdp"]) == (8, 4)
    return jax.shard_map(
        fused_device if fused else per_device,
        mesh=mesh,
        in_specs=placed,
        out_specs=(
            P(("dp", "fsdp"), None),
            P(("dp", "fsdp"), None),
            P(("dp", "fsdp"), None),
            P(("dp", "fsdp"), None),
            P(("dp", "fsdp")),
            P(("dp", "fsdp"), None),
            P(("dp", "fsdp"), None),
            P(None, ("dp", "fsdp"), None),
            P(None, ("dp", "fsdp"), None),
            P(("dp", "fsdp"), None),
            P(("dp", "fsdp")),
        ),
        check_vma=False,
    )
```

```python
import jax
import jax.numpy as jnp
from jax import lax
from jax.experimental import pallas as pl
from jax.experimental.pallas import tpu as pltpu
from jax.sharding import PartitionSpec as P

HEAD_DIM = 64
EXPERTS = 2
CAP = 112


def layer_norm(values_in, gain_vec):
    average = jnp.mean(values_in, axis=-1, keepdims=True)
    centred = values_in - average
    variance = jnp.mean(centred * centred, axis=-1, keepdims=True)
    return centred * lax.rsqrt(variance + 1e-05) * gain_vec


def gelu_tanh(values_in):
    return jax.nn.gelu(values_in, approximate=True)


def gelu_back(values_in, grad_in):
    return jax.vjp(gelu_tanh, values_in)[1](grad_in)[0]


def head_scores(query_h, key_h, allowed, score_scale):
    scores = (
        jnp.einsum("qd,kd->qk", query_h, key_h, preferred_element_type=jnp.float32) * score_scale
    )
    return jnp.where(allowed, scores, -1e30)


def head_forward(entries, allowed, score_scale):
    query_h, key_h, value_h = entries
    scores = head_scores(query_h, key_h, allowed, score_scale)
    row_max = jnp.max(scores, axis=-1, keepdims=True)
    exp_scores = jnp.exp(scores - row_max)
    row_total = jnp.sum(exp_scores, axis=-1, keepdims=True)
    prob_low = (exp_scores / row_total).astype(jnp.bfloat16)
    head_out = jnp.dot(prob_low, value_h, preferred_element_type=jnp.float32)
    return (head_out, (row_max + jnp.log(row_total))[:, 0])


def head_backward(entries, allowed, score_scale):
    query_h, key_h, value_h, grad_head, log_total = entries
    scores = head_scores(query_h, key_h, allowed, score_scale)
    prob_full = jnp.where(allowed, jnp.exp(scores - log_total[:, None]), 0.0)
    prob_low = prob_full.astype(jnp.bfloat16)
    grad_value = jnp.einsum("qk,qd->kd", prob_low, grad_head, preferred_element_type=jnp.float32)
    grad_prob = jnp.einsum("qd,kd->qk", grad_head, value_h, preferred_element_type=jnp.float32)
    grad_score = prob_full * (grad_prob - jnp.sum(prob_full * grad_prob, axis=-1, keepdims=True))
    grad_score = grad_score.astype(jnp.bfloat16)
    grad_query = jnp.dot(grad_score, key_h, preferred_element_type=jnp.float32) * score_scale
    grad_key = (
        jnp.einsum("qk,qd->kd", grad_score, query_h, preferred_element_type=jnp.float32)
        * score_scale
    )
    return (grad_query, grad_key, grad_value)


def per_device(
    tokens,
    cotangent,
    lengths,
    expert_ids,
    slot_ids,
    w_qkv,
    w_out,
    gain_one,
    w_in,
    w_down,
    w_expert_in,
    w_expert_out,
    w_mix,
    gain_two,
):
    row_count, model_width = tokens.shape
    head_count = model_width // HEAD_DIM
    score_scale = HEAD_DIM ** (-0.5)
    full_qkv, full_out, full_gain_one = (
        lax.all_gather(w_qkv, ("dp", "fsdp"), axis=0, tiled=True),
        lax.all_gather(w_out, ("dp", "fsdp"), axis=0, tiled=True),
        lax.all_gather(gain_one, ("dp", "fsdp"), axis=0, tiled=True),
    )
    full_in, full_down, full_expert_in, full_expert_out, full_mix, full_gain_two = (
        lax.all_gather(w_in, ("dp", "fsdp"), axis=0, tiled=True),
        lax.all_gather(w_down, ("dp", "fsdp"), axis=0, tiled=True),
        lax.all_gather(w_expert_in, ("dp", "fsdp"), axis=1, tiled=True),
        lax.all_gather(w_expert_out, ("dp", "fsdp"), axis=1, tiled=True),
        lax.all_gather(w_mix, ("dp", "fsdp"), axis=0, tiled=True),
        lax.all_gather(gain_two, ("dp", "fsdp"), axis=0, tiled=True),
    )
    position = jnp.arange(row_count, dtype=jnp.int32)
    seq_len = lengths[0]
    row_keep = (position < seq_len).astype(jnp.float32)[:, None]
    allowed = (position[None, :] <= position[:, None]) & (position[None, :] < seq_len)

    def to_heads(block):
        return block.reshape(row_count, head_count, HEAD_DIM).transpose(1, 0, 2)

    def from_heads(block):
        return block.transpose(1, 0, 2).reshape(row_count, model_width)

    stream = tokens.astype(jnp.float32)
    gain_first = full_gain_one.astype(jnp.float32)
    normed_one = layer_norm(stream, gain_first).astype(jnp.bfloat16)
    qkv_all = jnp.dot(normed_one, full_qkv, preferred_element_type=jnp.float32).astype(jnp.bfloat16)
    queries = to_heads(qkv_all[:, :model_width])
    key_heads = to_heads(qkv_all[:, model_width : 2 * model_width])
    value_heads = to_heads(qkv_all[:, 2 * model_width :])
    head_out, log_total = lax.map(
        lambda entries: head_forward(entries, allowed, score_scale),
        (queries, key_heads, value_heads),
    )
    attended = from_heads(head_out).astype(jnp.bfloat16)
    stream_two = stream + jnp.dot(attended, full_out, preferred_element_type=jnp.float32)
    gain_second = full_gain_two.astype(jnp.float32)
    normed_two = layer_norm(stream_two, gain_second).astype(jnp.bfloat16)
    dense_up = jnp.dot(normed_two, full_in, preferred_element_type=jnp.float32)
    dense_act = gelu_tanh(dense_up).astype(jnp.bfloat16)
    dense_out = jnp.dot(dense_act, full_down, preferred_element_type=jnp.float32)
    routed = slot_ids >= 0
    table_row = jnp.where(routed, expert_ids * CAP + slot_ids, 0)
    slot_total = EXPERTS * CAP
    dispatch = (
        (table_row[None, :] == jnp.arange(slot_total, dtype=jnp.int32)[:, None]) & routed[None, :]
    ).astype(jnp.bfloat16)
    buffer = jnp.dot(dispatch, normed_two, preferred_element_type=jnp.float32).astype(jnp.bfloat16)
    buffer = buffer.reshape(EXPERTS, CAP, model_width)
    expert_up = jnp.einsum(
        "ecd,edf->ecf", buffer, full_expert_in, preferred_element_type=jnp.float32
    )
    expert_act = gelu_tanh(expert_up).astype(jnp.bfloat16)
    expert_y = jnp.einsum(
        "ecf,efd->ecd", expert_act, full_expert_out, preferred_element_type=jnp.float32
    )
    expert_y = expert_y.reshape(slot_total, model_width)
    expert_mix = jnp.where(routed[:, None], expert_y[table_row], 0.0)
    logits = jnp.dot(normed_two, full_mix, preferred_element_type=jnp.float32)
    mix_coeff = jax.nn.softmax(logits, axis=-1)
    branch = mix_coeff[:, 0:1] * dense_out + mix_coeff[:, 1:2] * expert_mix
    block_out = ((stream_two + branch) * row_keep).astype(jnp.bfloat16)
    grad_out = cotangent.astype(jnp.float32) * row_keep
    grad_dense = (mix_coeff[:, 0:1] * grad_out).astype(jnp.bfloat16)
    grad_expert = (mix_coeff[:, 1:2] * grad_out).astype(jnp.bfloat16)
    grad_coeff = jnp.stack(
        [jnp.sum(grad_out * dense_out, axis=-1), jnp.sum(grad_out * expert_mix, axis=-1)], axis=-1
    )
    grad_logits = jax.vjp(lambda values_in: jax.nn.softmax(values_in, axis=-1), logits)[1](
        grad_coeff
    )[0]
    full_in, full_down, full_expert_in, full_expert_out, full_mix, full_gain_two = (
        lax.all_gather(w_in, ("dp", "fsdp"), axis=0, tiled=True),
        lax.all_gather(w_down, ("dp", "fsdp"), axis=0, tiled=True),
        lax.all_gather(w_expert_in, ("dp", "fsdp"), axis=1, tiled=True),
        lax.all_gather(w_expert_out, ("dp", "fsdp"), axis=1, tiled=True),
        lax.all_gather(w_mix, ("dp", "fsdp"), axis=0, tiled=True),
        lax.all_gather(gain_two, ("dp", "fsdp"), axis=0, tiled=True),
    )
    gain_second = full_gain_two.astype(jnp.float32)
    grad_w_down = jnp.einsum("tf,td->fd", dense_act, grad_dense, preferred_element_type=jnp.float32)
    grad_dense_act = jnp.einsum(
        "td,fd->tf", grad_dense, full_down, preferred_element_type=jnp.float32
    )
    grad_dense_up = gelu_back(dense_up, grad_dense_act).astype(jnp.bfloat16)
    grad_w_in = jnp.einsum(
        "td,tf->df", normed_two, grad_dense_up, preferred_element_type=jnp.float32
    )
    grad_normed_two = jnp.einsum(
        "tf,df->td", grad_dense_up, full_in, preferred_element_type=jnp.float32
    )
    grad_y = jnp.dot(dispatch, grad_expert, preferred_element_type=jnp.float32).astype(jnp.bfloat16)
    grad_y = grad_y.reshape(EXPERTS, CAP, model_width)
    grad_expert_out_lead = jnp.einsum(
        "ecf,ecd->fed", expert_act, grad_y, preferred_element_type=jnp.float32
    )
    grad_expert_act = jnp.einsum(
        "ecd,efd->ecf", grad_y, full_expert_out, preferred_element_type=jnp.float32
    )
    grad_expert_up = gelu_back(expert_up, grad_expert_act).astype(jnp.bfloat16)
    grad_expert_in_lead = jnp.einsum(
        "ecd,ecf->def", buffer, grad_expert_up, preferred_element_type=jnp.float32
    )
    grad_buffer = jnp.einsum(
        "ecf,edf->ecd", grad_expert_up, full_expert_in, preferred_element_type=jnp.float32
    )
    grad_buffer = grad_buffer.reshape(slot_total, model_width)
    grad_normed_two = grad_normed_two + jnp.where(routed[:, None], grad_buffer[table_row], 0.0)
    mix_full = full_mix.astype(jnp.float32)
    normed_full = normed_two.astype(jnp.float32)
    grad_normed_two = grad_normed_two + jnp.dot(
        grad_logits, mix_full.T, precision=lax.Precision.HIGHEST
    )
    grad_w_mix = jnp.dot(normed_full.T, grad_logits, precision=lax.Precision.HIGHEST)
    _, pull_two = jax.vjp(layer_norm, stream_two, gain_second)
    grad_stream_ln, grad_gain_two = pull_two(grad_normed_two)
    grad_stream_two = grad_out + grad_stream_ln
    full_qkv, full_out, full_gain_one = (
        lax.all_gather(w_qkv, ("dp", "fsdp"), axis=0, tiled=True),
        lax.all_gather(w_out, ("dp", "fsdp"), axis=0, tiled=True),
        lax.all_gather(gain_one, ("dp", "fsdp"), axis=0, tiled=True),
    )
    gain_first = full_gain_one.astype(jnp.float32)
    grad_attn = grad_stream_two.astype(jnp.bfloat16)
    grad_w_out = jnp.einsum("td,te->de", attended, grad_attn, preferred_element_type=jnp.float32)
    grad_attended = jnp.einsum(
        "te,de->td", grad_attn, full_out, preferred_element_type=jnp.float32
    ).astype(jnp.bfloat16)
    grad_query, grad_key, grad_value = lax.map(
        lambda entries: head_backward(entries, allowed, score_scale),
        (queries, key_heads, value_heads, to_heads(grad_attended), log_total),
    )
    grad_qkv = jnp.concatenate(
        [from_heads(grad_query), from_heads(grad_key), from_heads(grad_value)], axis=1
    ).astype(jnp.bfloat16)
    grad_w_qkv = jnp.einsum("td,te->de", normed_one, grad_qkv, preferred_element_type=jnp.float32)
    grad_normed_one = jnp.einsum(
        "te,de->td", grad_qkv, full_qkv, preferred_element_type=jnp.float32
    )
    _, pull_one = jax.vjp(layer_norm, stream, gain_first)
    grad_stream_one, grad_gain_one = pull_one(grad_normed_one)
    grad_tokens = grad_stream_two + grad_stream_one
    (
        part_qkv,
        part_out,
        part_gain_one,
        part_in,
        part_down,
        lead_expert_in,
        lead_expert_out,
        part_mix,
        part_gain_two,
    ) = (
        lax.psum_scatter(grad_w_qkv, ("dp", "fsdp"), scatter_dimension=0, tiled=True),
        lax.psum_scatter(grad_w_out, ("dp", "fsdp"), scatter_dimension=0, tiled=True),
        lax.psum_scatter(grad_gain_one, ("dp", "fsdp"), scatter_dimension=0, tiled=True),
        lax.psum_scatter(grad_w_in, ("dp", "fsdp"), scatter_dimension=0, tiled=True),
        lax.psum_scatter(grad_w_down, ("dp", "fsdp"), scatter_dimension=0, tiled=True),
        lax.psum_scatter(grad_expert_in_lead, ("dp", "fsdp"), scatter_dimension=0, tiled=True),
        lax.psum_scatter(grad_expert_out_lead, ("dp", "fsdp"), scatter_dimension=0, tiled=True),
        lax.psum_scatter(grad_w_mix, ("dp", "fsdp"), scatter_dimension=0, tiled=True),
        lax.psum_scatter(grad_gain_two, ("dp", "fsdp"), scatter_dimension=0, tiled=True),
    )
    part_expert_in = lead_expert_in.transpose(1, 0, 2)
    part_expert_out = lead_expert_out.transpose(1, 0, 2)
    return (
        block_out,
        grad_tokens,
        part_qkv,
        part_out,
        part_gain_one,
        part_in,
        part_down,
        part_expert_in,
        part_expert_out,
        part_mix,
        part_gain_two,
    )


BF = jnp.bfloat16
F32 = jnp.float32
MESH = pl.DeviceIdType.MESH
ANY = pl.BlockSpec(memory_space=pl.ANY)
VM = pl.BlockSpec(memory_space=pltpu.VMEM)
SM = pl.BlockSpec(memory_space=pltpu.SMEM)
MIB = 1024 * 1024


def dot_nn(a, b):
    return lax.dot_general(a, b, (((1,), (0,)), ((), ())), preferred_element_type=F32)


def dot_nt(a, b):
    return lax.dot_general(a, b, (((1,), (1,)), ((), ())), preferred_element_type=F32)


def dot_tn(a, b):
    return lax.dot_general(a, b, (((0,), (0,)), ((), ())), preferred_element_type=F32)


class Place:
    def __init__(self):
        dp, fs = lax.axis_index("dp"), lax.axis_index("fsdp")
        z, y, x, c = dp // 2, dp % 2, fs // 2, fs % 2
        self.z, self.y, self.x, self.c = z, y, x, c
        self.own = (y, x, c)
        self.sib = (y, x, 1 - c)
        self.d1 = ((y + c) % 2, (x + 1 - c) % 2, c)
        self.d2 = ((y + 1 - c) % 2, (x + c) % 2, c)
        self.dd = (1 - y, 1 - x, c)
        self.zk = [z, z + 1 - 2 * (z % 2), (z + 2) % 4, 3 - z]
        self.t = self.rank(self.own)
        self.b = z * 8 + self.t

    @staticmethod
    def rank(p):
        return p[0] * 4 + p[1] * 2 + p[2]

    def flip(self, p):
        return (p[0], p[1], 1 - p[2])

    def dev(self, p, z=None):
        z = self.z if z is None else z
        return (z * 2 + p[0], p[1] * 2 + p[2])

    def plane_others(self):
        y, x, c = self.own
        return [
            ((y + k // 4) % 2, (x + (k // 2) % 2) % 2, (c + k % 2) % 2) for k in range(1, 8)
        ]


def rcopy(src, dst, send, recv, dev):
    return pltpu.make_async_remote_copy(
        src_ref=src, dst_ref=dst, send_sem=send, recv_sem=recv, device_id=dev, device_id_type=MESH
    )


def meet(devs):
    bar = pltpu.get_barrier_semaphore()
    for dev in devs:
        pl.semaphore_signal(bar, inc=1, device_id=dev, device_id_type=MESH)
    pl.semaphore_wait(bar, len(devs))


def norm_parts(v):
    mean = jnp.mean(v, axis=-1, keepdims=True)
    cen = v - mean
    var = jnp.mean(cen * cen, axis=-1, keepdims=True)
    r = lax.rsqrt(var + 1e-05)
    return cen * r, r


def row_of(extra, lane):
    pick = (lax.broadcasted_iota(jnp.int32, (8, 128), 1) == lane).astype(BF)
    return dot_nt(pick, extra)[0:1]


class ZSum:
    def __init__(self, P_, src, land, via, send, recv):
        self.P, self.src, self.land, self.via = P_, src, land, via
        self.send, self.recv = send, recv
        self.mid = (P_.z == 1) | (P_.z == 2)

    def copy(self, n, w, j):
        P_ = self.P
        to = P_.dev(P_.own, P_.zk[1 if j == 4 else j])
        block = self.src[w].at[n, P_.zk[3 if j == 4 else j]]
        dst = self.via[w].at[n] if j == 4 else self.land[w].at[n, j - 1]
        i = w * 4 + j - 1
        return rcopy(block, dst, self.send.at[n, i], self.recv.at[n, i], to)

    def ship(self, n, ws=(0, 1)):
        @pl.when(self.mid)
        def _():
            for j in (3, 1):
                for w in ws:
                    self.copy(n, w, j).start()

        @pl.when(jnp.logical_not(self.mid))
        def _():
            for j in (4, 2, 1):
                for w in ws:
                    self.copy(n, w, j).start()

    def transit(self, n, ws=(0, 1)):
        @pl.when(self.mid)
        def _():
            k2 = self.P.zk[2]
            for w in ws:
                self.copy(n, w, 4).wait_recv()
                self.src[w][n, k2] = self.src[w][n, k2] + self.via[w][n]
                self.copy(n, w, 2).start()

    def arrived(self, n, ws=(0, 1)):
        for w in ws:
            self.copy(n, w, 1).wait_recv()
            self.copy(n, w, 2).wait_recv()

        @pl.when(self.mid)
        def _():
            for w in ws:
                self.copy(n, w, 3).wait_recv()

    def sent(self, n, ws=(0, 1)):
        for w in ws:
            self.copy(n, w, 1).wait_send()
            self.copy(n, w, 2).wait_send()

        @pl.when(self.mid)
        def _():
            for w in ws:
                self.copy(n, w, 3).wait_send()

        @pl.when(jnp.logical_not(self.mid))
        def _():
            for w in ws:
                self.copy(n, w, 4).wait_send()


class ZGather:
    def __init__(self, P_, mine, full, send, recv):
        self.P, self.mine, self.full, self.send, self.recv = P_, mine, full, send, recv
        self.mid = (P_.z == 1) | (P_.z == 2)
        self.all = range(len(mine))

    def copy(self, w, j):
        P_ = self.P
        zs = P_.zk[2] if j == 4 else P_.z
        block = self.full[w](zs) if j == 4 else self.mine[w]
        to = P_.dev(P_.own, P_.zk[1 if j == 4 else j])
        return rcopy(block, self.full[w](zs), self.send.at[w * 4 + j - 1], self.recv.at[w * 4 + zs], to)

    def landed(self, w, j):
        P_ = self.P
        zs = P_.zk[j]
        rcopy(
            self.mine[w], self.full[w](zs), self.send.at[0], self.recv.at[w * 4 + zs], P_.dev(P_.sib)
        ).wait_recv()

    def ship(self):
        for w in self.all:
            self.copy(w, 2).start()

        @pl.when(self.mid)
        def _():
            for w in self.all:
                self.copy(w, 3).start()

        for w in self.all:
            self.copy(w, 1).start()

    def relay(self):
        for w in self.all:
            self.landed(w, 2)

        @pl.when(self.mid)
        def _():
            for w in self.all:
                self.copy(w, 4).start()

    def finish(self):
        for w in self.all:
            self.landed(w, 1)
            self.landed(w, 3)
            self.copy(w, 1).wait_send()
            self.copy(w, 2).wait_send()

        @pl.when(self.mid)
        def _():
            for w in self.all:
                self.copy(w, 3).wait_send()
                self.copy(w, 4).wait_send()


PW = 4224
EX = 3072
WO = 3200


def enter_kernel(
    len_ref, tok, cot, tab, w_qkv, w_out, small, w_in, w_ein, w_down, w_eout,
    qkv_o, lse_o, att_o, s2_o, n1_o, wmix_o, pack_all, wi_all, wd_all, g_all, nt_all,
    pack_v, wia, gt, qkv, lse, att, s2, nt, n1,
    pz, ps, pr, asend, arecv, fsend, frecv, gs, gr, ts, tr, lsem, osem,
):
    P_ = Place()
    z, t, b = P_.z, P_.t, P_.b
    own, sib, d1, d2, dd = P_.own, P_.sib, P_.d1, P_.d2, P_.dd
    others = P_.plane_others()
    pack = pack_v.at[b]
    pack_v[b, :, 0:3072] = w_qkv[...]
    pack_v[b, :, EX : EX + 128] = small[...]
    pack_v[b, :, WO : WO + 1024] = w_out[...]
    meet([P_.dev(p) for p in others] + [P_.dev(own, zz) for zz in P_.zk[1:]])
    sends = []
    keeps = []

    def go(cp):
        cp.start()
        sends.append(cp)

    def store(src, dst):
        cp = pltpu.make_async_copy(src, dst, osem.at[len(keeps)])
        cp.start()
        keeps.append(cp)

    def gather(n, mine, full):
        return ZGather(P_, (mine,), (full,), fsend.at[n], frecv.at[n])

    out_a = gather(0, w_eout.at[0], lambda zs: wd_all.at[1, zs])
    out_b = gather(1, w_eout.at[1], lambda zs: wd_all.at[2, zs])
    in_a = gather(2, wi_all.at[1, z], lambda zs: wi_all.at[1, zs])
    in_b = gather(3, wi_all.at[2, z], lambda zs: wi_all.at[2, zs])
    mid = in_a.mid

    def z_copy(k, s, to):
        return rcopy(pack_v.at[s], pack_v.at[s], pz.at[k - 1], pr.at[s], P_.dev(own, P_.zk[to]))

    z_copy(2, b, 2).start()

    @pl.when(mid)
    def _():
        z_copy(3, b, 3).start()

    z_copy(1, b, 1).start()
    go(rcopy(pack, pack, ps.at[3], pr.at[b], P_.dev(d1)))
    go(rcopy(pack, pack, ps.at[7], pr.at[b], P_.dev(d2)))
    go(rcopy(pack, pack, ps.at[15], pr.at[b], P_.dev(sib)))
    out_a.ship()
    for r in range(8):
        for zz in range(4):
            at = slice((zz * 8 + r) * 128, (zz * 8 + r + 1) * 128)
            to = slice(zz * 128, (zz + 1) * 128)
            wia[r, 0, :, to] = w_in[:, at]
            wia[r, 1:3, :, to] = w_ein[:, :, at]
    rows = pl.ds(pl.multiple_of(t * 32, 32), 32)
    lw = pltpu.make_async_copy(wia.at[t], wi_all.at[:, z, rows], lsem.at[1])
    lw.start()
    for i, p in enumerate(others):
        go(rcopy(wia.at[P_.rank(p)], wi_all.at[:, z, rows], asend.at[i], arecv.at[t], P_.dev(p)))
    store(w_down, wd_all.at[0, z])
    store(w_eout, wd_all.at[1:3, z])
    keep = lax.broadcasted_iota(jnp.int32, (384, 1), 0) < len_ref[0]
    gt[0:384] = jnp.where(keep, cot[...], jnp.zeros_like(cot[...]))
    gt[384:400] = jnp.zeros((16, 1024), BF)
    gt[384:385, 0:384] = tab[...].astype(BF)

    def landed(slot):
        rcopy(pack, pack_v.at[slot], ps.at[0], pr.at[slot], P_.dev(sib)).wait_recv()

    def fwd(slot, sem, p):
        go(rcopy(pack_v.at[slot], pack_v.at[slot], ps.at[sem], pr.at[slot], P_.dev(p)))

    def slot(k, p):
        return P_.zk[k] * 8 + P_.rank(p)

    for k in range(0, 6):
        if k == 2:
            out_b.ship()
        if 1 <= k <= 3:
            s = slot(k, own)
            landed(s)
            if k == 2:

                @pl.when(mid)
                def _():
                    z_copy(4, s, 1).start()

            fwd(s, 3 + k, d1)
            fwd(s, 7 + k, d2)
            fwd(s, 15 + k, sib)
        if k == 3:
            lw.wait()
            for p in others:
                rr = P_.rank(p)
                rq = pl.ds(pl.multiple_of(rr * 32, 32), 32)
                rcopy(
                    wia.at[0], wi_all.at[:, z, rq], asend.at[0], arecv.at[rr], P_.dev(sib)
                ).wait_recv()
            out_a.relay()
            in_a.ship()
        if k == 4:
            store(gt, g_all.at[t])
            for i, p in enumerate((d1, d2, sib)):
                go(rcopy(gt, g_all.at[t], gs.at[i], gr.at[t], P_.dev(p)))
        if 1 <= k <= 4:
            s = slot(k - 1, d1)
            landed(s)
            fwd(s, 11 + k - 1, d2)
            fwd(s, 19 + k - 1, sib)
            s = slot(k - 1, d2)
            landed(s)
            fwd(s, 23 + k - 1, sib)
        if k >= 2:
            s = slot(k - 2, dd)
            landed(s)
            fwd(s, 27 + k - 2, sib)
    out_b.relay()
    in_b.ship()
    stream = tok[...].astype(F32)
    for k in range(4):
        for p in (own, d1, d2, dd):
            landed(slot(k, P_.flip(p)))
    store(pack_v, pack_all)
    store(pack_v.at[:, :, EX : EX + 128], wmix_o)

    extra = pack_v[:, :, EX : EX + 128].reshape(1024, 128)
    n_one, _ = norm_parts(stream)
    n1[...] = (n_one * row_of(extra, 2)).astype(BF)
    store(n1, n1_o)

    def qkv_step(j, carry):
        cols = pl.ds(pl.multiple_of(j * 512, 512), 512)
        qkv[:, cols] = dot_nn(n1[...], pack_v[:, :, cols].reshape(1024, 512)).astype(BF)
        return carry

    lax.fori_loop(0, 6, qkv_step, 0)
    store(qkv, qkv_o)

    def plane(src_own, full, send, recv):
        def landed_at(p):
            r = P_.rank(p)
            rcopy(src_own, full.at[r], send.at[0], recv.at[r], P_.dev(sib)).wait_recv()
            return r

        def pass_on(p, *dests):
            r = landed_at(p)
            for i, q in dests:
                go(rcopy(full.at[r], full.at[r], send.at[i], recv.at[r], P_.dev(q)))

        return landed_at, pass_on

    g_landed, g_pass = plane(gt, g_all, gs, gr)
    n_landed, n_pass = plane(nt, nt_all, ts, tr)
    g_pass(d1, (4, sib))

    allowed = masks(len_ref[0])
    lane = lax.broadcasted_iota(jnp.int32, (384, 128), 1)
    lse[...] = jnp.zeros_like(lse)

    def pair_step(p, carry):
        q2 = qkv[:, pl.ds(pl.multiple_of(p * 128, 128), 128)]
        k2 = qkv[:, pl.ds(pl.multiple_of(1024 + p * 128, 128), 128)]
        v2 = qkv[:, pl.ds(pl.multiple_of(2048 + p * 128, 128), 128)]
        outs = []
        for hh in range(2):
            qm = jnp.where(lane // 64 == hh, q2, jnp.zeros_like(q2))
            sc = jnp.where(allowed, dot_nt(qm, k2) * 0.125, -1e30)
            top = jnp.max(sc, axis=-1, keepdims=True)
            ex = jnp.exp(sc - top)
            tot = jnp.sum(ex, axis=-1, keepdims=True)
            outs.append(dot_nn((ex * (1.0 / tot)).astype(BF), v2))
            lse[...] = jnp.where(lane == 2 * p + hh, top + jnp.log(tot), lse[...])
        att[:, pl.ds(pl.multiple_of(p * 128, 128), 128)] = jnp.where(
            lane < 64, outs[0], outs[1]
        ).astype(BF)

        @pl.when(p == 4)
        def _():
            in_a.relay()

        return carry

    lax.fori_loop(0, 8, pair_step, 0)
    store(lse, lse_o)
    store(att, att_o)
    for j in range(2):
        w = pack_v[:, :, WO + j * 512 : WO + (j + 1) * 512].reshape(1024, 512)
        s2[:, j * 512 : (j + 1) * 512] = stream[:, j * 512 : (j + 1) * 512] + dot_nn(att[...], w)
    store(s2, s2_o)
    n_two, _ = norm_parts(s2[...])
    nt[...] = (n_two * row_of(extra, 3)).astype(BF)
    store(nt, nt_all.at[t])
    for i, p in enumerate((d1, d2, sib)):
        go(rcopy(nt, nt_all.at[t], ts.at[i], tr.at[t], P_.dev(p)))
    g_pass(d2, (5, sib))
    in_b.relay()
    n_pass(d1, (4, sib))
    n_pass(d2, (5, sib))
    for p in (own, d1, d2):
        g_landed(P_.flip(p))
    for p in (own, d2, d1):
        n_landed(P_.flip(p))
    for part in (out_a, out_b, in_a, in_b):
        part.finish()
    z_copy(1, b, 1).wait_send()
    z_copy(2, b, 2).wait_send()

    @pl.when(mid)
    def _():
        z_copy(3, b, 3).wait_send()
        z_copy(4, b, 1).wait_send()

    for cp in keeps:
        cp.wait()
    for cp in sends:
        cp.wait_send()


def masks(seq_len):
    row = lax.broadcasted_iota(jnp.int32, (384, 384), 0)
    col = lax.broadcasted_iota(jnp.int32, (384, 384), 1)
    return (col <= row) & (col < seq_len)


def run_enter(*args):
    sd = jax.ShapeDtypeStruct
    dma = pltpu.SemaphoreType.DMA
    return pl.pallas_call(
        enter_kernel,
        out_shape=(
            sd((384, 3072), BF), sd((384, 128), F32), sd((384, 1024), BF), sd((384, 1024), F32),
            sd((384, 1024), BF), sd((32, 32, 128), BF),
            sd((32, 32, PW), BF), sd((3, 4, 256, 512), BF), sd((3, 4, 128, 1024), BF),
            sd((8, 400, 1024), BF), sd((8, 384, 1024), BF),
        ),
        in_specs=[SM] + [VM] * 10,
        out_specs=(ANY,) * 11,
        scratch_shapes=[
            pltpu.VMEM((32, 32, PW), BF), pltpu.VMEM((8, 3, 32, 512), BF), pltpu.VMEM((400, 1024), BF),
            pltpu.VMEM((384, 3072), BF), pltpu.VMEM((384, 128), F32), pltpu.VMEM((384, 1024), BF),
            pltpu.VMEM((384, 1024), F32), pltpu.VMEM((384, 1024), BF), pltpu.VMEM((384, 1024), BF),
            dma((4,)), dma((31,)), dma((32,)), dma((7,)), dma((8,)), dma((4, 4)), dma((4, 4)),
            dma((7,)), dma((8,)), dma((7,)), dma((8,)), dma((4,)), dma((12,)),
        ],
        compiler_params=pltpu.CompilerParams(
            collective_id=0, has_side_effects=True, vmem_limit_bytes=63 * MIB
        ),
    )(*args)


def mix_of(delta):
    return 1.0 / (1.0 + jnp.exp(-delta)), 1.0 / (1.0 + jnp.exp(delta))


def gelu_both(u):
    a, bb = 0.7978845608028654, 0.044715
    u2 = u * u
    th = jnp.tanh(a * u * (1.0 + bb * u2))
    half = 0.5 * (1.0 + th)
    return u * half, half + 0.5 * u * (1.0 - th * th) * a * (1.0 + 3.0 * bb * u2)


def ff_kernel(
    nt_hbm, wmix, g_all, wi_all, wd_all,
    gsum, gl_out, bnext, bown, eoi, eod, dgi, dgd, r1, r2, rin, rdn, dwi, dwd, gfar,
    nt_all, gbuf, br, gn, xb, yb, wi, wd, ai, ad, gin, gdn, tri, trd, tmp, gc, gcr, dots, gaps,
    ts, tr, gs, gr, gsem, wsem, dsem, zas, zar, zss, zsr, s1s, s1r, s2s, s2r, cs, cr, lsem, tsem,
):
    P_ = Place()
    z, t = P_.z, P_.t
    own, sib, d1, d2, dd = P_.own, P_.sib, P_.d1, P_.d2, P_.dd
    others = P_.plane_others()
    meet([P_.dev(p) for p in others] + [P_.dev(own, zz) for zz in P_.zk[1:]])
    sends = []

    def go(cp):
        cp.start()
        sends.append(cp)

    keeps = []

    def keep(src, dst):
        cp = pltpu.make_async_copy(src, dst, lsem.at[len(keeps)])
        cp.start()
        keeps.append(cp)

    dense = ZGather(
        P_, (wi_all.at[0, z], wd_all.at[0, z]), (lambda zs: dwi.at[zs], lambda zs: dwd.at[zs]), zas, zar
    )
    dense.ship()
    expert_load = (
        pltpu.make_async_copy(wi_all.at[1], wi.at[0], wsem.at[0, 0]),
        pltpu.make_async_copy(wd_all.at[1], wd.at[0], wsem.at[0, 1]),
        pltpu.make_async_copy(wi_all.at[2], wi.at[1], wsem.at[1, 0]),
        pltpu.make_async_copy(wd_all.at[2], wd.at[1], wsem.at[1, 1]),
    )
    for cp in expert_load:
        cp.start()

    def dense_load():
        copies = []
        for k in range(4):
            zz = P_.zk[k]
            for n, (full, far, dst) in enumerate(((wi_all, dwi, wi), (wd_all, dwd, wd))):
                src = full.at[0, z] if k == 0 else far.at[zz]
                copies.append(pltpu.make_async_copy(src, dst.at[0, zz], dsem.at[n, k]))
        return copies

    zsum = ZSum(P_, (gin, gdn), (rin, rdn), (tri, trd), zss, zsr)

    order = (own, sib, d1, P_.flip(d2), d2, P_.flip(d1), dd, P_.flip(dd))
    ranks = [P_.rank(p) for p in order]

    def seq_at(i):
        s = ranks[0]
        for k in range(1, 8):
            s = jnp.where(i == k, ranks[k], s)
        return s

    r1st, rdd = P_.rank(d1), P_.rank(dd)
    go(rcopy(nt_hbm.at[r1st], nt_all.at[r1st], ts.at[0], tr.at[r1st], P_.dev(d2)))
    go(rcopy(g_all.at[r1st], gfar.at[0], gs.at[0], gr.at[0], P_.dev(d2)))

    def far_on(start):
        cps = (
            rcopy(nt_all.at[rdd], nt_all.at[rdd], ts.at[1], tr.at[rdd], P_.dev(sib)),
            rcopy(gfar.at[0], gfar.at[1], gs.at[1], gr.at[1], P_.dev(sib)),
        )
        for cp in cps:
            if start:
                cp.start()
            else:
                cp.wait_send()

    def far_here(s, k):
        rcopy(gfar.at[0], gfar.at[k], gs.at[0], gr.at[k], P_.dev(sib)).wait_recv()
        rcopy(tmp.at[0], nt_all.at[s], ts.at[0], tr.at[s], P_.dev(sib)).wait_recv()

    class GCopy:
        def __init__(self, i):
            self.i = i

        def make(self, src):
            return pltpu.make_async_copy(src, gbuf.at[self.i % 2], gsem.at[self.i % 2])

        def start(self):
            @pl.when(self.i < 6)
            def _():
                self.make(g_all.at[seq_at(self.i)]).start()

            @pl.when(self.i >= 6)
            def _():
                self.make(gfar.at[jnp.maximum(self.i - 6, 0)]).start()

        def wait(self):
            self.make(g_all.at[0]).wait()

    def g_copy(i):
        return GCopy(i)

    def ff(xv, gv, k):
        wiv = wi[k].reshape(1024, 512)
        wdv = wd[k].reshape(512, 1024)
        act, dact = gelu_both(dot_nn(xv, wiv))
        act = act.astype(BF)
        gup = (dact * dot_nt(gv, wdv)).astype(BF)
        ad[k] += dot_tn(act, gv)
        ai[k] += dot_tn(xv, gup)
        return dot_nn(act, wdv), dot_nt(gup, wiv)

    lane = lax.broadcasted_iota(jnp.int32, (448, 128), 1)

    def shares(tab):
        slot = lax.broadcasted_iota(jnp.int32, (224, 384), 0)
        return (tab == slot.astype(F32)).astype(BF)

    def n_copy(s):
        return pltpu.make_async_copy(nt_hbm.at[s], nt_all.at[s], tr.at[s])

    for s in ranks[:6]:
        n_copy(s).start()
    g_copy(0).start()
    ai[...] = jnp.zeros_like(ai)
    ad[...] = jnp.zeros_like(ad)
    for cp in expert_load:
        cp.wait()

    def arrive(i, carry):
        s = seq_at(i)

        @pl.when(i == 5)
        def _():
            far_here(rdd, 0)
            far_on(True)

        @pl.when(i == 6)
        def _():
            far_here(P_.rank(P_.flip(dd)), 1)

        @pl.when(i + 1 < 8)
        def _():
            g_copy(i + 1).start()

        @pl.when(i < 6)
        def _():
            n_copy(s).wait()

        g_copy(i).wait()
        xv = nt_all[s]
        gv = gbuf[i % 2, :384]
        tab = gbuf[i % 2, 384:400][0:1, :384].astype(F32)
        lg = dot_nn(xv, wmix[...])
        gap = lg[:, 0:1] - lg[:, 1:2]
        gaps[i] = jnp.transpose(jnp.broadcast_to(gap, (384, 128)))[0:8]
        _, m1 = mix_of(gap)
        ge = (m1 * gv.astype(F32)).astype(BF)
        sh = shares(tab)
        xb[i] = dot_nn(sh, xv).astype(BF).reshape(2, 112, 1024)
        yb[i] = dot_nn(sh, ge).astype(BF).reshape(2, 112, 1024)
        return carry

    def expert(b, e):
        four = pl.ds(b * 4, 4)
        gq = yb[four, e].reshape(448, 1024)
        yv, gb = ff(xb[four, e].reshape(448, 1024), gq, e)
        rs = jnp.sum(gq.astype(F32) * yv, axis=-1, keepdims=True)
        high = rs.astype(BF).astype(F32)
        dots[four, e] = (
            jnp.where(lane == 0, high, jnp.where(lane == 1, rs - high, 0.0))
            .astype(BF)
            .reshape(4, 112, 128)
        )
        xb[four, e] = yv.astype(BF).reshape(4, 112, 1024)
        yb[four, e] = gb.astype(BF).reshape(4, 112, 1024)

    def stage(e):
        gin[e] = ai[e].astype(BF).reshape(4, 256, 512)
        gdn[e] = ad[e].astype(BF).reshape(4, 128, 1024)
        zsum.ship(e)
        keep(gin.at[e, z], eoi.at[e])
        keep(gdn.at[e, z], eod.at[e])

    def half(b, carry):
        lax.fori_loop(b * 4, b * 4 + 4, arrive, 0)
        @pl.when(b == 1)
        def _():
            dense.relay()

        expert(b, 0)
        expert(b, 1)
        return carry

    lax.fori_loop(0, 2, half, 0)
    stage(0)
    stage(1)
    far_on(False)
    g_copy(7).start()
    dense.finish()
    for cp in dense_load():
        cp.start()
    ai[0] = jnp.zeros_like(ai[0])
    ad[0] = jnp.zeros_like(ad[0])
    for cp in dense_load():
        cp.wait()

    chips = (dd, d1, d2, own)
    both = (gn, br)

    def give1(q, w):
        r = P_.rank(P_.flip(chips[q]))
        k = (0, 2, 1, 3)[q]
        return rcopy(both[w].at[r], r1.at[w, k], s1s.at[w, k], s1r.at[w, k], P_.dev(sib))

    def load1(q, w, start):
        cp = pltpu.make_async_copy(r1.at[w, q], tmp.at[w], tsem.at[w])
        if start:
            rcopy(tmp.at[0], r1.at[w, q], s1s.at[0, 0], s1r.at[w, q], P_.dev(sib)).wait_recv()
            cp.start()
        else:
            cp.wait()
            add_tmp(w, P_.rank(chips[q]))

    def load2(k, p, w, start):
        cp = pltpu.make_async_copy(r2.at[w, k], tmp.at[w], tsem.at[w])
        if start:
            rcopy(tmp.at[0], r2.at[w, k], s2s.at[0, 0], s2r.at[w, k], P_.dev(sib)).wait_recv()
            cp.start()
        else:
            cp.wait()
            add_tmp(w, P_.rank(p))

    def add_tmp(w, r):
        both[w][r] = both[w][r] + tmp[w]

    def give2(q, k, p, w):
        src = both[w].at[P_.rank(chips[q])]
        return rcopy(src, r2.at[w, k], s2s.at[w, k], s2r.at[w, k], P_.dev(p))

    def at_step(step, k, fn):
        @pl.when(step == k)
        def _():
            for w in range(2):
                fn(w)

    def dense_step(k, carry):
        i = 7 - k
        s = seq_at(i)

        @pl.when(i > 0)
        def _():
            g_copy(i - 1).start()

        g_copy(i).wait()
        xv = nt_all[s]
        gf = gbuf[i % 2, :384].astype(F32)
        tab = gbuf[i % 2, 384:400][0:1, :384].astype(F32)
        gap = jnp.transpose(jnp.broadcast_to(gaps[i][0:1], (128, 384)))[:, 0:1]
        m0, m1 = mix_of(gap)
        out, gxv = ff(xv, (m0 * gf).astype(BF), 0)
        at_step(k, 1, lambda w: load1(0, w, True))
        at_step(k, 3, lambda w: load1(2, w, True))
        at_step(k, 5, lambda w: load1(1, w, True))
        at_step(k, 7, lambda w: load1(3, w, True))
        col = jnp.broadcast_to(jnp.sum(gf * out, axis=-1, keepdims=True), (384, 128))
        gc[s, 0:8] = jnp.transpose(col)[0:8]
        sh = shares(tab)
        q1 = dot_tn(sh, dots[i].reshape(224, 128))
        gc[s, 8:16] = jnp.transpose(jnp.broadcast_to(q1[:, 0:1] + q1[:, 1:2], (384, 128)))[0:8]
        gn[s] = (gxv + dot_tn(sh, yb[i].reshape(224, 1024))).astype(BF)
        br[s] = (m0 * out + m1 * dot_tn(sh, xb[i].reshape(224, 1024))).astype(BF)

        for q in range(4):
            at_step(k, 2 * q, lambda w, q=q: give1(q, w).start())

        def pass_on(q, n, p):
            def fn(w):
                load1(q, w, False)
                give2(q, n, p, w).start()

            return fn

        at_step(k, 1, pass_on(0, 0, d2))
        at_step(k, 3, pass_on(2, 2, d2))
        at_step(k, 5, lambda w: load1(1, w, False))
        at_step(k, 5, lambda w: load2(0, d1, w, True))

        def turn(w):
            load2(0, d1, w, False)
            if w == 0:
                give2(1, 1, d1, w).start()

        at_step(k, 5, turn)
        at_step(k, 7, lambda w: load1(3, w, False))

        @pl.when(k == 2)
        def _():
            zsum.transit(0)

        @pl.when(k == 5)
        def _():
            zsum.transit(1)

        return carry

    lax.fori_loop(0, 8, dense_step, 0)
    for i, p in enumerate(others):
        go(rcopy(gc.at[P_.rank(p)], gcr.at[t], cs.at[i], cr.at[t], P_.dev(p)))
    keep(br.at[P_.rank(d1)], bnext)
    for w in range(2):
        load2(2, own, w, True)
    for w in range(2):
        load2(2, own, w, False)
    keep(br.at[t], bown)
    load2(1, own, 0, True)
    for p in others:
        r = P_.rank(p)
        rcopy(gc.at[0], gcr.at[r], cs.at[0], cr.at[r], P_.dev(sib)).wait_recv()
    gcr[t] = gc[t]
    tot = jnp.sum(gcr[...], axis=0)
    gc0 = jnp.transpose(jnp.broadcast_to(tot[0:1], (128, 384)))
    q1 = jnp.transpose(jnp.broadcast_to(tot[8:9], (128, 384)))
    m0, m1 = mix_of(jnp.transpose(jnp.broadcast_to(gaps[0][0:1], (128, 384))))
    gl_out[...] = m0 * (m1 * gc0 - q1)
    load2(1, own, 0, False)
    gsum[...] = gn[t].astype(F32)
    zsum.sent(0)
    for cp in keeps[0:2]:
        cp.wait()
    gin[0] = ai[0].astype(BF).reshape(4, 256, 512)
    gdn[0] = ad[0].astype(BF).reshape(4, 128, 1024)
    keep(gin.at[0], dgi)
    keep(gdn.at[0], dgd)
    for w in range(2):
        for q in range(4):
            give1(q, w).wait_send()
        give2(0, 0, d2, w).wait_send()
        give2(2, 2, d2, w).wait_send()
    give2(1, 1, d1, 0).wait_send()
    zsum.arrived(0)
    zsum.arrived(1)
    zsum.sent(1)
    for cp in keeps[2:]:
        cp.wait()
    for cp in sends:
        cp.wait_send()


def run_ff(*args):
    sd = jax.ShapeDtypeStruct
    dma = pltpu.SemaphoreType.DMA
    out = pl.pallas_call(
        ff_kernel,
        out_shape=(
            sd((384, 1024), F32), sd((384, 128), F32), sd((384, 1024), BF), sd((384, 1024), BF),
            sd((2, 256, 512), BF), sd((2, 128, 1024), BF),
            sd((4, 256, 512), BF), sd((4, 128, 1024), BF),
            sd((2, 4, 384, 1024), BF), sd((2, 3, 384, 1024), BF),
            sd((2, 3, 256, 512), BF), sd((2, 3, 128, 1024), BF),
            sd((4, 256, 512), BF), sd((4, 128, 1024), BF), sd((2, 400, 1024), BF),
        ),
        in_specs=[ANY, VM, ANY, ANY, ANY],
        out_specs=(VM,) * 2 + (ANY,) * 13,
        scratch_shapes=[
            pltpu.VMEM((8, 384, 1024), BF), pltpu.VMEM((2, 400, 1024), BF),
            pltpu.VMEM((8, 384, 1024), BF), pltpu.VMEM((8, 384, 1024), BF),
            pltpu.VMEM((8, 2, 112, 1024), BF), pltpu.VMEM((8, 2, 112, 1024), BF),
            pltpu.VMEM((2, 4, 256, 512), BF), pltpu.VMEM((2, 4, 128, 1024), BF),
            pltpu.VMEM((2, 1024, 512), F32), pltpu.VMEM((2, 512, 1024), F32),
            pltpu.VMEM((2, 4, 256, 512), BF), pltpu.VMEM((2, 4, 128, 1024), BF),
            pltpu.VMEM((2, 256, 512), BF), pltpu.VMEM((2, 128, 1024), BF),
            pltpu.VMEM((2, 384, 1024), BF),
            pltpu.VMEM((8, 16, 384), F32), pltpu.VMEM((8, 16, 384), F32), pltpu.VMEM((8, 2, 112, 128), BF),
            pltpu.VMEM((8, 8, 384), F32),
            dma((2,)), dma((8,)), dma((2,)), dma((2,)), dma((2,)), dma((2, 2)), dma((2, 4)), dma((8,)), dma((8,)),
            dma((2, 8)), dma((2, 8)),
            dma((2, 4)), dma((2, 4)), dma((2, 3)), dma((2, 3)), dma((7,)), dma((8,)), dma((10,)), dma((2,)),
        ],
        compiler_params=pltpu.CompilerParams(
            collective_id=1, has_side_effects=True, vmem_limit_bytes=63 * MIB
        ),
    )(*args)
    return (*out[:8], out[10], out[11])


class RowSum:
    swap = (0, 2, 1, 3)

    def __init__(self, P_, g, r1, r2, r3, sems):
        self.P, self.g, self.r1, self.r2, self.r3 = P_, g, r1, r2, r3
        self.s1s, self.s1r, self.s2s, self.s2r, self.s3s, self.s3r = sems
        self.chips = (P_.dd, P_.d1, P_.d2, P_.own)

    def rank(self, q):
        return self.P.rank(self.chips[q])

    def copy1(self, n, q):
        k = self.swap[q]
        src = self.g.at[n, self.P.rank(self.P.flip(self.chips[q]))]
        return rcopy(src, self.r1.at[n, k], self.s1s.at[n, k], self.s1r.at[n, k], self.P.dev(self.P.sib))

    def copy2(self, n, q, k, p):
        src = self.g.at[n, self.rank(q)]
        return rcopy(src, self.r2.at[n, k], self.s2s.at[n, k], self.s2r.at[n, k], self.P.dev(p))

    def copy3(self, n, k):
        P_ = self.P
        return rcopy(
            self.g.at[n, P_.t, P_.zk[k]], self.r3.at[n, k - 1], self.s3s.at[n, k - 1],
            self.s3r.at[n, k - 1], P_.dev(P_.own, P_.zk[k]),
        )

    def in1(self, n, q):
        rcopy(
            self.g.at[n, 0], self.r1.at[n, q], self.s1s.at[n, 0], self.s1r.at[n, q], self.P.dev(self.P.sib)
        ).wait_recv()
        r = self.rank(q)
        self.g[n, r] = self.g[n, r] + self.r1[n, q]

    def in2(self, n, k, q):
        rcopy(
            self.g.at[n, 0], self.r2.at[n, k], self.s2s.at[n, 0], self.s2r.at[n, k], self.P.dev(self.P.sib)
        ).wait_recv()
        r = self.rank(q)
        self.g[n, r] = self.g[n, r] + self.r2[n, k]

    def step1(self, n):
        for q in (0, 1, 2, 3):
            self.copy1(n, q).start()

    def step2(self, n):
        P_ = self.P
        self.in1(n, 0)
        self.copy2(n, 0, 0, P_.d2).start()
        self.in1(n, 2)
        self.copy2(n, 2, 2, P_.d2).start()
        self.in1(n, 1)

    def step3(self, n):
        self.in2(n, 0, 1)
        self.copy2(n, 1, 1, self.P.d1).start()
        self.in1(n, 3)

    def step4(self, n):
        self.in2(n, 2, 3)
        self.in2(n, 1, 3)
        for k in (3, 2, 1):
            self.copy3(n, k).start()

    def step5(self, n):
        P_ = self.P
        for k in (1, 2, 3):
            rcopy(
                self.g.at[n, 0, 0], self.r3.at[n, k - 1], self.s3s.at[n, 0], self.s3r.at[n, k - 1],
                P_.dev(P_.sib),
            ).wait_recv()
        total = self.g[n, P_.t, P_.z].astype(F32)
        for k in range(3):
            total += self.r3[n, k].astype(F32)
        return total

    def sent(self, n):
        P_ = self.P
        for q in range(4):
            self.copy1(n, q).wait_send()
        self.copy2(n, 0, 0, P_.d2).wait_send()
        self.copy2(n, 2, 2, P_.d2).wait_send()
        self.copy2(n, 1, 1, P_.d1).wait_send()
        for k in (1, 2, 3):
            self.copy3(n, k).wait_send()


def back_kernel(
    len_ref, tok, s2, n1, qkv, lse, att, gsum, gl, g_all, nt_all, pack_all,
    bnext, bown, eoi, eod, dgi, dgd, ein, edr,
    block, gtok, gqkv, gwo, gex, gdd, gde, gwi, gwe,
    gx, gt, nt, bin_, xe, er, ed, eo,
    pack_v, gq, gacc, n1t, ga_, gb_, gc_, ra1, ra2, ra3, rb1, rb2, rb3, rc1, rc2, rc3,
    gin, gdn, rin, rdn, tri, trd, *sems,
):
    P_ = Place()
    z, t = P_.z, P_.t
    own, sib, d1, d2, dd = P_.own, P_.sib, P_.d1, P_.d2, P_.dd
    others = P_.plane_others()
    zss, zsr, xs, xr, bs, lsem = sems[18:]
    sum_a = RowSum(P_, ga_, ra1, ra2, ra3, sems[0:6])
    sum_b = RowSum(P_, gb_, rb1, rb2, rb3, sems[6:12])
    sum_c = RowSum(P_, gc_, rc1, rc2, rc3, sems[12:18])
    lw = pltpu.make_async_copy(pack_all, pack_v, lsem.at[0])
    z_in = (
        pltpu.make_async_copy(dgi, gin.at[0], lsem.at[2]),
        pltpu.make_async_copy(dgd, gdn.at[0], lsem.at[7]),
    )
    own_in = (
        pltpu.make_async_copy(g_all.at[t], gt, lsem.at[5]),
        pltpu.make_async_copy(nt_all.at[t], nt, lsem.at[6]),
    )
    e_in = (
        pltpu.make_async_copy(eoi, xe, lsem.at[8]),
        pltpu.make_async_copy(ein, er, lsem.at[9]),
        pltpu.make_async_copy(eod, eo, lsem.at[10]),
        pltpu.make_async_copy(edr, ed, lsem.at[11]),
    )
    for cp in (*z_in, lw, *own_in, *e_in):
        cp.start()
    meet([P_.dev(p) for p in others] + [P_.dev(own, zz) for zz in P_.zk[1:]])
    sends = []

    def go(cp):
        cp.start()
        sends.append(cp)

    def rows(p):
        return pl.ds(pl.multiple_of(P_.rank(p) * 32, 32), 32)

    zsum = ZSum(P_, (gin, gdn), (rin, rdn), (tri, trd), zss, zsr)
    for cp in z_in:
        cp.wait()
    zsum.ship(0)
    go(rcopy(bnext, bin_, bs.at[0], bs.at[1], P_.dev(d1)))

    lw.wait()
    for cp in own_in:
        cp.wait()
    extra = pack_v[:, :, EX : EX + 128].reshape(1024, 128)
    lane = lax.broadcasted_iota(jnp.int32, (384, 128), 1)
    glv = gl[...]
    gnt = gsum[...] + glv[:, 0:1] * (row_of(extra, 0) - row_of(extra, 1))
    two = jnp.where(lane == 0, glv, jnp.where(lane == 1, -glv, 0.0)).astype(BF)
    n_two, r_two = norm_parts(s2[...])
    gain_two_row = jnp.sum(gnt * n_two, axis=0, keepdims=True)

    def norm_back(gv, gain, n, r):
        tt = gv * gain
        return r * (tt - jnp.mean(tt, -1, keepdims=True) - n * jnp.mean(tt * n, -1, keepdims=True))

    gs2 = gt[0:384].astype(F32) + norm_back(gnt, row_of(extra, 3), n_two, r_two)
    gtok[...] = gs2
    ga = gs2.astype(BF)

    def put(ref, n, cols, val):
        low = val.astype(BF)
        for zz in range(4):
            ref[n, :, zz, :, cols] = low[zz * 256 : (zz + 1) * 256].reshape(8, 32, low.shape[1])

    for j in range(2):
        cols = slice(j * 512, (j + 1) * 512)
        put(ga_, 0, cols, dot_tn(att[...], ga[:, cols]))
    sum_a.step1(0)
    for cp in e_in:
        cp.wait()
    mid = zsum.mid
    for e in range(2):
        total = xe[e].astype(F32) + er[e, 0].astype(F32) + er[e, 1].astype(F32)
        xe[e] = (total + jnp.where(mid, er[e, 2].astype(F32), 0.0)).astype(BF)
        total = eo[e].astype(F32) + ed[e, 0].astype(F32) + ed[e, 1].astype(F32)
        gde[e] = total + jnp.where(mid, ed[e, 2].astype(F32), 0.0)
    le = pltpu.make_async_copy(xe.at[:, rows(own)], gx.at[t, 1:3], lsem.at[3])
    le.start()
    for i, p in enumerate(others):
        go(rcopy(xe.at[:, rows(p)], gx.at[t, 1:3], xs.at[i], xr.at[t, 0], P_.dev(p)))
    gatt = dot_nt(ga[:, 0:512], pack_v[:, :, WO : WO + 512].reshape(1024, 512))
    gatt += dot_nt(ga[:, 512:1024], pack_v[:, :, WO + 512 : WO + 1024].reshape(1024, 512))
    gq[:, 0:1024] = gatt.astype(BF)
    n1t[...] = jnp.transpose(n1[...])
    gacc[...] = jnp.zeros_like(gacc)
    allowed = masks(len_ref[0])
    sum_a.step2(0)

    def pair_step(p, carry):
        lo = pl.ds(pl.multiple_of(p * 128, 128), 128)
        mid = pl.ds(pl.multiple_of(1024 + p * 128, 128), 128)
        hi = pl.ds(pl.multiple_of(2048 + p * 128, 128), 128)
        q2, k2, v2, do = qkv[:, lo], qkv[:, mid], qkv[:, hi], gq[:, lo]
        dq = dk = dv = None
        for hh in range(2):
            mine = lane // 64 == hh
            zero = jnp.zeros_like(q2)
            qm, km, dm = (jnp.where(mine, v, zero) for v in (q2, k2, do))
            total = jnp.sum(jnp.where(lane == 2 * p + hh, lse[...], 0.0), axis=-1, keepdims=True)
            sc = dot_nt(qm, k2) * 0.125
            pf = jnp.where(allowed, jnp.exp(sc - total), 0.0)
            gp = dot_nt(dm, v2)
            ds = (pf * (gp - jnp.sum(pf * gp, axis=-1, keepdims=True))).astype(BF)
            terms = (dot_nn(ds, km), dot_tn(ds, qm), dot_tn(pf.astype(BF), dm))
            dq, dk, dv = terms if hh == 0 else (dq + terms[0], dk + terms[1], dv + terms[2])
        gq[:, lo] = (dq * 0.125).astype(BF)
        gq[:, mid] = (dk * 0.125).astype(BF)
        gq[:, hi] = dv.astype(BF)
        return carry

    def chunk_step(j, carry):
        lax.fori_loop(2 * j, 2 * j + 2, pair_step, 0)
        for seg in range(3):
            cols = pl.ds(pl.multiple_of(seg * 1024 + j * 256, 256), 256)
            gcols = gq[:, cols]
            put(gb_, j, slice(seg * 256, (seg + 1) * 256), dot_nn(n1t[...], gcols))
            gacc[...] += dot_nt(gcols, pack_v[:, :, cols].reshape(1024, 256))
        sum_b.step1(j)

        @pl.when(j == 0)
        def _():
            zsum.transit(0)
            sum_a.step3(0)

        @pl.when(j == 1)
        def _():
            sum_a.step4(0)

        @pl.when(j >= 1)
        def _():
            sum_b.step2(j - 1)

        @pl.when(j >= 2)
        def _():
            sum_b.step3(j - 2)

        @pl.when(j >= 3)
        def _():
            sum_b.step4(j - 3)

        return carry

    lax.fori_loop(0, 4, chunk_step, 0)
    gn1 = gacc[...]
    n_one, r_one = norm_parts(tok[...].astype(F32))
    gain_one_row = jnp.sum(gn1 * n_one, axis=0, keepdims=True)
    rowi = lax.broadcasted_iota(jnp.int32, (8, 1024), 0)
    rws = jnp.where(rowi == 0, gain_one_row, jnp.where(rowi == 1, gain_two_row, 0.0)).astype(BF)
    sel = (
        lax.broadcasted_iota(jnp.int32, (8, 128), 1) == lax.broadcasted_iota(jnp.int32, (8, 128), 0) + 2
    ).astype(BF)
    put(gc_, 0, slice(0, 128), dot_tn(nt[...], two) + dot_tn(rws, sel))
    sum_c.step1(0)
    sum_b.step2(3)
    sum_b.step3(2)
    sum_c.step2(0)
    gtok[...] += norm_back(gn1, row_of(extra, 2), n_one, r_one)
    sum_b.step3(3)
    sum_b.step4(1)
    sum_c.step3(0)

    zsum.arrived(0)
    gacc[0:256, 0:512] = gin[0, z].astype(F32) + rin[0, 0].astype(F32) + rin[0, 1].astype(F32)
    gdd[...] = gdn[0, z].astype(F32) + rdn[0, 0].astype(F32) + rdn[0, 1].astype(F32)

    @pl.when(mid)
    def _():
        gacc[0:256, 0:512] += rin[0, 2].astype(F32)
        gdd[...] += rdn[0, 2].astype(F32)

    gin[0, z] = gacc[0:256, 0:512].astype(BF)
    lx = pltpu.make_async_copy(gin.at[:, z, rows(own)], gx.at[t, 0:1], lsem.at[4])
    lx.start()
    for i, p in enumerate(others):
        go(rcopy(gin.at[:, z, rows(p)], gx.at[t, 0:1], xs.at[7 + i], xr.at[t, 1], P_.dev(p)))

    sum_b.step4(2)
    sum_b.step4(3)
    sum_c.step4(0)
    rcopy(bnext, bin_, bs.at[0], bs.at[1], P_.dev(sib)).wait_recv()
    b_in = pltpu.make_async_copy(bown, nt, lsem.at[6])
    b_in.start()
    b_in.wait()
    keep = (lax.broadcasted_iota(jnp.int32, (384, 1), 0) < len_ref[0]).astype(F32)
    block[...] = ((s2[...] + (nt[...].astype(F32) + bin_[...].astype(F32))) * keep).astype(BF)
    gwo[...] = sum_a.step5(0)
    for j in range(4):
        total = sum_b.step5(j)
        for seg in range(3):
            at = seg * 1024 + j * 256
            gqkv[:, at : at + 256] = total[:, seg * 256 : (seg + 1) * 256]
    gex[...] = sum_c.step5(0)
    for p in others:
        r = P_.rank(p)
        rcopy(xe.at[:, rows(own)], gx.at[r, 1:3], xs.at[0], xr.at[r, 0], P_.dev(sib)).wait_recv()
        rcopy(gin.at[:, 0, rows(own)], gx.at[r, 0:1], xs.at[0], xr.at[r, 1], P_.dev(sib)).wait_recv()
    le.wait()
    lx.wait()
    for r in range(8):
        for zz in range(4):
            to = slice((zz * 8 + r) * 128, (zz * 8 + r + 1) * 128)
            at = slice(zz * 128, (zz + 1) * 128)
            gwi[:, to] = gx[r, 0, :, at].astype(F32)
            gwe[:, :, to] = gx[r, 1:3, :, at].astype(F32)
    zsum.sent(0)
    sum_a.sent(0)
    for j in range(4):
        sum_b.sent(j)
    sum_c.sent(0)
    for cp in sends:
        cp.wait_send()


def run_back(*args):
    sd = jax.ShapeDtypeStruct
    dma = pltpu.SemaphoreType.DMA
    sizes = ((1, 1024), (4, 768), (1, 128))
    blocks = [pltpu.VMEM((n, 8, 4, 32, w), BF) for n, w in sizes]
    for n, w in sizes:
        blocks += [
            pltpu.VMEM((n, 4, 4, 32, w), BF), pltpu.VMEM((n, 3, 4, 32, w), BF), pltpu.VMEM((n, 4, 32, w), BF),
        ]
    sems = []
    for n, _ in sizes:
        sems += [dma((n, 4)), dma((n, 4)), dma((n, 3)), dma((n, 3)), dma((n, 4)), dma((n, 4))]
    return pl.pallas_call(
        back_kernel,
        out_shape=(
            sd((384, 1024), BF), sd((384, 1024), F32), sd((32, 3072), F32), sd((32, 1024), F32),
            sd((32, 128), F32), sd((128, 1024), F32), sd((2, 128, 1024), F32), sd((32, 4096), F32),
            sd((2, 32, 4096), F32),
        ),
        in_specs=[SM] + [VM] * 8 + [ANY] * 11,
        out_specs=(VM,) * 9,
        scratch_shapes=[
            pltpu.VMEM((8, 3, 32, 512), BF), pltpu.VMEM((400, 1024), BF), pltpu.VMEM((384, 1024), BF),
            pltpu.VMEM((384, 1024), BF), pltpu.VMEM((2, 256, 512), BF), pltpu.VMEM((2, 3, 256, 512), BF),
            pltpu.VMEM((2, 3, 128, 1024), BF), pltpu.VMEM((2, 128, 1024), BF),
            pltpu.VMEM((32, 32, PW), BF), pltpu.VMEM((384, 3072), BF), pltpu.VMEM((384, 1024), F32),
            pltpu.VMEM((1024, 384), BF), *blocks,
            pltpu.VMEM((1, 4, 256, 512), BF), pltpu.VMEM((1, 4, 128, 1024), BF),
            pltpu.VMEM((1, 3, 256, 512), BF), pltpu.VMEM((1, 3, 128, 1024), BF),
            pltpu.VMEM((1, 256, 512), BF), pltpu.VMEM((1, 128, 1024), BF),
            *sems, dma((1, 8)), dma((1, 8)), dma((14,)), dma((8, 2)), dma((2,)),
            dma((12,)),
        ],
        compiler_params=pltpu.CompilerParams(
            collective_id=2, has_side_effects=True, vmem_limit_bytes=63 * MIB
        ),
    )(*args)


def leave_kernel(*refs):
    n = 8
    srcs, gex, dsts, rows = refs[:n], refs[n], refs[n + 1 : 2 * n + 1], refs[2 * n + 1]
    bufs, sin, sout = refs[2 * n + 2 : 3 * n + 2], refs[3 * n + 2], refs[3 * n + 3]
    ins = [pltpu.make_async_copy(s, v, sin.at[i]) for i, (s, v) in enumerate(zip(srcs, bufs))]
    outs = [pltpu.make_async_copy(v, d, sout.at[i]) for i, (v, d) in enumerate(zip(bufs, dsts))]
    for cp in ins:
        cp.start()
    rows[...] = jnp.transpose(jnp.concatenate([gex[...]] * 4, axis=0))[0:8]
    for a, b in zip(ins, outs):
        a.wait()
        b.start()
    for cp in outs:
        cp.wait()


def run_leave(arrays, gex):
    shapes = [jax.ShapeDtypeStruct(a.shape, a.dtype) for a in arrays]
    return pl.pallas_call(
        leave_kernel,
        out_shape=(*shapes, jax.ShapeDtypeStruct((8, 128), F32)),
        in_specs=[ANY] * 8 + [VM],
        out_specs=(ANY,) * 8 + (VM,),
        scratch_shapes=[
            *(pltpu.VMEM(a.shape, a.dtype) for a in arrays),
            pltpu.SemaphoreType.DMA((8,)), pltpu.SemaphoreType.DMA((8,)),
        ],
        compiler_params=pltpu.CompilerParams(vmem_limit_bytes=63 * MIB),
    )(*arrays, gex)


def fused_device(
    tokens, cotangent, lengths, expert_ids, slot_ids, w_qkv, w_out, gain_one, w_in, w_down,
    w_expert_in, w_expert_out, w_mix, gain_two,
):
    table = jnp.where(slot_ids >= 0, expert_ids * CAP + slot_ids, -1).astype(F32)
    lane = jnp.arange(128, dtype=jnp.int32)[None, :]
    small = jnp.zeros((32, 128), BF)
    for k, col in enumerate((w_mix[:, 0], w_mix[:, 1], gain_one, gain_two)):
        small = jnp.where(lane == k, col[:, None], small)
    qkv, lse, att, s2, n1, wmix, pack_all, wi_all, wd_all, g_all, nt_all = run_enter(
        lengths, tokens, cotangent, table.reshape(1, 384),
        w_qkv, w_out, small, w_in, w_expert_in, w_down, w_expert_out,
    )
    gsum, gl, *rest = run_ff(nt_all, wmix.reshape(1024, 128), g_all, wi_all, wd_all)
    block, gtok, gqkv, gwo, gex, gdd, gde, gwi, gwe = run_back(
        lengths, tokens, s2, n1, qkv, lse, att, gsum, gl, g_all, nt_all, pack_all, *rest
    )
    *big, rows = run_leave((block, gtok, gqkv, gwo, gwi, gdd, gwe, gde), gex)
    block, gtok, gqkv, gwo, gwi, gdd, gwe, gde = big
    return (
        block, gtok, gqkv, gwo, rows[2, 0:32], gwi, gdd, gwe, gde, rows[0:2, 0:32].T, rows[3, 0:32],
    )


def solution(mesh):
    placed = (
        P(("dp", "fsdp"), None),
        P(("dp", "fsdp"), None),
        P(("dp", "fsdp")),
        P(("dp", "fsdp")),
        P(("dp", "fsdp")),
        P(("dp", "fsdp"), None),
        P(("dp", "fsdp"), None),
        P(("dp", "fsdp")),
        P(("dp", "fsdp"), None),
        P(("dp", "fsdp"), None),
        P(None, ("dp", "fsdp"), None),
        P(None, ("dp", "fsdp"), None),
        P(("dp", "fsdp"), None),
        P(("dp", "fsdp")),
    )
    fused = (mesh.shape["dp"], mesh.shape["fsdp"]) == (8, 4)
    return jax.shard_map(
        fused_device if fused else per_device,
        mesh=mesh,
        in_specs=placed,
        out_specs=(
            P(("dp", "fsdp"), None),
            P(("dp", "fsdp"), None),
            P(("dp", "fsdp"), None),
            P(("dp", "fsdp"), None),
            P(("dp", "fsdp")),
            P(("dp", "fsdp"), None),
            P(("dp", "fsdp"), None),
            P(None, ("dp", "fsdp"), None),
            P(None, ("dp", "fsdp"), None),
            P(("dp", "fsdp"), None),
            P(("dp", "fsdp")),
        ),
        check_vma=False,
    )
```

```python
import jax
import jax.numpy as jnp
from jax import lax
from jax.experimental import pallas as pl
from jax.experimental.pallas import tpu as pltpu
from jax.sharding import PartitionSpec as P

HEAD_DIM = 64
EXPERTS = 2
CAP = 112


def layer_norm(values_in, gain_vec):
    average = jnp.mean(values_in, axis=-1, keepdims=True)
    centred = values_in - average
    variance = jnp.mean(centred * centred, axis=-1, keepdims=True)
    return centred * lax.rsqrt(variance + 1e-05) * gain_vec


def gelu_tanh(values_in):
    return jax.nn.gelu(values_in, approximate=True)


def gelu_back(values_in, grad_in):
    return jax.vjp(gelu_tanh, values_in)[1](grad_in)[0]


def head_scores(query_h, key_h, allowed, score_scale):
    scores = (
        jnp.einsum("qd,kd->qk", query_h, key_h, preferred_element_type=jnp.float32) * score_scale
    )
    return jnp.where(allowed, scores, -1e30)


def head_forward(entries, allowed, score_scale):
    query_h, key_h, value_h = entries
    scores = head_scores(query_h, key_h, allowed, score_scale)
    row_max = jnp.max(scores, axis=-1, keepdims=True)
    exp_scores = jnp.exp(scores - row_max)
    row_total = jnp.sum(exp_scores, axis=-1, keepdims=True)
    prob_low = (exp_scores / row_total).astype(jnp.bfloat16)
    head_out = jnp.dot(prob_low, value_h, preferred_element_type=jnp.float32)
    return (head_out, (row_max + jnp.log(row_total))[:, 0])


def head_backward(entries, allowed, score_scale):
    query_h, key_h, value_h, grad_head, log_total = entries
    scores = head_scores(query_h, key_h, allowed, score_scale)
    prob_full = jnp.where(allowed, jnp.exp(scores - log_total[:, None]), 0.0)
    prob_low = prob_full.astype(jnp.bfloat16)
    grad_value = jnp.einsum("qk,qd->kd", prob_low, grad_head, preferred_element_type=jnp.float32)
    grad_prob = jnp.einsum("qd,kd->qk", grad_head, value_h, preferred_element_type=jnp.float32)
    grad_score = prob_full * (grad_prob - jnp.sum(prob_full * grad_prob, axis=-1, keepdims=True))
    grad_score = grad_score.astype(jnp.bfloat16)
    grad_query = jnp.dot(grad_score, key_h, preferred_element_type=jnp.float32) * score_scale
    grad_key = (
        jnp.einsum("qk,qd->kd", grad_score, query_h, preferred_element_type=jnp.float32)
        * score_scale
    )
    return (grad_query, grad_key, grad_value)


def per_device(
    tokens,
    cotangent,
    lengths,
    expert_ids,
    slot_ids,
    w_qkv,
    w_out,
    gain_one,
    w_in,
    w_down,
    w_expert_in,
    w_expert_out,
    w_mix,
    gain_two,
):
    row_count, model_width = tokens.shape
    head_count = model_width // HEAD_DIM
    score_scale = HEAD_DIM ** (-0.5)
    full_qkv, full_out, full_gain_one = (
        lax.all_gather(w_qkv, ("dp", "fsdp"), axis=0, tiled=True),
        lax.all_gather(w_out, ("dp", "fsdp"), axis=0, tiled=True),
        lax.all_gather(gain_one, ("dp", "fsdp"), axis=0, tiled=True),
    )
    full_in, full_down, full_expert_in, full_expert_out, full_mix, full_gain_two = (
        lax.all_gather(w_in, ("dp", "fsdp"), axis=0, tiled=True),
        lax.all_gather(w_down, ("dp", "fsdp"), axis=0, tiled=True),
        lax.all_gather(w_expert_in, ("dp", "fsdp"), axis=1, tiled=True),
        lax.all_gather(w_expert_out, ("dp", "fsdp"), axis=1, tiled=True),
        lax.all_gather(w_mix, ("dp", "fsdp"), axis=0, tiled=True),
        lax.all_gather(gain_two, ("dp", "fsdp"), axis=0, tiled=True),
    )
    position = jnp.arange(row_count, dtype=jnp.int32)
    seq_len = lengths[0]
    row_keep = (position < seq_len).astype(jnp.float32)[:, None]
    allowed = (position[None, :] <= position[:, None]) & (position[None, :] < seq_len)

    def to_heads(block):
        return block.reshape(row_count, head_count, HEAD_DIM).transpose(1, 0, 2)

    def from_heads(block):
        return block.transpose(1, 0, 2).reshape(row_count, model_width)

    stream = tokens.astype(jnp.float32)
    gain_first = full_gain_one.astype(jnp.float32)
    normed_one = layer_norm(stream, gain_first).astype(jnp.bfloat16)
    qkv_all = jnp.dot(normed_one, full_qkv, preferred_element_type=jnp.float32).astype(jnp.bfloat16)
    queries = to_heads(qkv_all[:, :model_width])
    key_heads = to_heads(qkv_all[:, model_width : 2 * model_width])
    value_heads = to_heads(qkv_all[:, 2 * model_width :])
    head_out, log_total = lax.map(
        lambda entries: head_forward(entries, allowed, score_scale),
        (queries, key_heads, value_heads),
    )
    attended = from_heads(head_out).astype(jnp.bfloat16)
    stream_two = stream + jnp.dot(attended, full_out, preferred_element_type=jnp.float32)
    gain_second = full_gain_two.astype(jnp.float32)
    normed_two = layer_norm(stream_two, gain_second).astype(jnp.bfloat16)
    dense_up = jnp.dot(normed_two, full_in, preferred_element_type=jnp.float32)
    dense_act = gelu_tanh(dense_up).astype(jnp.bfloat16)
    dense_out = jnp.dot(dense_act, full_down, preferred_element_type=jnp.float32)
    routed = slot_ids >= 0
    table_row = jnp.where(routed, expert_ids * CAP + slot_ids, 0)
    slot_total = EXPERTS * CAP
    dispatch = (
        (table_row[None, :] == jnp.arange(slot_total, dtype=jnp.int32)[:, None]) & routed[None, :]
    ).astype(jnp.bfloat16)
    buffer = jnp.dot(dispatch, normed_two, preferred_element_type=jnp.float32).astype(jnp.bfloat16)
    buffer = buffer.reshape(EXPERTS, CAP, model_width)
    expert_up = jnp.einsum(
        "ecd,edf->ecf", buffer, full_expert_in, preferred_element_type=jnp.float32
    )
    expert_act = gelu_tanh(expert_up).astype(jnp.bfloat16)
    expert_y = jnp.einsum(
        "ecf,efd->ecd", expert_act, full_expert_out, preferred_element_type=jnp.float32
    )
    expert_y = expert_y.reshape(slot_total, model_width)
    expert_mix = jnp.where(routed[:, None], expert_y[table_row], 0.0)
    logits = jnp.dot(normed_two, full_mix, preferred_element_type=jnp.float32)
    mix_coeff = jax.nn.softmax(logits, axis=-1)
    branch = mix_coeff[:, 0:1] * dense_out + mix_coeff[:, 1:2] * expert_mix
    block_out = ((stream_two + branch) * row_keep).astype(jnp.bfloat16)
    grad_out = cotangent.astype(jnp.float32) * row_keep
    grad_dense = (mix_coeff[:, 0:1] * grad_out).astype(jnp.bfloat16)
    grad_expert = (mix_coeff[:, 1:2] * grad_out).astype(jnp.bfloat16)
    grad_coeff = jnp.stack(
        [jnp.sum(grad_out * dense_out, axis=-1), jnp.sum(grad_out * expert_mix, axis=-1)], axis=-1
    )
    grad_logits = jax.vjp(lambda values_in: jax.nn.softmax(values_in, axis=-1), logits)[1](
        grad_coeff
    )[0]
    full_in, full_down, full_expert_in, full_expert_out, full_mix, full_gain_two = (
        lax.all_gather(w_in, ("dp", "fsdp"), axis=0, tiled=True),
        lax.all_gather(w_down, ("dp", "fsdp"), axis=0, tiled=True),
        lax.all_gather(w_expert_in, ("dp", "fsdp"), axis=1, tiled=True),
        lax.all_gather(w_expert_out, ("dp", "fsdp"), axis=1, tiled=True),
        lax.all_gather(w_mix, ("dp", "fsdp"), axis=0, tiled=True),
        lax.all_gather(gain_two, ("dp", "fsdp"), axis=0, tiled=True),
    )
    gain_second = full_gain_two.astype(jnp.float32)
    grad_w_down = jnp.einsum("tf,td->fd", dense_act, grad_dense, preferred_element_type=jnp.float32)
    grad_dense_act = jnp.einsum(
        "td,fd->tf", grad_dense, full_down, preferred_element_type=jnp.float32
    )
    grad_dense_up = gelu_back(dense_up, grad_dense_act).astype(jnp.bfloat16)
    grad_w_in = jnp.einsum(
        "td,tf->df", normed_two, grad_dense_up, preferred_element_type=jnp.float32
    )
    grad_normed_two = jnp.einsum(
        "tf,df->td", grad_dense_up, full_in, preferred_element_type=jnp.float32
    )
    grad_y = jnp.dot(dispatch, grad_expert, preferred_element_type=jnp.float32).astype(jnp.bfloat16)
    grad_y = grad_y.reshape(EXPERTS, CAP, model_width)
    grad_expert_out_lead = jnp.einsum(
        "ecf,ecd->fed", expert_act, grad_y, preferred_element_type=jnp.float32
    )
    grad_expert_act = jnp.einsum(
        "ecd,efd->ecf", grad_y, full_expert_out, preferred_element_type=jnp.float32
    )
    grad_expert_up = gelu_back(expert_up, grad_expert_act).astype(jnp.bfloat16)
    grad_expert_in_lead = jnp.einsum(
        "ecd,ecf->def", buffer, grad_expert_up, preferred_element_type=jnp.float32
    )
    grad_buffer = jnp.einsum(
        "ecf,edf->ecd", grad_expert_up, full_expert_in, preferred_element_type=jnp.float32
    )
    grad_buffer = grad_buffer.reshape(slot_total, model_width)
    grad_normed_two = grad_normed_two + jnp.where(routed[:, None], grad_buffer[table_row], 0.0)
    mix_full = full_mix.astype(jnp.float32)
    normed_full = normed_two.astype(jnp.float32)
    grad_normed_two = grad_normed_two + jnp.dot(
        grad_logits, mix_full.T, precision=lax.Precision.HIGHEST
    )
    grad_w_mix = jnp.dot(normed_full.T, grad_logits, precision=lax.Precision.HIGHEST)
    _, pull_two = jax.vjp(layer_norm, stream_two, gain_second)
    grad_stream_ln, grad_gain_two = pull_two(grad_normed_two)
    grad_stream_two = grad_out + grad_stream_ln
    full_qkv, full_out, full_gain_one = (
        lax.all_gather(w_qkv, ("dp", "fsdp"), axis=0, tiled=True),
        lax.all_gather(w_out, ("dp", "fsdp"), axis=0, tiled=True),
        lax.all_gather(gain_one, ("dp", "fsdp"), axis=0, tiled=True),
    )
    gain_first = full_gain_one.astype(jnp.float32)
    grad_attn = grad_stream_two.astype(jnp.bfloat16)
    grad_w_out = jnp.einsum("td,te->de", attended, grad_attn, preferred_element_type=jnp.float32)
    grad_attended = jnp.einsum(
        "te,de->td", grad_attn, full_out, preferred_element_type=jnp.float32
    ).astype(jnp.bfloat16)
    grad_query, grad_key, grad_value = lax.map(
        lambda entries: head_backward(entries, allowed, score_scale),
        (queries, key_heads, value_heads, to_heads(grad_attended), log_total),
    )
    grad_qkv = jnp.concatenate(
        [from_heads(grad_query), from_heads(grad_key), from_heads(grad_value)], axis=1
    ).astype(jnp.bfloat16)
    grad_w_qkv = jnp.einsum("td,te->de", normed_one, grad_qkv, preferred_element_type=jnp.float32)
    grad_normed_one = jnp.einsum(
        "te,de->td", grad_qkv, full_qkv, preferred_element_type=jnp.float32
    )
    _, pull_one = jax.vjp(layer_norm, stream, gain_first)
    grad_stream_one, grad_gain_one = pull_one(grad_normed_one)
    grad_tokens = grad_stream_two + grad_stream_one
    (
        part_qkv,
        part_out,
        part_gain_one,
        part_in,
        part_down,
        lead_expert_in,
        lead_expert_out,
        part_mix,
        part_gain_two,
    ) = (
        lax.psum_scatter(grad_w_qkv, ("dp", "fsdp"), scatter_dimension=0, tiled=True),
        lax.psum_scatter(grad_w_out, ("dp", "fsdp"), scatter_dimension=0, tiled=True),
        lax.psum_scatter(grad_gain_one, ("dp", "fsdp"), scatter_dimension=0, tiled=True),
        lax.psum_scatter(grad_w_in, ("dp", "fsdp"), scatter_dimension=0, tiled=True),
        lax.psum_scatter(grad_w_down, ("dp", "fsdp"), scatter_dimension=0, tiled=True),
        lax.psum_scatter(grad_expert_in_lead, ("dp", "fsdp"), scatter_dimension=0, tiled=True),
        lax.psum_scatter(grad_expert_out_lead, ("dp", "fsdp"), scatter_dimension=0, tiled=True),
        lax.psum_scatter(grad_w_mix, ("dp", "fsdp"), scatter_dimension=0, tiled=True),
        lax.psum_scatter(grad_gain_two, ("dp", "fsdp"), scatter_dimension=0, tiled=True),
    )
    part_expert_in = lead_expert_in.transpose(1, 0, 2)
    part_expert_out = lead_expert_out.transpose(1, 0, 2)
    return (
        block_out,
        grad_tokens,
        part_qkv,
        part_out,
        part_gain_one,
        part_in,
        part_down,
        part_expert_in,
        part_expert_out,
        part_mix,
        part_gain_two,
    )


BF = jnp.bfloat16
F32 = jnp.float32
MESH = pl.DeviceIdType.MESH
ANY = pl.BlockSpec(memory_space=pl.ANY)
VM = pl.BlockSpec(memory_space=pltpu.VMEM)
SM = pl.BlockSpec(memory_space=pltpu.SMEM)
MIB = 1024 * 1024


def dot_nn(a, b):
    return lax.dot_general(a, b, (((1,), (0,)), ((), ())), preferred_element_type=F32)


def dot_nt(a, b):
    return lax.dot_general(a, b, (((1,), (1,)), ((), ())), preferred_element_type=F32)


def dot_tn(a, b):
    return lax.dot_general(a, b, (((0,), (0,)), ((), ())), preferred_element_type=F32)


class Place:
    def __init__(self):
        dp, fs = lax.axis_index("dp"), lax.axis_index("fsdp")
        z, y, x, c = dp // 2, dp % 2, fs // 2, fs % 2
        self.z, self.y, self.x, self.c = z, y, x, c
        self.own = (y, x, c)
        self.sib = (y, x, 1 - c)
        self.d1 = ((y + c) % 2, (x + 1 - c) % 2, c)
        self.d2 = ((y + 1 - c) % 2, (x + c) % 2, c)
        self.dd = (1 - y, 1 - x, c)
        self.zk = [z, z + 1 - 2 * (z % 2), (z + 2) % 4, 3 - z]
        self.t = self.rank(self.own)
        self.b = z * 8 + self.t

    @staticmethod
    def rank(p):
        return p[0] * 4 + p[1] * 2 + p[2]

    def flip(self, p):
        return (p[0], p[1], 1 - p[2])

    def dev(self, p, z=None):
        z = self.z if z is None else z
        return (z * 2 + p[0], p[1] * 2 + p[2])

    def plane_others(self):
        y, x, c = self.own
        return [
            ((y + k // 4) % 2, (x + (k // 2) % 2) % 2, (c + k % 2) % 2) for k in range(1, 8)
        ]


def rcopy(src, dst, send, recv, dev):
    return pltpu.make_async_remote_copy(
        src_ref=src, dst_ref=dst, send_sem=send, recv_sem=recv, device_id=dev, device_id_type=MESH
    )


def meet(devs):
    bar = pltpu.get_barrier_semaphore()
    for dev in devs:
        pl.semaphore_signal(bar, inc=1, device_id=dev, device_id_type=MESH)
    pl.semaphore_wait(bar, len(devs))


def norm_parts(v):
    mean = jnp.mean(v, axis=-1, keepdims=True)
    cen = v - mean
    var = jnp.mean(cen * cen, axis=-1, keepdims=True)
    r = lax.rsqrt(var + 1e-05)
    return cen * r, r


def row_of(extra, lane):
    pick = (lax.broadcasted_iota(jnp.int32, (8, 128), 1) == lane).astype(BF)
    return dot_nt(pick, extra)[0:1]


class ZSum:
    def __init__(self, P_, src, land, via, send, recv):
        self.P, self.src, self.land, self.via = P_, src, land, via
        self.send, self.recv = send, recv
        self.mid = (P_.z == 1) | (P_.z == 2)

    def copy(self, n, w, j):
        P_ = self.P
        to = P_.dev(P_.own, P_.zk[1 if j == 4 else j])
        block = self.src[w].at[n, P_.zk[3 if j == 4 else j]]
        dst = self.via[w].at[n] if j == 4 else self.land[w].at[n, j - 1]
        i = w * 4 + j - 1
        return rcopy(block, dst, self.send.at[n, i], self.recv.at[n, i], to)

    def ship(self, n, ws=(0, 1)):
        @pl.when(self.mid)
        def _():
            for j in (3, 1):
                for w in ws:
                    self.copy(n, w, j).start()

        @pl.when(jnp.logical_not(self.mid))
        def _():
            for j in (4, 2, 1):
                for w in ws:
                    self.copy(n, w, j).start()

    def transit(self, n, ws=(0, 1)):
        @pl.when(self.mid)
        def _():
            k2 = self.P.zk[2]
            for w in ws:
                self.copy(n, w, 4).wait_recv()
                self.src[w][n, k2] = self.src[w][n, k2] + self.via[w][n]
                self.copy(n, w, 2).start()

    def arrived(self, n, ws=(0, 1)):
        for w in ws:
            self.copy(n, w, 1).wait_recv()
            self.copy(n, w, 2).wait_recv()

        @pl.when(self.mid)
        def _():
            for w in ws:
                self.copy(n, w, 3).wait_recv()

    def sent(self, n, ws=(0, 1)):
        for w in ws:
            self.copy(n, w, 1).wait_send()
            self.copy(n, w, 2).wait_send()

        @pl.when(self.mid)
        def _():
            for w in ws:
                self.copy(n, w, 3).wait_send()

        @pl.when(jnp.logical_not(self.mid))
        def _():
            for w in ws:
                self.copy(n, w, 4).wait_send()


class ZGather:
    def __init__(self, P_, mine, full, send, recv):
        self.P, self.mine, self.full, self.send, self.recv = P_, mine, full, send, recv
        self.mid = (P_.z == 1) | (P_.z == 2)
        self.all = range(len(mine))

    def copy(self, w, j):
        P_ = self.P
        zs = P_.zk[2] if j == 4 else P_.z
        block = self.full[w](zs) if j == 4 else self.mine[w]
        to = P_.dev(P_.own, P_.zk[1 if j == 4 else j])
        return rcopy(block, self.full[w](zs), self.send.at[w * 4 + j - 1], self.recv.at[w * 4 + zs], to)

    def landed(self, w, j):
        P_ = self.P
        zs = P_.zk[j]
        rcopy(
            self.mine[w], self.full[w](zs), self.send.at[0], self.recv.at[w * 4 + zs], P_.dev(P_.sib)
        ).wait_recv()

    def ship(self):
        for w in self.all:
            self.copy(w, 2).start()

        @pl.when(self.mid)
        def _():
            for w in self.all:
                self.copy(w, 3).start()

        for w in self.all:
            self.copy(w, 1).start()

    def relay(self):
        for w in self.all:
            self.landed(w, 2)

        @pl.when(self.mid)
        def _():
            for w in self.all:
                self.copy(w, 4).start()

    def finish(self):
        for w in self.all:
            self.landed(w, 1)
            self.landed(w, 3)
            self.copy(w, 1).wait_send()
            self.copy(w, 2).wait_send()

        @pl.when(self.mid)
        def _():
            for w in self.all:
                self.copy(w, 3).wait_send()
                self.copy(w, 4).wait_send()


PW = 4224
EX = 3072
WO = 3200


def enter_kernel(
    len_ref, tok, cot, tab, w_qkv, w_out, small, w_in, w_ein, w_down, w_eout,
    qkv_o, lse_o, att_o, s2_o, n1_o, wmix_o, pack_all, wi_all, wd_all, g_all, nt_all,
    pack_v, wia, gt, qkv, lse, att, s2, nt, n1,
    pz, ps, pr, asend, arecv, fsend, frecv, gs, gr, ts, tr, lsem, osem,
):
    P_ = Place()
    z, t, b = P_.z, P_.t, P_.b
    own, sib, d1, d2, dd = P_.own, P_.sib, P_.d1, P_.d2, P_.dd
    others = P_.plane_others()
    pack = pack_v.at[b]
    pack_v[b, :, 0:3072] = w_qkv[...]
    pack_v[b, :, EX : EX + 128] = small[...]
    pack_v[b, :, WO : WO + 1024] = w_out[...]
    meet([P_.dev(p) for p in others] + [P_.dev(own, zz) for zz in P_.zk[1:]])
    sends = []
    keeps = []

    def go(cp):
        cp.start()
        sends.append(cp)

    def store(src, dst):
        cp = pltpu.make_async_copy(src, dst, osem.at[len(keeps)])
        cp.start()
        keeps.append(cp)

    def gather(n, mine, full):
        return ZGather(P_, (mine,), (full,), fsend.at[n], frecv.at[n])

    out_a = gather(0, w_eout.at[0], lambda zs: wd_all.at[1, zs])
    out_b = gather(1, w_eout.at[1], lambda zs: wd_all.at[2, zs])
    in_a = gather(2, wi_all.at[1, z], lambda zs: wi_all.at[1, zs])
    in_b = gather(3, wi_all.at[2, z], lambda zs: wi_all.at[2, zs])
    mid = in_a.mid

    def z_copy(k, s, to):
        return rcopy(pack_v.at[s], pack_v.at[s], pz.at[k - 1], pr.at[s], P_.dev(own, P_.zk[to]))

    z_copy(2, b, 2).start()

    @pl.when(mid)
    def _():
        z_copy(3, b, 3).start()

    z_copy(1, b, 1).start()
    go(rcopy(pack, pack, ps.at[3], pr.at[b], P_.dev(d1)))
    go(rcopy(pack, pack, ps.at[7], pr.at[b], P_.dev(d2)))
    go(rcopy(pack, pack, ps.at[15], pr.at[b], P_.dev(sib)))
    out_a.ship()
    for r in range(8):
        for zz in range(4):
            at = slice((zz * 8 + r) * 128, (zz * 8 + r + 1) * 128)
            to = slice(zz * 128, (zz + 1) * 128)
            wia[r, 0, :, to] = w_in[:, at]
            wia[r, 1:3, :, to] = w_ein[:, :, at]
    rows = pl.ds(pl.multiple_of(t * 32, 32), 32)
    lw = pltpu.make_async_copy(wia.at[t], wi_all.at[:, z, rows], lsem.at[1])
    lw.start()
    for i, p in enumerate(others):
        go(rcopy(wia.at[P_.rank(p)], wi_all.at[:, z, rows], asend.at[i], arecv.at[t], P_.dev(p)))
    store(w_down, wd_all.at[0, z])
    store(w_eout, wd_all.at[1:3, z])
    keep = lax.broadcasted_iota(jnp.int32, (384, 1), 0) < len_ref[0]
    gt[0:384] = jnp.where(keep, cot[...], jnp.zeros_like(cot[...]))
    gt[384:400] = jnp.zeros((16, 1024), BF)
    gt[384:385, 0:384] = tab[...].astype(BF)

    def landed(slot):
        rcopy(pack, pack_v.at[slot], ps.at[0], pr.at[slot], P_.dev(sib)).wait_recv()

    def fwd(slot, sem, p):
        go(rcopy(pack_v.at[slot], pack_v.at[slot], ps.at[sem], pr.at[slot], P_.dev(p)))

    def slot(k, p):
        return P_.zk[k] * 8 + P_.rank(p)

    for k in range(0, 6):
        if k == 2:
            out_b.ship()
        if 1 <= k <= 3:
            s = slot(k, own)
            landed(s)
            if k == 2:

                @pl.when(mid)
                def _():
                    z_copy(4, s, 1).start()

            fwd(s, 3 + k, d1)
            fwd(s, 7 + k, d2)
            fwd(s, 15 + k, sib)
        if k == 3:
            lw.wait()
            for p in others:
                rr = P_.rank(p)
                rq = pl.ds(pl.multiple_of(rr * 32, 32), 32)
                rcopy(
                    wia.at[0], wi_all.at[:, z, rq], asend.at[0], arecv.at[rr], P_.dev(sib)
                ).wait_recv()
            out_a.relay()
            in_a.ship()
        if 1 <= k <= 4:
            s = slot(k - 1, d1)
            landed(s)
            fwd(s, 11 + k - 1, d2)
            fwd(s, 19 + k - 1, sib)
            s = slot(k - 1, d2)
            landed(s)
            fwd(s, 23 + k - 1, sib)
        if k >= 2:
            s = slot(k - 2, dd)
            landed(s)
            fwd(s, 27 + k - 2, sib)
    in_b.ship()
    stream = tok[...].astype(F32)
    for k in range(4):
        for p in (own, d1, d2, dd):
            landed(slot(k, P_.flip(p)))
    store(gt, g_all.at[t])
    for i, p in enumerate((d1, d2, sib)):
        go(rcopy(gt, g_all.at[t], gs.at[i], gr.at[t], P_.dev(p)))
    store(pack_v, pack_all)
    store(pack_v.at[:, :, EX : EX + 128], wmix_o)

    extra = pack_v[:, :, EX : EX + 128].reshape(1024, 128)
    n_one, _ = norm_parts(stream)
    n1[...] = (n_one * row_of(extra, 2)).astype(BF)
    store(n1, n1_o)

    def qkv_step(j, carry):
        cols = pl.ds(pl.multiple_of(j * 512, 512), 512)
        qkv[:, cols] = dot_nn(n1[...], pack_v[:, :, cols].reshape(1024, 512)).astype(BF)
        return carry

    lax.fori_loop(0, 6, qkv_step, 0)
    store(qkv, qkv_o)

    def plane(src_own, full, send, recv):
        def landed_at(p):
            r = P_.rank(p)
            rcopy(src_own, full.at[r], send.at[0], recv.at[r], P_.dev(sib)).wait_recv()
            return r

        def pass_on(p, *dests):
            r = landed_at(p)
            for i, q in dests:
                go(rcopy(full.at[r], full.at[r], send.at[i], recv.at[r], P_.dev(q)))

        return landed_at, pass_on

    g_landed, g_pass = plane(gt, g_all, gs, gr)
    n_landed, n_pass = plane(nt, nt_all, ts, tr)

    allowed = masks(len_ref[0])
    lane = lax.broadcasted_iota(jnp.int32, (384, 128), 1)
    lse[...] = jnp.zeros_like(lse)

    def pair_step(p, carry):
        q2 = qkv[:, pl.ds(pl.multiple_of(p * 128, 128), 128)]
        k2 = qkv[:, pl.ds(pl.multiple_of(1024 + p * 128, 128), 128)]
        v2 = qkv[:, pl.ds(pl.multiple_of(2048 + p * 128, 128), 128)]
        outs = []
        for hh in range(2):
            qm = jnp.where(lane // 64 == hh, q2, jnp.zeros_like(q2))
            sc = jnp.where(allowed, dot_nt(qm, k2) * 0.125, -1e30)
            top = jnp.max(sc, axis=-1, keepdims=True)
            ex = jnp.exp(sc - top)
            tot = jnp.sum(ex, axis=-1, keepdims=True)
            outs.append(dot_nn((ex * (1.0 / tot)).astype(BF), v2))
            lse[...] = jnp.where(lane == 2 * p + hh, top + jnp.log(tot), lse[...])
        att[:, pl.ds(pl.multiple_of(p * 128, 128), 128)] = jnp.where(
            lane < 64, outs[0], outs[1]
        ).astype(BF)
        return carry

    lax.fori_loop(0, 8, pair_step, 0)
    store(lse, lse_o)
    store(att, att_o)
    for j in range(2):
        w = pack_v[:, :, WO + j * 512 : WO + (j + 1) * 512].reshape(1024, 512)
        s2[:, j * 512 : (j + 1) * 512] = stream[:, j * 512 : (j + 1) * 512] + dot_nn(att[...], w)
    store(s2, s2_o)
    n_two, _ = norm_parts(s2[...])
    nt[...] = (n_two * row_of(extra, 3)).astype(BF)
    store(nt, nt_all.at[t])
    for i, p in enumerate((d1, d2, sib)):
        go(rcopy(nt, nt_all.at[t], ts.at[i], tr.at[t], P_.dev(p)))
    out_b.relay()
    in_a.relay()
    g_pass(d1, (4, sib))
    g_pass(d2, (5, sib))
    in_b.relay()
    n_pass(d1, (4, sib))
    n_pass(d2, (5, sib))
    for p in (own, d1, d2):
        g_landed(P_.flip(p))
    for p in (own, d2, d1):
        n_landed(P_.flip(p))
    for part in (out_a, out_b, in_a, in_b):
        part.finish()
    z_copy(1, b, 1).wait_send()
    z_copy(2, b, 2).wait_send()

    @pl.when(mid)
    def _():
        z_copy(3, b, 3).wait_send()
        z_copy(4, b, 1).wait_send()

    for cp in keeps:
        cp.wait()
    for cp in sends:
        cp.wait_send()


def masks(seq_len):
    row = lax.broadcasted_iota(jnp.int32, (384, 384), 0)
    col = lax.broadcasted_iota(jnp.int32, (384, 384), 1)
    return (col <= row) & (col < seq_len)


def run_enter(*args):
    sd = jax.ShapeDtypeStruct
    dma = pltpu.SemaphoreType.DMA
    return pl.pallas_call(
        enter_kernel,
        out_shape=(
            sd((384, 3072), BF), sd((384, 128), F32), sd((384, 1024), BF), sd((384, 1024), F32),
            sd((384, 1024), BF), sd((32, 32, 128), BF),
            sd((32, 32, PW), BF), sd((3, 4, 256, 512), BF), sd((3, 4, 128, 1024), BF),
            sd((8, 400, 1024), BF), sd((8, 384, 1024), BF),
        ),
        in_specs=[SM] + [VM] * 10,
        out_specs=(ANY,) * 11,
        scratch_shapes=[
            pltpu.VMEM((32, 32, PW), BF), pltpu.VMEM((8, 3, 32, 512), BF), pltpu.VMEM((400, 1024), BF),
            pltpu.VMEM((384, 3072), BF), pltpu.VMEM((384, 128), F32), pltpu.VMEM((384, 1024), BF),
            pltpu.VMEM((384, 1024), F32), pltpu.VMEM((384, 1024), BF), pltpu.VMEM((384, 1024), BF),
            dma((4,)), dma((31,)), dma((32,)), dma((7,)), dma((8,)), dma((4, 4)), dma((4, 4)),
            dma((7,)), dma((8,)), dma((7,)), dma((8,)), dma((4,)), dma((12,)),
        ],
        compiler_params=pltpu.CompilerParams(
            collective_id=0, has_side_effects=True, vmem_limit_bytes=63 * MIB
        ),
    )(*args)


def mix_of(delta):
    return 1.0 / (1.0 + jnp.exp(-delta)), 1.0 / (1.0 + jnp.exp(delta))


def gelu_both(u):
    a, bb = 0.7978845608028654, 0.044715
    u2 = u * u
    th = jnp.tanh(a * u * (1.0 + bb * u2))
    half = 0.5 * (1.0 + th)
    return u * half, half + 0.5 * u * (1.0 - th * th) * a * (1.0 + 3.0 * bb * u2)


def ff_kernel(
    nt_hbm, wmix, g_all, wi_all, wd_all,
    gsum, gl_out, bnext, bown, eoi, eod, dgi, dgd, r1, r2, rin, rdn, dwi, dwd, gfar,
    nt_all, gbuf, br, gn, xb, yb, wi, wd, ai, ad, gin, gdn, tri, trd, tmp, gc, gcr, dots, gaps,
    ts, tr, gs, gr, gsem, wsem, dsem, zas, zar, zss, zsr, s1s, s1r, s2s, s2r, cs, cr, lsem, tsem,
):
    P_ = Place()
    z, t = P_.z, P_.t
    own, sib, d1, d2, dd = P_.own, P_.sib, P_.d1, P_.d2, P_.dd
    others = P_.plane_others()
    meet([P_.dev(p) for p in others] + [P_.dev(own, zz) for zz in P_.zk[1:]])
    sends = []

    def go(cp):
        cp.start()
        sends.append(cp)

    keeps = []

    def keep(src, dst):
        cp = pltpu.make_async_copy(src, dst, lsem.at[len(keeps)])
        cp.start()
        keeps.append(cp)

    dense = ZGather(
        P_, (wi_all.at[0, z], wd_all.at[0, z]), (lambda zs: dwi.at[zs], lambda zs: dwd.at[zs]), zas, zar
    )
    dense.ship()
    expert_load = (
        pltpu.make_async_copy(wi_all.at[1], wi.at[0], wsem.at[0, 0]),
        pltpu.make_async_copy(wd_all.at[1], wd.at[0], wsem.at[0, 1]),
        pltpu.make_async_copy(wi_all.at[2], wi.at[1], wsem.at[1, 0]),
        pltpu.make_async_copy(wd_all.at[2], wd.at[1], wsem.at[1, 1]),
    )
    for cp in expert_load:
        cp.start()

    def dense_load():
        copies = []
        for k in range(4):
            zz = P_.zk[k]
            for n, (full, far, dst) in enumerate(((wi_all, dwi, wi), (wd_all, dwd, wd))):
                src = full.at[0, z] if k == 0 else far.at[zz]
                copies.append(pltpu.make_async_copy(src, dst.at[0, zz], dsem.at[n, k]))
        return copies

    zsum = ZSum(P_, (gin, gdn), (rin, rdn), (tri, trd), zss, zsr)

    order = (own, sib, d1, P_.flip(d2), d2, P_.flip(d1), dd, P_.flip(dd))
    ranks = [P_.rank(p) for p in order]

    def seq_at(i):
        s = ranks[0]
        for k in range(1, 8):
            s = jnp.where(i == k, ranks[k], s)
        return s

    r1st, rdd = P_.rank(d1), P_.rank(dd)
    go(rcopy(nt_hbm.at[r1st], nt_all.at[r1st], ts.at[0], tr.at[r1st], P_.dev(d2)))
    go(rcopy(g_all.at[r1st], gfar.at[0], gs.at[0], gr.at[0], P_.dev(d2)))

    def far_on(start):
        cps = (
            rcopy(nt_all.at[rdd], nt_all.at[rdd], ts.at[1], tr.at[rdd], P_.dev(sib)),
            rcopy(gfar.at[0], gfar.at[1], gs.at[1], gr.at[1], P_.dev(sib)),
        )
        for cp in cps:
            if start:
                cp.start()
            else:
                cp.wait_send()

    def far_here(s, k):
        rcopy(gfar.at[0], gfar.at[k], gs.at[0], gr.at[k], P_.dev(sib)).wait_recv()
        rcopy(tmp.at[0], nt_all.at[s], ts.at[0], tr.at[s], P_.dev(sib)).wait_recv()

    class GCopy:
        def __init__(self, i):
            self.i = i

        def make(self, src):
            return pltpu.make_async_copy(src, gbuf.at[self.i % 2], gsem.at[self.i % 2])

        def start(self):
            @pl.when(self.i < 6)
            def _():
                self.make(g_all.at[seq_at(self.i)]).start()

            @pl.when(self.i >= 6)
            def _():
                self.make(gfar.at[jnp.maximum(self.i - 6, 0)]).start()

        def wait(self):
            self.make(g_all.at[0]).wait()

    def g_copy(i):
        return GCopy(i)

    def ff(xv, gv, k):
        wiv = wi[k].reshape(1024, 512)
        wdv = wd[k].reshape(512, 1024)
        act, dact = gelu_both(dot_nn(xv, wiv))
        act = act.astype(BF)
        gup = (dact * dot_nt(gv, wdv)).astype(BF)
        ad[k] += dot_tn(act, gv)
        ai[k] += dot_tn(xv, gup)
        return dot_nn(act, wdv), dot_nt(gup, wiv)

    lane = lax.broadcasted_iota(jnp.int32, (448, 128), 1)

    def shares(tab):
        slot = lax.broadcasted_iota(jnp.int32, (224, 384), 0)
        return (tab == slot.astype(F32)).astype(BF)

    def n_copy(s):
        return pltpu.make_async_copy(nt_hbm.at[s], nt_all.at[s], tr.at[s])

    for s in ranks[:6]:
        n_copy(s).start()
    g_copy(0).start()
    ai[...] = jnp.zeros_like(ai)
    ad[...] = jnp.zeros_like(ad)
    for cp in expert_load:
        cp.wait()

    def arrive(i, carry):
        s = seq_at(i)

        @pl.when(i == 5)
        def _():
            far_here(rdd, 0)
            far_on(True)

        @pl.when(i == 6)
        def _():
            far_here(P_.rank(P_.flip(dd)), 1)

        @pl.when(i + 1 < 8)
        def _():
            g_copy(i + 1).start()

        @pl.when(i < 6)
        def _():
            n_copy(s).wait()

        g_copy(i).wait()
        xv = nt_all[s]
        gv = gbuf[i % 2, :384]
        tab = gbuf[i % 2, 384:400][0:1, :384].astype(F32)
        lg = dot_nn(xv, wmix[...])
        gap = lg[:, 0:1] - lg[:, 1:2]
        gaps[i] = jnp.transpose(jnp.broadcast_to(gap, (384, 128)))[0:8]
        _, m1 = mix_of(gap)
        ge = (m1 * gv.astype(F32)).astype(BF)
        sh = shares(tab)
        xb[i] = dot_nn(sh, xv).astype(BF).reshape(2, 112, 1024)
        yb[i] = dot_nn(sh, ge).astype(BF).reshape(2, 112, 1024)
        return carry

    def expert(b, e):
        four = pl.ds(b * 4, 4)
        gq = yb[four, e].reshape(448, 1024)
        yv, gb = ff(xb[four, e].reshape(448, 1024), gq, e)
        rs = jnp.sum(gq.astype(F32) * yv, axis=-1, keepdims=True)
        high = rs.astype(BF).astype(F32)
        dots[four, e] = (
            jnp.where(lane == 0, high, jnp.where(lane == 1, rs - high, 0.0))
            .astype(BF)
            .reshape(4, 112, 128)
        )
        xb[four, e] = yv.astype(BF).reshape(4, 112, 1024)
        yb[four, e] = gb.astype(BF).reshape(4, 112, 1024)

    def stage(e):
        gin[e] = ai[e].astype(BF).reshape(4, 256, 512)
        gdn[e] = ad[e].astype(BF).reshape(4, 128, 1024)
        zsum.ship(e)
        keep(gin.at[e, z], eoi.at[e])
        keep(gdn.at[e, z], eod.at[e])

    def half(b, carry):
        lax.fori_loop(b * 4, b * 4 + 4, arrive, 0)
        @pl.when(b == 1)
        def _():
            dense.relay()

        expert(b, 0)
        expert(b, 1)
        return carry

    lax.fori_loop(0, 2, half, 0)
    stage(0)
    stage(1)
    far_on(False)
    g_copy(7).start()
    dense.finish()
    for cp in dense_load():
        cp.start()
    ai[0] = jnp.zeros_like(ai[0])
    ad[0] = jnp.zeros_like(ad[0])
    for cp in dense_load():
        cp.wait()

    chips = (dd, d1, d2, own)
    both = (gn, br)

    def give1(q, w):
        r = P_.rank(P_.flip(chips[q]))
        k = (0, 2, 1, 3)[q]
        return rcopy(both[w].at[r], r1.at[w, k], s1s.at[w, k], s1r.at[w, k], P_.dev(sib))

    def load1(q, w, start):
        cp = pltpu.make_async_copy(r1.at[w, q], tmp.at[w], tsem.at[w])
        if start:
            rcopy(tmp.at[0], r1.at[w, q], s1s.at[0, 0], s1r.at[w, q], P_.dev(sib)).wait_recv()
            cp.start()
        else:
            cp.wait()
            add_tmp(w, P_.rank(chips[q]))

    def load2(k, p, w, start):
        cp = pltpu.make_async_copy(r2.at[w, k], tmp.at[w], tsem.at[w])
        if start:
            rcopy(tmp.at[0], r2.at[w, k], s2s.at[0, 0], s2r.at[w, k], P_.dev(sib)).wait_recv()
            cp.start()
        else:
            cp.wait()
            add_tmp(w, P_.rank(p))

    def add_tmp(w, r):
        both[w][r] = both[w][r] + tmp[w]

    def give2(q, k, p, w):
        src = both[w].at[P_.rank(chips[q])]
        return rcopy(src, r2.at[w, k], s2s.at[w, k], s2r.at[w, k], P_.dev(p))

    def at_step(step, k, fn):
        @pl.when(step == k)
        def _():
            for w in range(2):
                fn(w)

    def dense_step(k, carry):
        i = 7 - k
        s = seq_at(i)

        @pl.when(i > 0)
        def _():
            g_copy(i - 1).start()

        g_copy(i).wait()
        xv = nt_all[s]
        gf = gbuf[i % 2, :384].astype(F32)
        tab = gbuf[i % 2, 384:400][0:1, :384].astype(F32)
        gap = jnp.transpose(jnp.broadcast_to(gaps[i][0:1], (128, 384)))[:, 0:1]
        m0, m1 = mix_of(gap)
        out, gxv = ff(xv, (m0 * gf).astype(BF), 0)
        at_step(k, 1, lambda w: load1(0, w, True))
        at_step(k, 3, lambda w: load1(2, w, True))
        at_step(k, 5, lambda w: load1(1, w, True))
        at_step(k, 7, lambda w: load1(3, w, True))
        col = jnp.broadcast_to(jnp.sum(gf * out, axis=-1, keepdims=True), (384, 128))
        gc[s, 0:8] = jnp.transpose(col)[0:8]
        sh = shares(tab)
        q1 = dot_tn(sh, dots[i].reshape(224, 128))
        gc[s, 8:16] = jnp.transpose(jnp.broadcast_to(q1[:, 0:1] + q1[:, 1:2], (384, 128)))[0:8]
        gn[s] = (gxv + dot_tn(sh, yb[i].reshape(224, 1024))).astype(BF)
        br[s] = (m0 * out + m1 * dot_tn(sh, xb[i].reshape(224, 1024))).astype(BF)

        for q in range(4):
            at_step(k, 2 * q, lambda w, q=q: give1(q, w).start())

        def pass_on(q, n, p):
            def fn(w):
                load1(q, w, False)
                give2(q, n, p, w).start()

            return fn

        at_step(k, 1, pass_on(0, 0, d2))
        at_step(k, 3, pass_on(2, 2, d2))
        at_step(k, 5, lambda w: load1(1, w, False))
        at_step(k, 5, lambda w: load2(0, d1, w, True))

        def turn(w):
            load2(0, d1, w, False)
            if w == 0:
                give2(1, 1, d1, w).start()

        at_step(k, 5, turn)
        at_step(k, 7, lambda w: load1(3, w, False))

        @pl.when(k == 2)
        def _():
            zsum.transit(0)

        @pl.when(k == 5)
        def _():
            zsum.transit(1)

        return carry

    lax.fori_loop(0, 8, dense_step, 0)
    for i, p in enumerate(others):
        go(rcopy(gc.at[P_.rank(p)], gcr.at[t], cs.at[i], cr.at[t], P_.dev(p)))
    keep(br.at[P_.rank(d1)], bnext)
    for w in range(2):
        load2(2, own, w, True)
    for w in range(2):
        load2(2, own, w, False)
    keep(br.at[t], bown)
    load2(1, own, 0, True)
    for p in others:
        r = P_.rank(p)
        rcopy(gc.at[0], gcr.at[r], cs.at[0], cr.at[r], P_.dev(sib)).wait_recv()
    gcr[t] = gc[t]
    tot = jnp.sum(gcr[...], axis=0)
    gc0 = jnp.transpose(jnp.broadcast_to(tot[0:1], (128, 384)))
    q1 = jnp.transpose(jnp.broadcast_to(tot[8:9], (128, 384)))
    m0, m1 = mix_of(jnp.transpose(jnp.broadcast_to(gaps[0][0:1], (128, 384))))
    gl_out[...] = m0 * (m1 * gc0 - q1)
    load2(1, own, 0, False)
    gsum[...] = gn[t].astype(F32)
    zsum.sent(0)
    for cp in keeps[0:2]:
        cp.wait()
    gin[0] = ai[0].astype(BF).reshape(4, 256, 512)
    gdn[0] = ad[0].astype(BF).reshape(4, 128, 1024)
    keep(gin.at[0], dgi)
    keep(gdn.at[0], dgd)
    for w in range(2):
        for q in range(4):
            give1(q, w).wait_send()
        give2(0, 0, d2, w).wait_send()
        give2(2, 2, d2, w).wait_send()
    give2(1, 1, d1, 0).wait_send()
    zsum.arrived(0)
    zsum.arrived(1)
    zsum.sent(1)
    for cp in keeps[2:]:
        cp.wait()
    for cp in sends:
        cp.wait_send()


def run_ff(*args):
    sd = jax.ShapeDtypeStruct
    dma = pltpu.SemaphoreType.DMA
    out = pl.pallas_call(
        ff_kernel,
        out_shape=(
            sd((384, 1024), F32), sd((384, 128), F32), sd((384, 1024), BF), sd((384, 1024), BF),
            sd((2, 256, 512), BF), sd((2, 128, 1024), BF),
            sd((4, 256, 512), BF), sd((4, 128, 1024), BF),
            sd((2, 4, 384, 1024), BF), sd((2, 3, 384, 1024), BF),
            sd((2, 3, 256, 512), BF), sd((2, 3, 128, 1024), BF),
            sd((4, 256, 512), BF), sd((4, 128, 1024), BF), sd((2, 400, 1024), BF),
        ),
        in_specs=[ANY, VM, ANY, ANY, ANY],
        out_specs=(VM,) * 2 + (ANY,) * 13,
        scratch_shapes=[
            pltpu.VMEM((8, 384, 1024), BF), pltpu.VMEM((2, 400, 1024), BF),
            pltpu.VMEM((8, 384, 1024), BF), pltpu.VMEM((8, 384, 1024), BF),
            pltpu.VMEM((8, 2, 112, 1024), BF), pltpu.VMEM((8, 2, 112, 1024), BF),
            pltpu.VMEM((2, 4, 256, 512), BF), pltpu.VMEM((2, 4, 128, 1024), BF),
            pltpu.VMEM((2, 1024, 512), F32), pltpu.VMEM((2, 512, 1024), F32),
            pltpu.VMEM((2, 4, 256, 512), BF), pltpu.VMEM((2, 4, 128, 1024), BF),
            pltpu.VMEM((2, 256, 512), BF), pltpu.VMEM((2, 128, 1024), BF),
            pltpu.VMEM((2, 384, 1024), BF),
            pltpu.VMEM((8, 16, 384), F32), pltpu.VMEM((8, 16, 384), F32), pltpu.VMEM((8, 2, 112, 128), BF),
            pltpu.VMEM((8, 8, 384), F32),
            dma((2,)), dma((8,)), dma((2,)), dma((2,)), dma((2,)), dma((2, 2)), dma((2, 4)), dma((8,)), dma((8,)),
            dma((2, 8)), dma((2, 8)),
            dma((2, 4)), dma((2, 4)), dma((2, 3)), dma((2, 3)), dma((7,)), dma((8,)), dma((10,)), dma((2,)),
        ],
        compiler_params=pltpu.CompilerParams(
            collective_id=1, has_side_effects=True, vmem_limit_bytes=63 * MIB
        ),
    )(*args)
    return (*out[:8], out[10], out[11])


class RowSum:
    swap = (0, 2, 1, 3)

    def __init__(self, P_, g, r1, r2, r3, sems):
        self.P, self.g, self.r1, self.r2, self.r3 = P_, g, r1, r2, r3
        self.s1s, self.s1r, self.s2s, self.s2r, self.s3s, self.s3r = sems
        self.chips = (P_.dd, P_.d1, P_.d2, P_.own)

    def rank(self, q):
        return self.P.rank(self.chips[q])

    def copy1(self, n, q):
        k = self.swap[q]
        src = self.g.at[n, self.P.rank(self.P.flip(self.chips[q]))]
        return rcopy(src, self.r1.at[n, k], self.s1s.at[n, k], self.s1r.at[n, k], self.P.dev(self.P.sib))

    def copy2(self, n, q, k, p):
        src = self.g.at[n, self.rank(q)]
        return rcopy(src, self.r2.at[n, k], self.s2s.at[n, k], self.s2r.at[n, k], self.P.dev(p))

    def copy3(self, n, k):
        P_ = self.P
        return rcopy(
            self.g.at[n, P_.t, P_.zk[k]], self.r3.at[n, k - 1], self.s3s.at[n, k - 1],
            self.s3r.at[n, k - 1], P_.dev(P_.own, P_.zk[k]),
        )

    def in1(self, n, q):
        rcopy(
            self.g.at[n, 0], self.r1.at[n, q], self.s1s.at[n, 0], self.s1r.at[n, q], self.P.dev(self.P.sib)
        ).wait_recv()
        r = self.rank(q)
        self.g[n, r] = self.g[n, r] + self.r1[n, q]

    def in2(self, n, k, q):
        rcopy(
            self.g.at[n, 0], self.r2.at[n, k], self.s2s.at[n, 0], self.s2r.at[n, k], self.P.dev(self.P.sib)
        ).wait_recv()
        r = self.rank(q)
        self.g[n, r] = self.g[n, r] + self.r2[n, k]

    def step1(self, n):
        for q in (0, 1, 2, 3):
            self.copy1(n, q).start()

    def step2(self, n):
        P_ = self.P
        self.in1(n, 0)
        self.copy2(n, 0, 0, P_.d2).start()
        self.in1(n, 2)
        self.copy2(n, 2, 2, P_.d2).start()
        self.in1(n, 1)

    def step3(self, n):
        self.in2(n, 0, 1)
        self.copy2(n, 1, 1, self.P.d1).start()
        self.in1(n, 3)

    def step4(self, n):
        self.in2(n, 2, 3)
        self.in2(n, 1, 3)
        for k in (3, 2, 1):
            self.copy3(n, k).start()

    def step5(self, n):
        P_ = self.P
        for k in (1, 2, 3):
            rcopy(
                self.g.at[n, 0, 0], self.r3.at[n, k - 1], self.s3s.at[n, 0], self.s3r.at[n, k - 1],
                P_.dev(P_.sib),
            ).wait_recv()
        total = self.g[n, P_.t, P_.z].astype(F32)
        for k in range(3):
            total += self.r3[n, k].astype(F32)
        return total

    def sent(self, n):
        P_ = self.P
        for q in range(4):
            self.copy1(n, q).wait_send()
        self.copy2(n, 0, 0, P_.d2).wait_send()
        self.copy2(n, 2, 2, P_.d2).wait_send()
        self.copy2(n, 1, 1, P_.d1).wait_send()
        for k in (1, 2, 3):
            self.copy3(n, k).wait_send()


def back_kernel(
    len_ref, tok, s2, n1, qkv, lse, att, gsum, gl, g_all, nt_all, pack_all,
    bnext, bown, eoi, eod, dgi, dgd, ein, edr,
    block, gtok, gqkv, gwo, gex, gdd, gde, gwi, gwe,
    gx, gt, nt, bin_, xe, er, ed, eo,
    pack_v, gq, gacc, n1t, ga_, gb_, gc_, ra1, ra2, ra3, rb1, rb2, rb3, rc1, rc2, rc3,
    gin, gdn, rin, rdn, tri, trd, *sems,
):
    P_ = Place()
    z, t = P_.z, P_.t
    own, sib, d1, d2, dd = P_.own, P_.sib, P_.d1, P_.d2, P_.dd
    others = P_.plane_others()
    zss, zsr, xs, xr, bs, lsem = sems[18:]
    sum_a = RowSum(P_, ga_, ra1, ra2, ra3, sems[0:6])
    sum_b = RowSum(P_, gb_, rb1, rb2, rb3, sems[6:12])
    sum_c = RowSum(P_, gc_, rc1, rc2, rc3, sems[12:18])
    lw = pltpu.make_async_copy(pack_all, pack_v, lsem.at[0])
    z_in = (
        pltpu.make_async_copy(dgi, gin.at[0], lsem.at[2]),
        pltpu.make_async_copy(dgd, gdn.at[0], lsem.at[7]),
    )
    own_in = (
        pltpu.make_async_copy(g_all.at[t], gt, lsem.at[5]),
        pltpu.make_async_copy(nt_all.at[t], nt, lsem.at[6]),
    )
    e_in = (
        pltpu.make_async_copy(eoi, xe, lsem.at[8]),
        pltpu.make_async_copy(ein, er, lsem.at[9]),
        pltpu.make_async_copy(eod, eo, lsem.at[10]),
        pltpu.make_async_copy(edr, ed, lsem.at[11]),
    )
    for cp in (*z_in, lw, *own_in, *e_in):
        cp.start()
    meet([P_.dev(p) for p in others] + [P_.dev(own, zz) for zz in P_.zk[1:]])
    sends = []

    def go(cp):
        cp.start()
        sends.append(cp)

    def rows(p):
        return pl.ds(pl.multiple_of(P_.rank(p) * 32, 32), 32)

    zsum = ZSum(P_, (gin, gdn), (rin, rdn), (tri, trd), zss, zsr)
    for cp in z_in:
        cp.wait()
    zsum.ship(0)
    go(rcopy(bnext, bin_, bs.at[0], bs.at[1], P_.dev(d1)))

    lw.wait()
    for cp in own_in:
        cp.wait()
    extra = pack_v[:, :, EX : EX + 128].reshape(1024, 128)
    lane = lax.broadcasted_iota(jnp.int32, (384, 128), 1)
    glv = gl[...]
    gnt = gsum[...] + glv[:, 0:1] * (row_of(extra, 0) - row_of(extra, 1))
    two = jnp.where(lane == 0, glv, jnp.where(lane == 1, -glv, 0.0)).astype(BF)
    n_two, r_two = norm_parts(s2[...])
    gain_two_row = jnp.sum(gnt * n_two, axis=0, keepdims=True)

    def norm_back(gv, gain, n, r):
        tt = gv * gain
        return r * (tt - jnp.mean(tt, -1, keepdims=True) - n * jnp.mean(tt * n, -1, keepdims=True))

    gs2 = gt[0:384].astype(F32) + norm_back(gnt, row_of(extra, 3), n_two, r_two)
    gtok[...] = gs2
    ga = gs2.astype(BF)

    def put(ref, n, cols, val):
        low = val.astype(BF)
        for zz in range(4):
            ref[n, :, zz, :, cols] = low[zz * 256 : (zz + 1) * 256].reshape(8, 32, low.shape[1])

    for j in range(2):
        cols = slice(j * 512, (j + 1) * 512)
        put(ga_, 0, cols, dot_tn(att[...], ga[:, cols]))
    sum_a.step1(0)
    for cp in e_in:
        cp.wait()
    mid = zsum.mid
    for e in range(2):
        total = xe[e].astype(F32) + er[e, 0].astype(F32) + er[e, 1].astype(F32)
        xe[e] = (total + jnp.where(mid, er[e, 2].astype(F32), 0.0)).astype(BF)
        total = eo[e].astype(F32) + ed[e, 0].astype(F32) + ed[e, 1].astype(F32)
        gde[e] = total + jnp.where(mid, ed[e, 2].astype(F32), 0.0)
    le = pltpu.make_async_copy(xe.at[:, rows(own)], gx.at[t, 1:3], lsem.at[3])
    le.start()
    for i, p in enumerate(others):
        go(rcopy(xe.at[:, rows(p)], gx.at[t, 1:3], xs.at[i], xr.at[t, 0], P_.dev(p)))
    gatt = dot_nt(ga[:, 0:512], pack_v[:, :, WO : WO + 512].reshape(1024, 512))
    gatt += dot_nt(ga[:, 512:1024], pack_v[:, :, WO + 512 : WO + 1024].reshape(1024, 512))
    gq[:, 0:1024] = gatt.astype(BF)
    n1t[...] = jnp.transpose(n1[...])
    gacc[...] = jnp.zeros_like(gacc)
    allowed = masks(len_ref[0])
    sum_a.step2(0)

    def pair_step(p, carry):
        lo = pl.ds(pl.multiple_of(p * 128, 128), 128)
        mid = pl.ds(pl.multiple_of(1024 + p * 128, 128), 128)
        hi = pl.ds(pl.multiple_of(2048 + p * 128, 128), 128)
        q2, k2, v2, do = qkv[:, lo], qkv[:, mid], qkv[:, hi], gq[:, lo]
        dq = dk = dv = None
        for hh in range(2):
            mine = lane // 64 == hh
            zero = jnp.zeros_like(q2)
            qm, km, dm = (jnp.where(mine, v, zero) for v in (q2, k2, do))
            total = jnp.sum(jnp.where(lane == 2 * p + hh, lse[...], 0.0), axis=-1, keepdims=True)
            sc = dot_nt(qm, k2) * 0.125
            pf = jnp.where(allowed, jnp.exp(sc - total), 0.0)
            gp = dot_nt(dm, v2)
            ds = (pf * (gp - jnp.sum(pf * gp, axis=-1, keepdims=True))).astype(BF)
            terms = (dot_nn(ds, km), dot_tn(ds, qm), dot_tn(pf.astype(BF), dm))
            dq, dk, dv = terms if hh == 0 else (dq + terms[0], dk + terms[1], dv + terms[2])
        gq[:, lo] = (dq * 0.125).astype(BF)
        gq[:, mid] = (dk * 0.125).astype(BF)
        gq[:, hi] = dv.astype(BF)
        return carry

    def chunk_step(j, carry):
        lax.fori_loop(2 * j, 2 * j + 2, pair_step, 0)
        for seg in range(3):
            cols = pl.ds(pl.multiple_of(seg * 1024 + j * 256, 256), 256)
            gcols = gq[:, cols]
            put(gb_, j, slice(seg * 256, (seg + 1) * 256), dot_nn(n1t[...], gcols))
            gacc[...] += dot_nt(gcols, pack_v[:, :, cols].reshape(1024, 256))
        sum_b.step1(j)

        @pl.when(j == 0)
        def _():
            zsum.transit(0)
            sum_a.step3(0)

        @pl.when(j == 1)
        def _():
            sum_a.step4(0)

        @pl.when(j >= 1)
        def _():
            sum_b.step2(j - 1)

        @pl.when(j >= 2)
        def _():
            sum_b.step3(j - 2)

        @pl.when(j >= 3)
        def _():
            sum_b.step4(j - 3)

        return carry

    lax.fori_loop(0, 4, chunk_step, 0)
    gn1 = gacc[...]
    n_one, r_one = norm_parts(tok[...].astype(F32))
    gain_one_row = jnp.sum(gn1 * n_one, axis=0, keepdims=True)
    rowi = lax.broadcasted_iota(jnp.int32, (8, 1024), 0)
    rws = jnp.where(rowi == 0, gain_one_row, jnp.where(rowi == 1, gain_two_row, 0.0)).astype(BF)
    sel = (
        lax.broadcasted_iota(jnp.int32, (8, 128), 1) == lax.broadcasted_iota(jnp.int32, (8, 128), 0) + 2
    ).astype(BF)
    put(gc_, 0, slice(0, 128), dot_tn(nt[...], two) + dot_tn(rws, sel))
    sum_c.step1(0)
    sum_b.step2(3)
    sum_b.step3(2)
    sum_c.step2(0)
    gtok[...] += norm_back(gn1, row_of(extra, 2), n_one, r_one)
    sum_b.step3(3)
    sum_b.step4(1)
    sum_c.step3(0)

    zsum.arrived(0)
    gacc[0:256, 0:512] = gin[0, z].astype(F32) + rin[0, 0].astype(F32) + rin[0, 1].astype(F32)
    gdd[...] = gdn[0, z].astype(F32) + rdn[0, 0].astype(F32) + rdn[0, 1].astype(F32)

    @pl.when(mid)
    def _():
        gacc[0:256, 0:512] += rin[0, 2].astype(F32)
        gdd[...] += rdn[0, 2].astype(F32)

    gin[0, z] = gacc[0:256, 0:512].astype(BF)
    lx = pltpu.make_async_copy(gin.at[:, z, rows(own)], gx.at[t, 0:1], lsem.at[4])
    lx.start()
    for i, p in enumerate(others):
        go(rcopy(gin.at[:, z, rows(p)], gx.at[t, 0:1], xs.at[7 + i], xr.at[t, 1], P_.dev(p)))

    sum_b.step4(2)
    sum_b.step4(3)
    sum_c.step4(0)
    rcopy(bnext, bin_, bs.at[0], bs.at[1], P_.dev(sib)).wait_recv()
    b_in = pltpu.make_async_copy(bown, nt, lsem.at[6])
    b_in.start()
    b_in.wait()
    keep = (lax.broadcasted_iota(jnp.int32, (384, 1), 0) < len_ref[0]).astype(F32)
    block[...] = ((s2[...] + (nt[...].astype(F32) + bin_[...].astype(F32))) * keep).astype(BF)
    gwo[...] = sum_a.step5(0)
    for j in range(4):
        total = sum_b.step5(j)
        for seg in range(3):
            at = seg * 1024 + j * 256
            gqkv[:, at : at + 256] = total[:, seg * 256 : (seg + 1) * 256]
    gex[...] = sum_c.step5(0)
    for p in others:
        r = P_.rank(p)
        rcopy(xe.at[:, rows(own)], gx.at[r, 1:3], xs.at[0], xr.at[r, 0], P_.dev(sib)).wait_recv()
        rcopy(gin.at[:, 0, rows(own)], gx.at[r, 0:1], xs.at[0], xr.at[r, 1], P_.dev(sib)).wait_recv()
    le.wait()
    lx.wait()
    for r in range(8):
        for zz in range(4):
            to = slice((zz * 8 + r) * 128, (zz * 8 + r + 1) * 128)
            at = slice(zz * 128, (zz + 1) * 128)
            gwi[:, to] = gx[r, 0, :, at].astype(F32)
            gwe[:, :, to] = gx[r, 1:3, :, at].astype(F32)
    zsum.sent(0)
    sum_a.sent(0)
    for j in range(4):
        sum_b.sent(j)
    sum_c.sent(0)
    for cp in sends:
        cp.wait_send()


def run_back(*args):
    sd = jax.ShapeDtypeStruct
    dma = pltpu.SemaphoreType.DMA
    sizes = ((1, 1024), (4, 768), (1, 128))
    blocks = [pltpu.VMEM((n, 8, 4, 32, w), BF) for n, w in sizes]
    for n, w in sizes:
        blocks += [
            pltpu.VMEM((n, 4, 4, 32, w), BF), pltpu.VMEM((n, 3, 4, 32, w), BF), pltpu.VMEM((n, 4, 32, w), BF),
        ]
    sems = []
    for n, _ in sizes:
        sems += [dma((n, 4)), dma((n, 4)), dma((n, 3)), dma((n, 3)), dma((n, 4)), dma((n, 4))]
    return pl.pallas_call(
        back_kernel,
        out_shape=(
            sd((384, 1024), BF), sd((384, 1024), F32), sd((32, 3072), F32), sd((32, 1024), F32),
            sd((32, 128), F32), sd((128, 1024), F32), sd((2, 128, 1024), F32), sd((32, 4096), F32),
            sd((2, 32, 4096), F32),
        ),
        in_specs=[SM] + [VM] * 8 + [ANY] * 11,
        out_specs=(VM,) * 9,
        scratch_shapes=[
            pltpu.VMEM((8, 3, 32, 512), BF), pltpu.VMEM((400, 1024), BF), pltpu.VMEM((384, 1024), BF),
            pltpu.VMEM((384, 1024), BF), pltpu.VMEM((2, 256, 512), BF), pltpu.VMEM((2, 3, 256, 512), BF),
            pltpu.VMEM((2, 3, 128, 1024), BF), pltpu.VMEM((2, 128, 1024), BF),
            pltpu.VMEM((32, 32, PW), BF), pltpu.VMEM((384, 3072), BF), pltpu.VMEM((384, 1024), F32),
            pltpu.VMEM((1024, 384), BF), *blocks,
            pltpu.VMEM((1, 4, 256, 512), BF), pltpu.VMEM((1, 4, 128, 1024), BF),
            pltpu.VMEM((1, 3, 256, 512), BF), pltpu.VMEM((1, 3, 128, 1024), BF),
            pltpu.VMEM((1, 256, 512), BF), pltpu.VMEM((1, 128, 1024), BF),
            *sems, dma((1, 8)), dma((1, 8)), dma((14,)), dma((8, 2)), dma((2,)),
            dma((12,)),
        ],
        compiler_params=pltpu.CompilerParams(
            collective_id=2, has_side_effects=True, vmem_limit_bytes=63 * MIB
        ),
    )(*args)


def leave_kernel(*refs):
    n = 8
    srcs, gex, dsts, rows = refs[:n], refs[n], refs[n + 1 : 2 * n + 1], refs[2 * n + 1]
    bufs, sin, sout = refs[2 * n + 2 : 3 * n + 2], refs[3 * n + 2], refs[3 * n + 3]
    ins = [pltpu.make_async_copy(s, v, sin.at[i]) for i, (s, v) in enumerate(zip(srcs, bufs))]
    outs = [pltpu.make_async_copy(v, d, sout.at[i]) for i, (v, d) in enumerate(zip(bufs, dsts))]
    for cp in ins:
        cp.start()
    rows[...] = jnp.transpose(jnp.concatenate([gex[...]] * 4, axis=0))[0:8]
    for a, b in zip(ins, outs):
        a.wait()
        b.start()
    for cp in outs:
        cp.wait()


def run_leave(arrays, gex):
    shapes = [jax.ShapeDtypeStruct(a.shape, a.dtype) for a in arrays]
    return pl.pallas_call(
        leave_kernel,
        out_shape=(*shapes, jax.ShapeDtypeStruct((8, 128), F32)),
        in_specs=[ANY] * 8 + [VM],
        out_specs=(ANY,) * 8 + (VM,),
        scratch_shapes=[
            *(pltpu.VMEM(a.shape, a.dtype) for a in arrays),
            pltpu.SemaphoreType.DMA((8,)), pltpu.SemaphoreType.DMA((8,)),
        ],
        compiler_params=pltpu.CompilerParams(vmem_limit_bytes=63 * MIB),
    )(*arrays, gex)


def fused_device(
    tokens, cotangent, lengths, expert_ids, slot_ids, w_qkv, w_out, gain_one, w_in, w_down,
    w_expert_in, w_expert_out, w_mix, gain_two,
):
    table = jnp.where(slot_ids >= 0, expert_ids * CAP + slot_ids, -1).astype(F32)
    lane = jnp.arange(128, dtype=jnp.int32)[None, :]
    small = jnp.zeros((32, 128), BF)
    for k, col in enumerate((w_mix[:, 0], w_mix[:, 1], gain_one, gain_two)):
        small = jnp.where(lane == k, col[:, None], small)
    qkv, lse, att, s2, n1, wmix, pack_all, wi_all, wd_all, g_all, nt_all = run_enter(
        lengths, tokens, cotangent, table.reshape(1, 384),
        w_qkv, w_out, small, w_in, w_expert_in, w_down, w_expert_out,
    )
    gsum, gl, *rest = run_ff(nt_all, wmix.reshape(1024, 128), g_all, wi_all, wd_all)
    block, gtok, gqkv, gwo, gex, gdd, gde, gwi, gwe = run_back(
        lengths, tokens, s2, n1, qkv, lse, att, gsum, gl, g_all, nt_all, pack_all, *rest
    )
    *big, rows = run_leave((block, gtok, gqkv, gwo, gwi, gdd, gwe, gde), gex)
    block, gtok, gqkv, gwo, gwi, gdd, gwe, gde = big
    return (
        block, gtok, gqkv, gwo, rows[2, 0:32], gwi, gdd, gwe, gde, rows[0:2, 0:32].T, rows[3, 0:32],
    )


def solution(mesh):
    placed = (
        P(("dp", "fsdp"), None),
        P(("dp", "fsdp"), None),
        P(("dp", "fsdp")),
        P(("dp", "fsdp")),
        P(("dp", "fsdp")),
        P(("dp", "fsdp"), None),
        P(("dp", "fsdp"), None),
        P(("dp", "fsdp")),
        P(("dp", "fsdp"), None),
        P(("dp", "fsdp"), None),
        P(None, ("dp", "fsdp"), None),
        P(None, ("dp", "fsdp"), None),
        P(("dp", "fsdp"), None),
        P(("dp", "fsdp")),
    )
    fused = (mesh.shape["dp"], mesh.shape["fsdp"]) == (8, 4)
    return jax.shard_map(
        fused_device if fused else per_device,
        mesh=mesh,
        in_specs=placed,
        out_specs=(
            P(("dp", "fsdp"), None),
            P(("dp", "fsdp"), None),
            P(("dp", "fsdp"), None),
            P(("dp", "fsdp"), None),
            P(("dp", "fsdp")),
            P(("dp", "fsdp"), None),
            P(("dp", "fsdp"), None),
            P(None, ("dp", "fsdp"), None),
            P(None, ("dp", "fsdp"), None),
            P(("dp", "fsdp"), None),
            P(("dp", "fsdp")),
        ),
        check_vma=False,
    )
```

```python
import jax
import jax.numpy as jnp
from jax import lax
from jax.experimental import pallas as pl
from jax.experimental.pallas import tpu as pltpu
from jax.sharding import PartitionSpec as P

HEAD_DIM = 64
EXPERTS = 2
CAP = 112


def layer_norm(values_in, gain_vec):
    average = jnp.mean(values_in, axis=-1, keepdims=True)
    centred = values_in - average
    variance = jnp.mean(centred * centred, axis=-1, keepdims=True)
    return centred * lax.rsqrt(variance + 1e-05) * gain_vec


def gelu_tanh(values_in):
    return jax.nn.gelu(values_in, approximate=True)


def gelu_back(values_in, grad_in):
    return jax.vjp(gelu_tanh, values_in)[1](grad_in)[0]


def head_scores(query_h, key_h, allowed, score_scale):
    scores = (
        jnp.einsum("qd,kd->qk", query_h, key_h, preferred_element_type=jnp.float32) * score_scale
    )
    return jnp.where(allowed, scores, -1e30)


def head_forward(entries, allowed, score_scale):
    query_h, key_h, value_h = entries
    scores = head_scores(query_h, key_h, allowed, score_scale)
    row_max = jnp.max(scores, axis=-1, keepdims=True)
    exp_scores = jnp.exp(scores - row_max)
    row_total = jnp.sum(exp_scores, axis=-1, keepdims=True)
    prob_low = (exp_scores / row_total).astype(jnp.bfloat16)
    head_out = jnp.dot(prob_low, value_h, preferred_element_type=jnp.float32)
    return (head_out, (row_max + jnp.log(row_total))[:, 0])


def head_backward(entries, allowed, score_scale):
    query_h, key_h, value_h, grad_head, log_total = entries
    scores = head_scores(query_h, key_h, allowed, score_scale)
    prob_full = jnp.where(allowed, jnp.exp(scores - log_total[:, None]), 0.0)
    prob_low = prob_full.astype(jnp.bfloat16)
    grad_value = jnp.einsum("qk,qd->kd", prob_low, grad_head, preferred_element_type=jnp.float32)
    grad_prob = jnp.einsum("qd,kd->qk", grad_head, value_h, preferred_element_type=jnp.float32)
    grad_score = prob_full * (grad_prob - jnp.sum(prob_full * grad_prob, axis=-1, keepdims=True))
    grad_score = grad_score.astype(jnp.bfloat16)
    grad_query = jnp.dot(grad_score, key_h, preferred_element_type=jnp.float32) * score_scale
    grad_key = (
        jnp.einsum("qk,qd->kd", grad_score, query_h, preferred_element_type=jnp.float32)
        * score_scale
    )
    return (grad_query, grad_key, grad_value)


def per_device(
    tokens,
    cotangent,
    lengths,
    expert_ids,
    slot_ids,
    w_qkv,
    w_out,
    gain_one,
    w_in,
    w_down,
    w_expert_in,
    w_expert_out,
    w_mix,
    gain_two,
):
    row_count, model_width = tokens.shape
    head_count = model_width // HEAD_DIM
    score_scale = HEAD_DIM ** (-0.5)
    full_qkv, full_out, full_gain_one = (
        lax.all_gather(w_qkv, ("dp", "fsdp"), axis=0, tiled=True),
        lax.all_gather(w_out, ("dp", "fsdp"), axis=0, tiled=True),
        lax.all_gather(gain_one, ("dp", "fsdp"), axis=0, tiled=True),
    )
    full_in, full_down, full_expert_in, full_expert_out, full_mix, full_gain_two = (
        lax.all_gather(w_in, ("dp", "fsdp"), axis=0, tiled=True),
        lax.all_gather(w_down, ("dp", "fsdp"), axis=0, tiled=True),
        lax.all_gather(w_expert_in, ("dp", "fsdp"), axis=1, tiled=True),
        lax.all_gather(w_expert_out, ("dp", "fsdp"), axis=1, tiled=True),
        lax.all_gather(w_mix, ("dp", "fsdp"), axis=0, tiled=True),
        lax.all_gather(gain_two, ("dp", "fsdp"), axis=0, tiled=True),
    )
    position = jnp.arange(row_count, dtype=jnp.int32)
    seq_len = lengths[0]
    row_keep = (position < seq_len).astype(jnp.float32)[:, None]
    allowed = (position[None, :] <= position[:, None]) & (position[None, :] < seq_len)

    def to_heads(block):
        return block.reshape(row_count, head_count, HEAD_DIM).transpose(1, 0, 2)

    def from_heads(block):
        return block.transpose(1, 0, 2).reshape(row_count, model_width)

    stream = tokens.astype(jnp.float32)
    gain_first = full_gain_one.astype(jnp.float32)
    normed_one = layer_norm(stream, gain_first).astype(jnp.bfloat16)
    qkv_all = jnp.dot(normed_one, full_qkv, preferred_element_type=jnp.float32).astype(jnp.bfloat16)
    queries = to_heads(qkv_all[:, :model_width])
    key_heads = to_heads(qkv_all[:, model_width : 2 * model_width])
    value_heads = to_heads(qkv_all[:, 2 * model_width :])
    head_out, log_total = lax.map(
        lambda entries: head_forward(entries, allowed, score_scale),
        (queries, key_heads, value_heads),
    )
    attended = from_heads(head_out).astype(jnp.bfloat16)
    stream_two = stream + jnp.dot(attended, full_out, preferred_element_type=jnp.float32)
    gain_second = full_gain_two.astype(jnp.float32)
    normed_two = layer_norm(stream_two, gain_second).astype(jnp.bfloat16)
    dense_up = jnp.dot(normed_two, full_in, preferred_element_type=jnp.float32)
    dense_act = gelu_tanh(dense_up).astype(jnp.bfloat16)
    dense_out = jnp.dot(dense_act, full_down, preferred_element_type=jnp.float32)
    routed = slot_ids >= 0
    table_row = jnp.where(routed, expert_ids * CAP + slot_ids, 0)
    slot_total = EXPERTS * CAP
    dispatch = (
        (table_row[None, :] == jnp.arange(slot_total, dtype=jnp.int32)[:, None]) & routed[None, :]
    ).astype(jnp.bfloat16)
    buffer = jnp.dot(dispatch, normed_two, preferred_element_type=jnp.float32).astype(jnp.bfloat16)
    buffer = buffer.reshape(EXPERTS, CAP, model_width)
    expert_up = jnp.einsum(
        "ecd,edf->ecf", buffer, full_expert_in, preferred_element_type=jnp.float32
    )
    expert_act = gelu_tanh(expert_up).astype(jnp.bfloat16)
    expert_y = jnp.einsum(
        "ecf,efd->ecd", expert_act, full_expert_out, preferred_element_type=jnp.float32
    )
    expert_y = expert_y.reshape(slot_total, model_width)
    expert_mix = jnp.where(routed[:, None], expert_y[table_row], 0.0)
    logits = jnp.dot(normed_two, full_mix, preferred_element_type=jnp.float32)
    mix_coeff = jax.nn.softmax(logits, axis=-1)
    branch = mix_coeff[:, 0:1] * dense_out + mix_coeff[:, 1:2] * expert_mix
    block_out = ((stream_two + branch) * row_keep).astype(jnp.bfloat16)
    grad_out = cotangent.astype(jnp.float32) * row_keep
    grad_dense = (mix_coeff[:, 0:1] * grad_out).astype(jnp.bfloat16)
    grad_expert = (mix_coeff[:, 1:2] * grad_out).astype(jnp.bfloat16)
    grad_coeff = jnp.stack(
        [jnp.sum(grad_out * dense_out, axis=-1), jnp.sum(grad_out * expert_mix, axis=-1)], axis=-1
    )
    grad_logits = jax.vjp(lambda values_in: jax.nn.softmax(values_in, axis=-1), logits)[1](
        grad_coeff
    )[0]
    full_in, full_down, full_expert_in, full_expert_out, full_mix, full_gain_two = (
        lax.all_gather(w_in, ("dp", "fsdp"), axis=0, tiled=True),
        lax.all_gather(w_down, ("dp", "fsdp"), axis=0, tiled=True),
        lax.all_gather(w_expert_in, ("dp", "fsdp"), axis=1, tiled=True),
        lax.all_gather(w_expert_out, ("dp", "fsdp"), axis=1, tiled=True),
        lax.all_gather(w_mix, ("dp", "fsdp"), axis=0, tiled=True),
        lax.all_gather(gain_two, ("dp", "fsdp"), axis=0, tiled=True),
    )
    gain_second = full_gain_two.astype(jnp.float32)
    grad_w_down = jnp.einsum("tf,td->fd", dense_act, grad_dense, preferred_element_type=jnp.float32)
    grad_dense_act = jnp.einsum(
        "td,fd->tf", grad_dense, full_down, preferred_element_type=jnp.float32
    )
    grad_dense_up = gelu_back(dense_up, grad_dense_act).astype(jnp.bfloat16)
    grad_w_in = jnp.einsum(
        "td,tf->df", normed_two, grad_dense_up, preferred_element_type=jnp.float32
    )
    grad_normed_two = jnp.einsum(
        "tf,df->td", grad_dense_up, full_in, preferred_element_type=jnp.float32
    )
    grad_y = jnp.dot(dispatch, grad_expert, preferred_element_type=jnp.float32).astype(jnp.bfloat16)
    grad_y = grad_y.reshape(EXPERTS, CAP, model_width)
    grad_expert_out_lead = jnp.einsum(
        "ecf,ecd->fed", expert_act, grad_y, preferred_element_type=jnp.float32
    )
    grad_expert_act = jnp.einsum(
        "ecd,efd->ecf", grad_y, full_expert_out, preferred_element_type=jnp.float32
    )
    grad_expert_up = gelu_back(expert_up, grad_expert_act).astype(jnp.bfloat16)
    grad_expert_in_lead = jnp.einsum(
        "ecd,ecf->def", buffer, grad_expert_up, preferred_element_type=jnp.float32
    )
    grad_buffer = jnp.einsum(
        "ecf,edf->ecd", grad_expert_up, full_expert_in, preferred_element_type=jnp.float32
    )
    grad_buffer = grad_buffer.reshape(slot_total, model_width)
    grad_normed_two = grad_normed_two + jnp.where(routed[:, None], grad_buffer[table_row], 0.0)
    mix_full = full_mix.astype(jnp.float32)
    normed_full = normed_two.astype(jnp.float32)
    grad_normed_two = grad_normed_two + jnp.dot(
        grad_logits, mix_full.T, precision=lax.Precision.HIGHEST
    )
    grad_w_mix = jnp.dot(normed_full.T, grad_logits, precision=lax.Precision.HIGHEST)
    _, pull_two = jax.vjp(layer_norm, stream_two, gain_second)
    grad_stream_ln, grad_gain_two = pull_two(grad_normed_two)
    grad_stream_two = grad_out + grad_stream_ln
    full_qkv, full_out, full_gain_one = (
        lax.all_gather(w_qkv, ("dp", "fsdp"), axis=0, tiled=True),
        lax.all_gather(w_out, ("dp", "fsdp"), axis=0, tiled=True),
        lax.all_gather(gain_one, ("dp", "fsdp"), axis=0, tiled=True),
    )
    gain_first = full_gain_one.astype(jnp.float32)
    grad_attn = grad_stream_two.astype(jnp.bfloat16)
    grad_w_out = jnp.einsum("td,te->de", attended, grad_attn, preferred_element_type=jnp.float32)
    grad_attended = jnp.einsum(
        "te,de->td", grad_attn, full_out, preferred_element_type=jnp.float32
    ).astype(jnp.bfloat16)
    grad_query, grad_key, grad_value = lax.map(
        lambda entries: head_backward(entries, allowed, score_scale),
        (queries, key_heads, value_heads, to_heads(grad_attended), log_total),
    )
    grad_qkv = jnp.concatenate(
        [from_heads(grad_query), from_heads(grad_key), from_heads(grad_value)], axis=1
    ).astype(jnp.bfloat16)
    grad_w_qkv = jnp.einsum("td,te->de", normed_one, grad_qkv, preferred_element_type=jnp.float32)
    grad_normed_one = jnp.einsum(
        "te,de->td", grad_qkv, full_qkv, preferred_element_type=jnp.float32
    )
    _, pull_one = jax.vjp(layer_norm, stream, gain_first)
    grad_stream_one, grad_gain_one = pull_one(grad_normed_one)
    grad_tokens = grad_stream_two + grad_stream_one
    (
        part_qkv,
        part_out,
        part_gain_one,
        part_in,
        part_down,
        lead_expert_in,
        lead_expert_out,
        part_mix,
        part_gain_two,
    ) = (
        lax.psum_scatter(grad_w_qkv, ("dp", "fsdp"), scatter_dimension=0, tiled=True),
        lax.psum_scatter(grad_w_out, ("dp", "fsdp"), scatter_dimension=0, tiled=True),
        lax.psum_scatter(grad_gain_one, ("dp", "fsdp"), scatter_dimension=0, tiled=True),
        lax.psum_scatter(grad_w_in, ("dp", "fsdp"), scatter_dimension=0, tiled=True),
        lax.psum_scatter(grad_w_down, ("dp", "fsdp"), scatter_dimension=0, tiled=True),
        lax.psum_scatter(grad_expert_in_lead, ("dp", "fsdp"), scatter_dimension=0, tiled=True),
        lax.psum_scatter(grad_expert_out_lead, ("dp", "fsdp"), scatter_dimension=0, tiled=True),
        lax.psum_scatter(grad_w_mix, ("dp", "fsdp"), scatter_dimension=0, tiled=True),
        lax.psum_scatter(grad_gain_two, ("dp", "fsdp"), scatter_dimension=0, tiled=True),
    )
    part_expert_in = lead_expert_in.transpose(1, 0, 2)
    part_expert_out = lead_expert_out.transpose(1, 0, 2)
    return (
        block_out,
        grad_tokens,
        part_qkv,
        part_out,
        part_gain_one,
        part_in,
        part_down,
        part_expert_in,
        part_expert_out,
        part_mix,
        part_gain_two,
    )


BF = jnp.bfloat16
F32 = jnp.float32
MESH = pl.DeviceIdType.MESH
ANY = pl.BlockSpec(memory_space=pl.ANY)
VM = pl.BlockSpec(memory_space=pltpu.VMEM)
SM = pl.BlockSpec(memory_space=pltpu.SMEM)
MIB = 1024 * 1024


def dot_nn(a, b):
    return lax.dot_general(a, b, (((1,), (0,)), ((), ())), preferred_element_type=F32)


def dot_nt(a, b):
    return lax.dot_general(a, b, (((1,), (1,)), ((), ())), preferred_element_type=F32)


def dot_tn(a, b):
    return lax.dot_general(a, b, (((0,), (0,)), ((), ())), preferred_element_type=F32)


class Place:
    def __init__(self):
        dp, fs = lax.axis_index("dp"), lax.axis_index("fsdp")
        z, y, x, c = dp // 2, dp % 2, fs // 2, fs % 2
        self.z, self.y, self.x, self.c = z, y, x, c
        self.own = (y, x, c)
        self.sib = (y, x, 1 - c)
        self.d1 = ((y + c) % 2, (x + 1 - c) % 2, c)
        self.d2 = ((y + 1 - c) % 2, (x + c) % 2, c)
        self.dd = (1 - y, 1 - x, c)
        self.zk = [z, z + 1 - 2 * (z % 2), (z + 2) % 4, 3 - z]
        self.t = self.rank(self.own)
        self.b = z * 8 + self.t

    @staticmethod
    def rank(p):
        return p[0] * 4 + p[1] * 2 + p[2]

    def flip(self, p):
        return (p[0], p[1], 1 - p[2])

    def dev(self, p, z=None):
        z = self.z if z is None else z
        return (z * 2 + p[0], p[1] * 2 + p[2])

    def plane_others(self):
        y, x, c = self.own
        return [
            ((y + k // 4) % 2, (x + (k // 2) % 2) % 2, (c + k % 2) % 2) for k in range(1, 8)
        ]


def rcopy(src, dst, send, recv, dev):
    return pltpu.make_async_remote_copy(
        src_ref=src, dst_ref=dst, send_sem=send, recv_sem=recv, device_id=dev, device_id_type=MESH
    )


def meet(devs):
    bar = pltpu.get_barrier_semaphore()
    for dev in devs:
        pl.semaphore_signal(bar, inc=1, device_id=dev, device_id_type=MESH)
    pl.semaphore_wait(bar, len(devs))


def norm_parts(v):
    mean = jnp.mean(v, axis=-1, keepdims=True)
    cen = v - mean
    var = jnp.mean(cen * cen, axis=-1, keepdims=True)
    r = lax.rsqrt(var + 1e-05)
    return cen * r, r


def row_of(extra, lane):
    pick = (lax.broadcasted_iota(jnp.int32, (8, 128), 1) == lane).astype(BF)
    return dot_nt(pick, extra)[0:1]


class ZSum:
    def __init__(self, P_, src, land, via, send, recv):
        self.P, self.src, self.land, self.via = P_, src, land, via
        self.send, self.recv = send, recv
        self.mid = (P_.z == 1) | (P_.z == 2)

    def copy(self, n, w, j):
        P_ = self.P
        to = P_.dev(P_.own, P_.zk[1 if j == 4 else j])
        block = self.src[w].at[n, P_.zk[3 if j == 4 else j]]
        dst = self.via[w].at[n] if j == 4 else self.land[w].at[n, j - 1]
        i = w * 4 + j - 1
        return rcopy(block, dst, self.send.at[n, i], self.recv.at[n, i], to)

    def ship(self, n, ws=(0, 1)):
        @pl.when(self.mid)
        def _():
            for j in (3, 1):
                for w in ws:
                    self.copy(n, w, j).start()

        @pl.when(jnp.logical_not(self.mid))
        def _():
            for j in (4, 2, 1):
                for w in ws:
                    self.copy(n, w, j).start()

    def transit(self, n, ws=(0, 1)):
        @pl.when(self.mid)
        def _():
            k2 = self.P.zk[2]
            for w in ws:
                self.copy(n, w, 4).wait_recv()
                self.src[w][n, k2] = self.src[w][n, k2] + self.via[w][n]
                self.copy(n, w, 2).start()

    def arrived(self, n, ws=(0, 1)):
        for w in ws:
            self.copy(n, w, 1).wait_recv()
            self.copy(n, w, 2).wait_recv()

        @pl.when(self.mid)
        def _():
            for w in ws:
                self.copy(n, w, 3).wait_recv()

    def sent(self, n, ws=(0, 1)):
        for w in ws:
            self.copy(n, w, 1).wait_send()
            self.copy(n, w, 2).wait_send()

        @pl.when(self.mid)
        def _():
            for w in ws:
                self.copy(n, w, 3).wait_send()

        @pl.when(jnp.logical_not(self.mid))
        def _():
            for w in ws:
                self.copy(n, w, 4).wait_send()


class ZGather:
    def __init__(self, P_, mine, full, send, recv):
        self.P, self.mine, self.full, self.send, self.recv = P_, mine, full, send, recv
        self.mid = (P_.z == 1) | (P_.z == 2)
        self.all = range(len(mine))

    def copy(self, w, j):
        P_ = self.P
        zs = P_.zk[2] if j == 4 else P_.z
        block = self.full[w](zs) if j == 4 else self.mine[w]
        to = P_.dev(P_.own, P_.zk[1 if j == 4 else j])
        return rcopy(block, self.full[w](zs), self.send.at[w * 4 + j - 1], self.recv.at[w * 4 + zs], to)

    def landed(self, w, j):
        P_ = self.P
        zs = P_.zk[j]
        rcopy(
            self.mine[w], self.full[w](zs), self.send.at[0], self.recv.at[w * 4 + zs], P_.dev(P_.sib)
        ).wait_recv()

    def ship(self):
        for w in self.all:
            self.copy(w, 2).start()

        @pl.when(self.mid)
        def _():
            for w in self.all:
                self.copy(w, 3).start()

        for w in self.all:
            self.copy(w, 1).start()

    def relay(self):
        for w in self.all:
            self.landed(w, 2)

        @pl.when(self.mid)
        def _():
            for w in self.all:
                self.copy(w, 4).start()

    def finish(self):
        for w in self.all:
            self.landed(w, 1)
            self.landed(w, 3)
            self.copy(w, 1).wait_send()
            self.copy(w, 2).wait_send()

        @pl.when(self.mid)
        def _():
            for w in self.all:
                self.copy(w, 3).wait_send()
                self.copy(w, 4).wait_send()


PW = 4224
EX = 3072
WO = 3200


def enter_kernel(
    len_ref, tok, cot, tab, w_qkv, w_out, small, w_in, w_ein, w_down, w_eout,
    qkv_o, lse_o, att_o, s2_o, n1_o, wmix_o, pack_all, wi_all, wd_all, g_all, nt_all,
    pack_v, wia, gt, qkv, lse, att, s2, nt, n1,
    pz, ps, pr, asend, arecv, fsend, frecv, gs, gr, ts, tr, lsem, osem,
):
    P_ = Place()
    z, t, b = P_.z, P_.t, P_.b
    own, sib, d1, d2, dd = P_.own, P_.sib, P_.d1, P_.d2, P_.dd
    others = P_.plane_others()
    pack = pack_v.at[b]
    pack_v[b, :, 0:3072] = w_qkv[...]
    pick = (
        lax.broadcasted_iota(jnp.int32, (4, 128), 1) == lax.broadcasted_iota(jnp.int32, (4, 128), 0)
    ).astype(BF)
    pack_v[b, :, EX : EX + 128] = dot_tn(small[...], pick).astype(BF)
    pack_v[b, :, WO : WO + 1024] = w_out[...]
    meet([P_.dev(p) for p in others] + [P_.dev(own, zz) for zz in P_.zk[1:]])
    sends = []
    keeps = []

    def go(cp):
        cp.start()
        sends.append(cp)

    def store(src, dst):
        cp = pltpu.make_async_copy(src, dst, osem.at[len(keeps)])
        cp.start()
        keeps.append(cp)

    def gather(n, mine, full):
        return ZGather(P_, (mine,), (full,), fsend.at[n], frecv.at[n])

    out_a = gather(0, w_eout.at[0], lambda zs: wd_all.at[1, zs])
    out_b = gather(1, w_eout.at[1], lambda zs: wd_all.at[2, zs])
    in_a = gather(2, wi_all.at[1, z], lambda zs: wi_all.at[1, zs])
    in_b = gather(3, wi_all.at[2, z], lambda zs: wi_all.at[2, zs])
    mid = in_a.mid

    def z_copy(k, s, to):
        return rcopy(pack_v.at[s], pack_v.at[s], pz.at[k - 1], pr.at[s], P_.dev(own, P_.zk[to]))

    z_copy(2, b, 2).start()

    @pl.when(mid)
    def _():
        z_copy(3, b, 3).start()

    z_copy(1, b, 1).start()
    go(rcopy(pack, pack, ps.at[3], pr.at[b], P_.dev(d1)))
    go(rcopy(pack, pack, ps.at[7], pr.at[b], P_.dev(d2)))
    go(rcopy(pack, pack, ps.at[15], pr.at[b], P_.dev(sib)))
    out_a.ship()
    for r in range(8):
        for zz in range(4):
            at = slice((zz * 8 + r) * 128, (zz * 8 + r + 1) * 128)
            to = slice(zz * 128, (zz + 1) * 128)
            wia[r, 0, :, to] = w_in[:, at]
            wia[r, 1:3, :, to] = w_ein[:, :, at]
    rows = pl.ds(pl.multiple_of(t * 32, 32), 32)
    lw = pltpu.make_async_copy(wia.at[t], wi_all.at[:, z, rows], lsem.at[1])
    lw.start()
    for i, p in enumerate(others):
        go(rcopy(wia.at[P_.rank(p)], wi_all.at[:, z, rows], asend.at[i], arecv.at[t], P_.dev(p)))
    store(w_down, wd_all.at[0, z])
    store(w_eout, wd_all.at[1:3, z])
    keep = lax.broadcasted_iota(jnp.int32, (384, 1), 0) < len_ref[0]
    gt[0:384] = jnp.where(keep, cot[...], jnp.zeros_like(cot[...]))
    gt[384:400] = jnp.zeros((16, 1024), BF)
    gt[384:385, 0:384] = tab[...].astype(BF)

    def landed(slot):
        rcopy(pack, pack_v.at[slot], ps.at[0], pr.at[slot], P_.dev(sib)).wait_recv()

    def fwd(slot, sem, p):
        go(rcopy(pack_v.at[slot], pack_v.at[slot], ps.at[sem], pr.at[slot], P_.dev(p)))

    def slot(k, p):
        return P_.zk[k] * 8 + P_.rank(p)

    for k in range(0, 6):
        if k == 2:
            out_b.ship()
        if 1 <= k <= 3:
            s = slot(k, own)
            landed(s)
            if k == 2:

                @pl.when(mid)
                def _():
                    z_copy(4, s, 1).start()

            fwd(s, 3 + k, d1)
            fwd(s, 7 + k, d2)
            fwd(s, 15 + k, sib)
        if k == 3:
            lw.wait()
            for p in others:
                rr = P_.rank(p)
                rq = pl.ds(pl.multiple_of(rr * 32, 32), 32)
                rcopy(
                    wia.at[0], wi_all.at[:, z, rq], asend.at[0], arecv.at[rr], P_.dev(sib)
                ).wait_recv()
            out_a.relay()
            in_a.ship()
        if 1 <= k <= 4:
            s = slot(k - 1, d1)
            landed(s)
            fwd(s, 11 + k - 1, d2)
            fwd(s, 19 + k - 1, sib)
            s = slot(k - 1, d2)
            landed(s)
            fwd(s, 23 + k - 1, sib)
        if k >= 2:
            s = slot(k - 2, dd)
            landed(s)
            fwd(s, 27 + k - 2, sib)
    in_b.ship()
    stream = tok[...].astype(F32)
    for k in range(4):
        for p in (own, d1, d2, dd):
            landed(slot(k, P_.flip(p)))
    store(gt, g_all.at[t])
    for i, p in enumerate((d1, d2, sib)):
        go(rcopy(gt, g_all.at[t], gs.at[i], gr.at[t], P_.dev(p)))
    store(pack_v, pack_all)
    store(pack_v.at[:, :, EX : EX + 128], wmix_o)

    extra = pack_v[:, :, EX : EX + 128].reshape(1024, 128)
    n_one, _ = norm_parts(stream)
    n1[...] = (n_one * row_of(extra, 2)).astype(BF)
    store(n1, n1_o)

    def qkv_step(j, carry):
        cols = pl.ds(pl.multiple_of(j * 512, 512), 512)
        qkv[:, cols] = dot_nn(n1[...], pack_v[:, :, cols].reshape(1024, 512)).astype(BF)
        return carry

    lax.fori_loop(0, 6, qkv_step, 0)
    store(qkv, qkv_o)

    def plane(src_own, full, send, recv):
        def landed_at(p):
            r = P_.rank(p)
            rcopy(src_own, full.at[r], send.at[0], recv.at[r], P_.dev(sib)).wait_recv()
            return r

        def pass_on(p, *dests):
            r = landed_at(p)
            for i, q in dests:
                go(rcopy(full.at[r], full.at[r], send.at[i], recv.at[r], P_.dev(q)))

        return landed_at, pass_on

    g_landed, g_pass = plane(gt, g_all, gs, gr)
    n_landed, n_pass = plane(nt, nt_all, ts, tr)

    allowed = masks(len_ref[0])
    lane = lax.broadcasted_iota(jnp.int32, (384, 128), 1)
    lse[...] = jnp.zeros_like(lse)

    def pair_step(p, carry):
        q2 = qkv[:, pl.ds(pl.multiple_of(p * 128, 128), 128)]
        k2 = qkv[:, pl.ds(pl.multiple_of(1024 + p * 128, 128), 128)]
        v2 = qkv[:, pl.ds(pl.multiple_of(2048 + p * 128, 128), 128)]
        outs = []
        for hh in range(2):
            qm = jnp.where(lane // 64 == hh, q2, jnp.zeros_like(q2))
            sc = jnp.where(allowed, dot_nt(qm, k2) * 0.125, -1e30)
            top = jnp.max(sc, axis=-1, keepdims=True)
            ex = jnp.exp(sc - top)
            tot = jnp.sum(ex, axis=-1, keepdims=True)
            outs.append(dot_nn((ex * (1.0 / tot)).astype(BF), v2))
            lse[...] = jnp.where(lane == 2 * p + hh, top + jnp.log(tot), lse[...])
        att[:, pl.ds(pl.multiple_of(p * 128, 128), 128)] = jnp.where(
            lane < 64, outs[0], outs[1]
        ).astype(BF)
        return carry

    lax.fori_loop(0, 8, pair_step, 0)
    store(lse, lse_o)
    store(att, att_o)
    for j in range(2):
        w = pack_v[:, :, WO + j * 512 : WO + (j + 1) * 512].reshape(1024, 512)
        s2[:, j * 512 : (j + 1) * 512] = stream[:, j * 512 : (j + 1) * 512] + dot_nn(att[...], w)
    store(s2, s2_o)
    n_two, _ = norm_parts(s2[...])
    nt[...] = (n_two * row_of(extra, 3)).astype(BF)
    store(nt, nt_all.at[t])
    for i, p in enumerate((d1, d2, sib)):
        go(rcopy(nt, nt_all.at[t], ts.at[i], tr.at[t], P_.dev(p)))
    out_b.relay()
    in_a.relay()
    g_pass(d1, (4, sib))
    g_pass(d2, (5, sib))
    in_b.relay()
    n_pass(d1, (4, sib))
    n_pass(d2, (5, sib))
    for p in (own, d1, d2):
        g_landed(P_.flip(p))
    for p in (own, d2, d1):
        n_landed(P_.flip(p))
    for part in (out_a, out_b, in_a, in_b):
        part.finish()
    z_copy(1, b, 1).wait_send()
    z_copy(2, b, 2).wait_send()

    @pl.when(mid)
    def _():
        z_copy(3, b, 3).wait_send()
        z_copy(4, b, 1).wait_send()

    for cp in keeps:
        cp.wait()
    for cp in sends:
        cp.wait_send()


def masks(seq_len):
    row = lax.broadcasted_iota(jnp.int32, (384, 384), 0)
    col = lax.broadcasted_iota(jnp.int32, (384, 384), 1)
    return (col <= row) & (col < seq_len)


def run_enter(*args):
    sd = jax.ShapeDtypeStruct
    dma = pltpu.SemaphoreType.DMA
    return pl.pallas_call(
        enter_kernel,
        out_shape=(
            sd((384, 3072), BF), sd((384, 128), F32), sd((384, 1024), BF), sd((384, 1024), F32),
            sd((384, 1024), BF), sd((32, 32, 128), BF),
            sd((32, 32, PW), BF), sd((3, 4, 256, 512), BF), sd((3, 4, 128, 1024), BF),
            sd((8, 400, 1024), BF), sd((8, 384, 1024), BF),
        ),
        in_specs=[SM] + [VM] * 10,
        out_specs=(ANY,) * 11,
        scratch_shapes=[
            pltpu.VMEM((32, 32, PW), BF), pltpu.VMEM((8, 3, 32, 512), BF), pltpu.VMEM((400, 1024), BF),
            pltpu.VMEM((384, 3072), BF), pltpu.VMEM((384, 128), F32), pltpu.VMEM((384, 1024), BF),
            pltpu.VMEM((384, 1024), F32), pltpu.VMEM((384, 1024), BF), pltpu.VMEM((384, 1024), BF),
            dma((4,)), dma((31,)), dma((32,)), dma((7,)), dma((8,)), dma((4, 4)), dma((4, 4)),
            dma((7,)), dma((8,)), dma((7,)), dma((8,)), dma((4,)), dma((12,)),
        ],
        compiler_params=pltpu.CompilerParams(
            collective_id=0, has_side_effects=True, vmem_limit_bytes=63 * MIB
        ),
    )(*args)


def mix_of(delta):
    return 1.0 / (1.0 + jnp.exp(-delta)), 1.0 / (1.0 + jnp.exp(delta))


def gelu_both(u):
    a, bb = 0.7978845608028654, 0.044715
    u2 = u * u
    th = jnp.tanh(a * u * (1.0 + bb * u2))
    half = 0.5 * (1.0 + th)
    return u * half, half + 0.5 * u * (1.0 - th * th) * a * (1.0 + 3.0 * bb * u2)


def ff_kernel(
    nt_hbm, wmix, g_all, wi_all, wd_all,
    gsum, gl_out, bnext, bown, eoi, eod, dgi, dgd, r1, r2, rin, rdn, dwi, dwd, gfar,
    nt_all, gbuf, br, gn, xb, yb, wi, wd, ai, ad, gin, gdn, tri, trd, tmp, gc, gcr, dots, gaps,
    ts, tr, gs, gr, gsem, wsem, dsem, zas, zar, zss, zsr, s1s, s1r, s2s, s2r, cs, cr, lsem, tsem,
):
    P_ = Place()
    z, t = P_.z, P_.t
    own, sib, d1, d2, dd = P_.own, P_.sib, P_.d1, P_.d2, P_.dd
    others = P_.plane_others()
    meet([P_.dev(p) for p in others] + [P_.dev(own, zz) for zz in P_.zk[1:]])
    sends = []

    def go(cp):
        cp.start()
        sends.append(cp)

    keeps = []

    def keep(src, dst):
        cp = pltpu.make_async_copy(src, dst, lsem.at[len(keeps)])
        cp.start()
        keeps.append(cp)

    dense = ZGather(
        P_, (wi_all.at[0, z], wd_all.at[0, z]), (lambda zs: dwi.at[zs], lambda zs: dwd.at[zs]), zas, zar
    )
    dense.ship()
    expert_load = (
        pltpu.make_async_copy(wi_all.at[1], wi.at[0], wsem.at[0, 0]),
        pltpu.make_async_copy(wd_all.at[1], wd.at[0], wsem.at[0, 1]),
        pltpu.make_async_copy(wi_all.at[2], wi.at[1], wsem.at[1, 0]),
        pltpu.make_async_copy(wd_all.at[2], wd.at[1], wsem.at[1, 1]),
    )
    for cp in expert_load:
        cp.start()

    def dense_load():
        copies = []
        for k in range(4):
            zz = P_.zk[k]
            for n, (full, far, dst) in enumerate(((wi_all, dwi, wi), (wd_all, dwd, wd))):
                src = full.at[0, z] if k == 0 else far.at[zz]
                copies.append(pltpu.make_async_copy(src, dst.at[0, zz], dsem.at[n, k]))
        return copies

    zsum = ZSum(P_, (gin, gdn), (rin, rdn), (tri, trd), zss, zsr)

    order = (own, sib, d1, P_.flip(d2), d2, P_.flip(d1), dd, P_.flip(dd))
    ranks = [P_.rank(p) for p in order]

    def seq_at(i):
        s = ranks[0]
        for k in range(1, 8):
            s = jnp.where(i == k, ranks[k], s)
        return s

    r1st, rdd = P_.rank(d1), P_.rank(dd)
    go(rcopy(nt_hbm.at[r1st], nt_all.at[r1st], ts.at[0], tr.at[r1st], P_.dev(d2)))
    go(rcopy(g_all.at[r1st], gfar.at[0], gs.at[0], gr.at[0], P_.dev(d2)))

    def far_on(start):
        cps = (
            rcopy(nt_all.at[rdd], nt_all.at[rdd], ts.at[1], tr.at[rdd], P_.dev(sib)),
            rcopy(gfar.at[0], gfar.at[1], gs.at[1], gr.at[1], P_.dev(sib)),
        )
        for cp in cps:
            if start:
                cp.start()
            else:
                cp.wait_send()

    def far_here(s, k):
        rcopy(gfar.at[0], gfar.at[k], gs.at[0], gr.at[k], P_.dev(sib)).wait_recv()
        rcopy(tmp.at[0], nt_all.at[s], ts.at[0], tr.at[s], P_.dev(sib)).wait_recv()

    class GCopy:
        def __init__(self, i):
            self.i = i

        def make(self, src):
            return pltpu.make_async_copy(src, gbuf.at[self.i % 2], gsem.at[self.i % 2])

        def start(self):
            @pl.when(self.i < 6)
            def _():
                self.make(g_all.at[seq_at(self.i)]).start()

            @pl.when(self.i >= 6)
            def _():
                self.make(gfar.at[jnp.maximum(self.i - 6, 0)]).start()

        def wait(self):
            self.make(g_all.at[0]).wait()

    def g_copy(i):
        return GCopy(i)

    def ff(xv, gv, k):
        wiv = wi[k].reshape(1024, 512)
        wdv = wd[k].reshape(512, 1024)
        act, dact = gelu_both(dot_nn(xv, wiv))
        act = act.astype(BF)
        gup = (dact * dot_nt(gv, wdv)).astype(BF)
        ad[k] += dot_tn(act, gv)
        ai[k] += dot_tn(xv, gup)
        return dot_nn(act, wdv), dot_nt(gup, wiv)

    lane = lax.broadcasted_iota(jnp.int32, (448, 128), 1)

    def shares(tab):
        slot = lax.broadcasted_iota(jnp.int32, (224, 384), 0)
        return (tab == slot.astype(F32)).astype(BF)

    def n_copy(s):
        return pltpu.make_async_copy(nt_hbm.at[s], nt_all.at[s], tr.at[s])

    for s in ranks[:6]:
        n_copy(s).start()
    g_copy(0).start()
    ai[...] = jnp.zeros_like(ai)
    ad[...] = jnp.zeros_like(ad)
    for cp in expert_load:
        cp.wait()

    def arrive(i, carry):
        s = seq_at(i)

        @pl.when(i == 5)
        def _():
            far_here(rdd, 0)
            far_on(True)

        @pl.when(i == 6)
        def _():
            far_here(P_.rank(P_.flip(dd)), 1)

        @pl.when(i + 1 < 8)
        def _():
            g_copy(i + 1).start()

        @pl.when(i < 6)
        def _():
            n_copy(s).wait()

        g_copy(i).wait()
        xv = nt_all[s]
        gv = gbuf[i % 2, :384]
        tab = gbuf[i % 2, 384:400][0:1, :384].astype(F32)
        lg = dot_nn(xv, wmix[...])
        gap = lg[:, 0:1] - lg[:, 1:2]
        gaps[i] = jnp.transpose(jnp.broadcast_to(gap, (384, 128)))[0:8]
        _, m1 = mix_of(gap)
        ge = (m1 * gv.astype(F32)).astype(BF)
        sh = shares(tab)
        xb[i] = dot_nn(sh, xv).astype(BF).reshape(2, 112, 1024)
        yb[i] = dot_nn(sh, ge).astype(BF).reshape(2, 112, 1024)
        return carry

    def expert(b, e):
        four = pl.ds(b * 4, 4)
        gq = yb[four, e].reshape(448, 1024)
        yv, gb = ff(xb[four, e].reshape(448, 1024), gq, e)
        rs = jnp.sum(gq.astype(F32) * yv, axis=-1, keepdims=True)
        high = rs.astype(BF).astype(F32)
        dots[four, e] = (
            jnp.where(lane == 0, high, jnp.where(lane == 1, rs - high, 0.0))
            .astype(BF)
            .reshape(4, 112, 128)
        )
        xb[four, e] = yv.astype(BF).reshape(4, 112, 1024)
        yb[four, e] = gb.astype(BF).reshape(4, 112, 1024)

    def stage(e):
        gin[e] = ai[e].astype(BF).reshape(4, 256, 512)
        gdn[e] = ad[e].astype(BF).reshape(4, 128, 1024)
        zsum.ship(e)
        keep(gin.at[e, z], eoi.at[e])
        keep(gdn.at[e, z], eod.at[e])

    def half(b, carry):
        lax.fori_loop(b * 4, b * 4 + 4, arrive, 0)
        @pl.when(b == 1)
        def _():
            dense.relay()

        expert(b, 0)
        expert(b, 1)
        return carry

    lax.fori_loop(0, 2, half, 0)
    stage(0)
    stage(1)
    far_on(False)
    g_copy(7).start()
    dense.finish()
    for cp in dense_load():
        cp.start()
    ai[0] = jnp.zeros_like(ai[0])
    ad[0] = jnp.zeros_like(ad[0])
    for cp in dense_load():
        cp.wait()

    chips = (dd, d1, d2, own)
    both = (gn, br)

    def give1(q, w):
        r = P_.rank(P_.flip(chips[q]))
        k = (0, 2, 1, 3)[q]
        return rcopy(both[w].at[r], r1.at[w, k], s1s.at[w, k], s1r.at[w, k], P_.dev(sib))

    def load1(q, w, start):
        cp = pltpu.make_async_copy(r1.at[w, q], tmp.at[w], tsem.at[w])
        if start:
            rcopy(tmp.at[0], r1.at[w, q], s1s.at[0, 0], s1r.at[w, q], P_.dev(sib)).wait_recv()
            cp.start()
        else:
            cp.wait()
            add_tmp(w, P_.rank(chips[q]))

    def load2(k, p, w, start):
        cp = pltpu.make_async_copy(r2.at[w, k], tmp.at[w], tsem.at[w])
        if start:
            rcopy(tmp.at[0], r2.at[w, k], s2s.at[0, 0], s2r.at[w, k], P_.dev(sib)).wait_recv()
            cp.start()
        else:
            cp.wait()
            add_tmp(w, P_.rank(p))

    def add_tmp(w, r):
        both[w][r] = both[w][r] + tmp[w]

    def give2(q, k, p, w):
        src = both[w].at[P_.rank(chips[q])]
        return rcopy(src, r2.at[w, k], s2s.at[w, k], s2r.at[w, k], P_.dev(p))

    def at_step(step, k, fn):
        @pl.when(step == k)
        def _():
            for w in range(2):
                fn(w)

    def dense_step(k, carry):
        i = 7 - k
        s = seq_at(i)

        @pl.when(i > 0)
        def _():
            g_copy(i - 1).start()

        g_copy(i).wait()
        xv = nt_all[s]
        gf = gbuf[i % 2, :384].astype(F32)
        tab = gbuf[i % 2, 384:400][0:1, :384].astype(F32)
        gap = jnp.transpose(jnp.broadcast_to(gaps[i][0:1], (128, 384)))[:, 0:1]
        m0, m1 = mix_of(gap)
        out, gxv = ff(xv, (m0 * gf).astype(BF), 0)
        at_step(k, 1, lambda w: load1(0, w, True))
        at_step(k, 3, lambda w: load1(2, w, True))
        at_step(k, 5, lambda w: load1(1, w, True))
        at_step(k, 7, lambda w: load1(3, w, True))
        col = jnp.broadcast_to(jnp.sum(gf * out, axis=-1, keepdims=True), (384, 128))
        gc[s, 0:8] = jnp.transpose(col)[0:8]
        sh = shares(tab)
        q1 = dot_tn(sh, dots[i].reshape(224, 128))
        gc[s, 8:16] = jnp.transpose(jnp.broadcast_to(q1[:, 0:1] + q1[:, 1:2], (384, 128)))[0:8]
        gn[s] = (gxv + dot_tn(sh, yb[i].reshape(224, 1024))).astype(BF)
        br[s] = (m0 * out + m1 * dot_tn(sh, xb[i].reshape(224, 1024))).astype(BF)

        for q in range(4):
            at_step(k, 2 * q, lambda w, q=q: give1(q, w).start())

        def pass_on(q, n, p):
            def fn(w):
                load1(q, w, False)
                give2(q, n, p, w).start()

            return fn

        at_step(k, 1, pass_on(0, 0, d2))
        at_step(k, 3, pass_on(2, 2, d2))
        at_step(k, 5, lambda w: load1(1, w, False))
        at_step(k, 5, lambda w: load2(0, d1, w, True))

        def turn(w):
            load2(0, d1, w, False)
            if w == 0:
                give2(1, 1, d1, w).start()

        at_step(k, 5, turn)
        at_step(k, 7, lambda w: load1(3, w, False))

        @pl.when(k == 2)
        def _():
            zsum.transit(0)

        @pl.when(k == 5)
        def _():
            zsum.transit(1)

        return carry

    lax.fori_loop(0, 8, dense_step, 0)
    for i, p in enumerate(others):
        go(rcopy(gc.at[P_.rank(p)], gcr.at[t], cs.at[i], cr.at[t], P_.dev(p)))
    keep(br.at[P_.rank(d1)], bnext)
    for w in range(2):
        load2(2, own, w, True)
    for w in range(2):
        load2(2, own, w, False)
    keep(br.at[t], bown)
    load2(1, own, 0, True)
    for p in others:
        r = P_.rank(p)
        rcopy(gc.at[0], gcr.at[r], cs.at[0], cr.at[r], P_.dev(sib)).wait_recv()
    gcr[t] = gc[t]
    tot = jnp.sum(gcr[...], axis=0)
    gc0 = jnp.transpose(jnp.broadcast_to(tot[0:1], (128, 384)))
    q1 = jnp.transpose(jnp.broadcast_to(tot[8:9], (128, 384)))
    m0, m1 = mix_of(jnp.transpose(jnp.broadcast_to(gaps[0][0:1], (128, 384))))
    gl_out[...] = m0 * (m1 * gc0 - q1)
    load2(1, own, 0, False)
    gsum[...] = gn[t].astype(F32)
    zsum.sent(0)
    for cp in keeps[0:2]:
        cp.wait()
    gin[0] = ai[0].astype(BF).reshape(4, 256, 512)
    gdn[0] = ad[0].astype(BF).reshape(4, 128, 1024)
    keep(gin.at[0], dgi)
    keep(gdn.at[0], dgd)
    for w in range(2):
        for q in range(4):
            give1(q, w).wait_send()
        give2(0, 0, d2, w).wait_send()
        give2(2, 2, d2, w).wait_send()
    give2(1, 1, d1, 0).wait_send()
    zsum.arrived(0)
    zsum.arrived(1)
    zsum.sent(1)
    for cp in keeps[2:]:
        cp.wait()
    for cp in sends:
        cp.wait_send()


def run_ff(*args):
    sd = jax.ShapeDtypeStruct
    dma = pltpu.SemaphoreType.DMA
    out = pl.pallas_call(
        ff_kernel,
        out_shape=(
            sd((384, 1024), F32), sd((384, 128), F32), sd((384, 1024), BF), sd((384, 1024), BF),
            sd((2, 256, 512), BF), sd((2, 128, 1024), BF),
            sd((4, 256, 512), BF), sd((4, 128, 1024), BF),
            sd((2, 4, 384, 1024), BF), sd((2, 3, 384, 1024), BF),
            sd((2, 3, 256, 512), BF), sd((2, 3, 128, 1024), BF),
            sd((4, 256, 512), BF), sd((4, 128, 1024), BF), sd((2, 400, 1024), BF),
        ),
        in_specs=[ANY, VM, ANY, ANY, ANY],
        out_specs=(VM,) * 2 + (ANY,) * 13,
        scratch_shapes=[
            pltpu.VMEM((8, 384, 1024), BF), pltpu.VMEM((2, 400, 1024), BF),
            pltpu.VMEM((8, 384, 1024), BF), pltpu.VMEM((8, 384, 1024), BF),
            pltpu.VMEM((8, 2, 112, 1024), BF), pltpu.VMEM((8, 2, 112, 1024), BF),
            pltpu.VMEM((2, 4, 256, 512), BF), pltpu.VMEM((2, 4, 128, 1024), BF),
            pltpu.VMEM((2, 1024, 512), F32), pltpu.VMEM((2, 512, 1024), F32),
            pltpu.VMEM((2, 4, 256, 512), BF), pltpu.VMEM((2, 4, 128, 1024), BF),
            pltpu.VMEM((2, 256, 512), BF), pltpu.VMEM((2, 128, 1024), BF),
            pltpu.VMEM((2, 384, 1024), BF),
            pltpu.VMEM((8, 16, 384), F32), pltpu.VMEM((8, 16, 384), F32), pltpu.VMEM((8, 2, 112, 128), BF),
            pltpu.VMEM((8, 8, 384), F32),
            dma((2,)), dma((8,)), dma((2,)), dma((2,)), dma((2,)), dma((2, 2)), dma((2, 4)), dma((8,)), dma((8,)),
            dma((2, 8)), dma((2, 8)),
            dma((2, 4)), dma((2, 4)), dma((2, 3)), dma((2, 3)), dma((7,)), dma((8,)), dma((10,)), dma((2,)),
        ],
        compiler_params=pltpu.CompilerParams(
            collective_id=1, has_side_effects=True, vmem_limit_bytes=63 * MIB
        ),
    )(*args)
    return (*out[:8], out[10], out[11])


class RowSum:
    swap = (0, 2, 1, 3)

    def __init__(self, P_, g, r1, r2, r3, sems):
        self.P, self.g, self.r1, self.r2, self.r3 = P_, g, r1, r2, r3
        self.s1s, self.s1r, self.s2s, self.s2r, self.s3s, self.s3r = sems
        self.chips = (P_.dd, P_.d1, P_.d2, P_.own)

    def rank(self, q):
        return self.P.rank(self.chips[q])

    def copy1(self, n, q):
        k = self.swap[q]
        src = self.g.at[n, self.P.rank(self.P.flip(self.chips[q]))]
        return rcopy(src, self.r1.at[n, k], self.s1s.at[n, k], self.s1r.at[n, k], self.P.dev(self.P.sib))

    def copy2(self, n, q, k, p):
        src = self.g.at[n, self.rank(q)]
        return rcopy(src, self.r2.at[n, k], self.s2s.at[n, k], self.s2r.at[n, k], self.P.dev(p))

    def copy3(self, n, k):
        P_ = self.P
        return rcopy(
            self.g.at[n, P_.t, P_.zk[k]], self.r3.at[n, k - 1], self.s3s.at[n, k - 1],
            self.s3r.at[n, k - 1], P_.dev(P_.own, P_.zk[k]),
        )

    def in1(self, n, q):
        rcopy(
            self.g.at[n, 0], self.r1.at[n, q], self.s1s.at[n, 0], self.s1r.at[n, q], self.P.dev(self.P.sib)
        ).wait_recv()
        r = self.rank(q)
        self.g[n, r] = self.g[n, r] + self.r1[n, q]

    def in2(self, n, k, q):
        rcopy(
            self.g.at[n, 0], self.r2.at[n, k], self.s2s.at[n, 0], self.s2r.at[n, k], self.P.dev(self.P.sib)
        ).wait_recv()
        r = self.rank(q)
        self.g[n, r] = self.g[n, r] + self.r2[n, k]

    def step1(self, n):
        for q in (0, 1, 2, 3):
            self.copy1(n, q).start()

    def step2(self, n):
        P_ = self.P
        self.in1(n, 0)
        self.copy2(n, 0, 0, P_.d2).start()
        self.in1(n, 2)
        self.copy2(n, 2, 2, P_.d2).start()
        self.in1(n, 1)

    def step3(self, n):
        self.in2(n, 0, 1)
        self.copy2(n, 1, 1, self.P.d1).start()
        self.in1(n, 3)

    def step4(self, n):
        self.in2(n, 2, 3)
        self.in2(n, 1, 3)
        for k in (3, 2, 1):
            self.copy3(n, k).start()

    def step5(self, n):
        P_ = self.P
        for k in (1, 2, 3):
            rcopy(
                self.g.at[n, 0, 0], self.r3.at[n, k - 1], self.s3s.at[n, 0], self.s3r.at[n, k - 1],
                P_.dev(P_.sib),
            ).wait_recv()
        total = self.g[n, P_.t, P_.z].astype(F32)
        for k in range(3):
            total += self.r3[n, k].astype(F32)
        return total

    def sent(self, n):
        P_ = self.P
        for q in range(4):
            self.copy1(n, q).wait_send()
        self.copy2(n, 0, 0, P_.d2).wait_send()
        self.copy2(n, 2, 2, P_.d2).wait_send()
        self.copy2(n, 1, 1, P_.d1).wait_send()
        for k in (1, 2, 3):
            self.copy3(n, k).wait_send()


def back_kernel(
    len_ref, tok, s2, n1, qkv, lse, att, gsum, gl, g_all, nt_all, pack_all,
    bnext, bown, eoi, eod, dgi, dgd, ein, edr,
    block, gtok, gqkv, gwo, gex, gdd, gde, gwi, gwe,
    gx, gt, nt, bin_, xe, er, ed, eo,
    pack_v, gq, gacc, n1t, ga_, gb_, gc_, ra1, ra2, ra3, rb1, rb2, rb3, rc1, rc2, rc3,
    gin, gdn, rin, rdn, tri, trd, *sems,
):
    P_ = Place()
    z, t = P_.z, P_.t
    own, sib, d1, d2, dd = P_.own, P_.sib, P_.d1, P_.d2, P_.dd
    others = P_.plane_others()
    zss, zsr, xs, xr, bs, lsem = sems[18:]
    sum_a = RowSum(P_, ga_, ra1, ra2, ra3, sems[0:6])
    sum_b = RowSum(P_, gb_, rb1, rb2, rb3, sems[6:12])
    sum_c = RowSum(P_, gc_, rc1, rc2, rc3, sems[12:18])
    lw = pltpu.make_async_copy(pack_all, pack_v, lsem.at[0])
    z_in = (
        pltpu.make_async_copy(dgi, gin.at[0], lsem.at[2]),
        pltpu.make_async_copy(dgd, gdn.at[0], lsem.at[7]),
    )
    own_in = (
        pltpu.make_async_copy(g_all.at[t], gt, lsem.at[5]),
        pltpu.make_async_copy(nt_all.at[t], nt, lsem.at[6]),
    )
    e_in = (
        pltpu.make_async_copy(eoi, xe, lsem.at[8]),
        pltpu.make_async_copy(ein, er, lsem.at[9]),
        pltpu.make_async_copy(eod, eo, lsem.at[10]),
        pltpu.make_async_copy(edr, ed, lsem.at[11]),
    )
    for cp in (*z_in, lw, *own_in, *e_in):
        cp.start()
    meet([P_.dev(p) for p in others] + [P_.dev(own, zz) for zz in P_.zk[1:]])
    sends = []

    def go(cp):
        cp.start()
        sends.append(cp)

    def rows(p):
        return pl.ds(pl.multiple_of(P_.rank(p) * 32, 32), 32)

    zsum = ZSum(P_, (gin, gdn), (rin, rdn), (tri, trd), zss, zsr)
    for cp in z_in:
        cp.wait()
    zsum.ship(0)
    go(rcopy(bnext, bin_, bs.at[0], bs.at[1], P_.dev(d1)))

    lw.wait()
    for cp in own_in:
        cp.wait()
    extra = pack_v[:, :, EX : EX + 128].reshape(1024, 128)
    lane = lax.broadcasted_iota(jnp.int32, (384, 128), 1)
    glv = gl[...]
    gnt = gsum[...] + glv[:, 0:1] * (row_of(extra, 0) - row_of(extra, 1))
    two = jnp.where(lane == 0, glv, jnp.where(lane == 1, -glv, 0.0)).astype(BF)
    n_two, r_two = norm_parts(s2[...])
    gain_two_row = jnp.sum(gnt * n_two, axis=0, keepdims=True)

    def norm_back(gv, gain, n, r):
        tt = gv * gain
        return r * (tt - jnp.mean(tt, -1, keepdims=True) - n * jnp.mean(tt * n, -1, keepdims=True))

    gs2 = gt[0:384].astype(F32) + norm_back(gnt, row_of(extra, 3), n_two, r_two)
    gtok[...] = gs2
    ga = gs2.astype(BF)

    def put(ref, n, cols, val):
        low = val.astype(BF)
        for zz in range(4):
            ref[n, :, zz, :, cols] = low[zz * 256 : (zz + 1) * 256].reshape(8, 32, low.shape[1])

    for j in range(2):
        cols = slice(j * 512, (j + 1) * 512)
        put(ga_, 0, cols, dot_tn(att[...], ga[:, cols]))
    sum_a.step1(0)
    for cp in e_in:
        cp.wait()
    mid = zsum.mid
    for e in range(2):
        total = xe[e].astype(F32) + er[e, 0].astype(F32) + er[e, 1].astype(F32)
        xe[e] = (total + jnp.where(mid, er[e, 2].astype(F32), 0.0)).astype(BF)
        total = eo[e].astype(F32) + ed[e, 0].astype(F32) + ed[e, 1].astype(F32)
        gde[e] = total + jnp.where(mid, ed[e, 2].astype(F32), 0.0)
    le = pltpu.make_async_copy(xe.at[:, rows(own)], gx.at[t, 1:3], lsem.at[3])
    le.start()
    for i, p in enumerate(others):
        go(rcopy(xe.at[:, rows(p)], gx.at[t, 1:3], xs.at[i], xr.at[t, 0], P_.dev(p)))
    gatt = dot_nt(ga[:, 0:512], pack_v[:, :, WO : WO + 512].reshape(1024, 512))
    gatt += dot_nt(ga[:, 512:1024], pack_v[:, :, WO + 512 : WO + 1024].reshape(1024, 512))
    gq[:, 0:1024] = gatt.astype(BF)
    n1t[...] = jnp.transpose(n1[...])
    gacc[...] = jnp.zeros_like(gacc)
    allowed = masks(len_ref[0])
    sum_a.step2(0)

    def pair_step(p, carry):
        lo = pl.ds(pl.multiple_of(p * 128, 128), 128)
        mid = pl.ds(pl.multiple_of(1024 + p * 128, 128), 128)
        hi = pl.ds(pl.multiple_of(2048 + p * 128, 128), 128)
        q2, k2, v2, do = qkv[:, lo], qkv[:, mid], qkv[:, hi], gq[:, lo]
        dq = dk = dv = None
        for hh in range(2):
            mine = lane // 64 == hh
            zero = jnp.zeros_like(q2)
            qm, km, dm = (jnp.where(mine, v, zero) for v in (q2, k2, do))
            total = jnp.sum(jnp.where(lane == 2 * p + hh, lse[...], 0.0), axis=-1, keepdims=True)
            sc = dot_nt(qm, k2) * 0.125
            pf = jnp.where(allowed, jnp.exp(sc - total), 0.0)
            gp = dot_nt(dm, v2)
            ds = (pf * (gp - jnp.sum(pf * gp, axis=-1, keepdims=True))).astype(BF)
            terms = (dot_nn(ds, km), dot_tn(ds, qm), dot_tn(pf.astype(BF), dm))
            dq, dk, dv = terms if hh == 0 else (dq + terms[0], dk + terms[1], dv + terms[2])
        gq[:, lo] = (dq * 0.125).astype(BF)
        gq[:, mid] = (dk * 0.125).astype(BF)
        gq[:, hi] = dv.astype(BF)
        return carry

    def chunk_step(j, carry):
        lax.fori_loop(2 * j, 2 * j + 2, pair_step, 0)
        for seg in range(3):
            cols = pl.ds(pl.multiple_of(seg * 1024 + j * 256, 256), 256)
            gcols = gq[:, cols]
            put(gb_, j, slice(seg * 256, (seg + 1) * 256), dot_nn(n1t[...], gcols))
            gacc[...] += dot_nt(gcols, pack_v[:, :, cols].reshape(1024, 256))
        sum_b.step1(j)

        @pl.when(j == 0)
        def _():
            zsum.transit(0)
            sum_a.step3(0)

        @pl.when(j == 1)
        def _():
            sum_a.step4(0)

        @pl.when(j >= 1)
        def _():
            sum_b.step2(j - 1)

        @pl.when(j >= 2)
        def _():
            sum_b.step3(j - 2)

        @pl.when(j >= 3)
        def _():
            sum_b.step4(j - 3)

        return carry

    lax.fori_loop(0, 4, chunk_step, 0)
    gn1 = gacc[...]
    n_one, r_one = norm_parts(tok[...].astype(F32))
    gain_one_row = jnp.sum(gn1 * n_one, axis=0, keepdims=True)
    rowi = lax.broadcasted_iota(jnp.int32, (8, 1024), 0)
    rws = jnp.where(rowi == 0, gain_one_row, jnp.where(rowi == 1, gain_two_row, 0.0)).astype(BF)
    sel = (
        lax.broadcasted_iota(jnp.int32, (8, 128), 1) == lax.broadcasted_iota(jnp.int32, (8, 128), 0) + 2
    ).astype(BF)
    put(gc_, 0, slice(0, 128), dot_tn(nt[...], two) + dot_tn(rws, sel))
    sum_c.step1(0)
    sum_b.step2(3)
    sum_b.step3(2)
    sum_c.step2(0)
    gtok[...] += norm_back(gn1, row_of(extra, 2), n_one, r_one)
    sum_b.step3(3)
    sum_b.step4(1)
    sum_c.step3(0)

    zsum.arrived(0)
    gacc[0:256, 0:512] = gin[0, z].astype(F32) + rin[0, 0].astype(F32) + rin[0, 1].astype(F32)
    gdd[...] = gdn[0, z].astype(F32) + rdn[0, 0].astype(F32) + rdn[0, 1].astype(F32)

    @pl.when(mid)
    def _():
        gacc[0:256, 0:512] += rin[0, 2].astype(F32)
        gdd[...] += rdn[0, 2].astype(F32)

    gin[0, z] = gacc[0:256, 0:512].astype(BF)
    lx = pltpu.make_async_copy(gin.at[:, z, rows(own)], gx.at[t, 0:1], lsem.at[4])
    lx.start()
    for i, p in enumerate(others):
        go(rcopy(gin.at[:, z, rows(p)], gx.at[t, 0:1], xs.at[7 + i], xr.at[t, 1], P_.dev(p)))

    sum_b.step4(2)
    sum_b.step4(3)
    sum_c.step4(0)
    rcopy(bnext, bin_, bs.at[0], bs.at[1], P_.dev(sib)).wait_recv()
    b_in = pltpu.make_async_copy(bown, nt, lsem.at[6])
    b_in.start()
    b_in.wait()
    keep = (lax.broadcasted_iota(jnp.int32, (384, 1), 0) < len_ref[0]).astype(F32)
    block[...] = ((s2[...] + (nt[...].astype(F32) + bin_[...].astype(F32))) * keep).astype(BF)
    gwo[...] = sum_a.step5(0)
    for j in range(4):
        total = sum_b.step5(j)
        for seg in range(3):
            at = seg * 1024 + j * 256
            gqkv[:, at : at + 256] = total[:, seg * 256 : (seg + 1) * 256]
    gex[...] = sum_c.step5(0)
    for p in others:
        r = P_.rank(p)
        rcopy(xe.at[:, rows(own)], gx.at[r, 1:3], xs.at[0], xr.at[r, 0], P_.dev(sib)).wait_recv()
        rcopy(gin.at[:, 0, rows(own)], gx.at[r, 0:1], xs.at[0], xr.at[r, 1], P_.dev(sib)).wait_recv()
    le.wait()
    lx.wait()
    for r in range(8):
        for zz in range(4):
            to = slice((zz * 8 + r) * 128, (zz * 8 + r + 1) * 128)
            at = slice(zz * 128, (zz + 1) * 128)
            gwi[:, to] = gx[r, 0, :, at].astype(F32)
            gwe[:, :, to] = gx[r, 1:3, :, at].astype(F32)
    zsum.sent(0)
    sum_a.sent(0)
    for j in range(4):
        sum_b.sent(j)
    sum_c.sent(0)
    for cp in sends:
        cp.wait_send()


def run_back(*args):
    sd = jax.ShapeDtypeStruct
    dma = pltpu.SemaphoreType.DMA
    sizes = ((1, 1024), (4, 768), (1, 128))
    blocks = [pltpu.VMEM((n, 8, 4, 32, w), BF) for n, w in sizes]
    for n, w in sizes:
        blocks += [
            pltpu.VMEM((n, 4, 4, 32, w), BF), pltpu.VMEM((n, 3, 4, 32, w), BF), pltpu.VMEM((n, 4, 32, w), BF),
        ]
    sems = []
    for n, _ in sizes:
        sems += [dma((n, 4)), dma((n, 4)), dma((n, 3)), dma((n, 3)), dma((n, 4)), dma((n, 4))]
    return pl.pallas_call(
        back_kernel,
        out_shape=(
            sd((384, 1024), BF), sd((384, 1024), F32), sd((32, 3072), F32), sd((32, 1024), F32),
            sd((32, 128), F32), sd((128, 1024), F32), sd((2, 128, 1024), F32), sd((32, 4096), F32),
            sd((2, 32, 4096), F32),
        ),
        in_specs=[SM] + [VM] * 8 + [ANY] * 11,
        out_specs=(VM,) * 9,
        scratch_shapes=[
            pltpu.VMEM((8, 3, 32, 512), BF), pltpu.VMEM((400, 1024), BF), pltpu.VMEM((384, 1024), BF),
            pltpu.VMEM((384, 1024), BF), pltpu.VMEM((2, 256, 512), BF), pltpu.VMEM((2, 3, 256, 512), BF),
            pltpu.VMEM((2, 3, 128, 1024), BF), pltpu.VMEM((2, 128, 1024), BF),
            pltpu.VMEM((32, 32, PW), BF), pltpu.VMEM((384, 3072), BF), pltpu.VMEM((384, 1024), F32),
            pltpu.VMEM((1024, 384), BF), *blocks,
            pltpu.VMEM((1, 4, 256, 512), BF), pltpu.VMEM((1, 4, 128, 1024), BF),
            pltpu.VMEM((1, 3, 256, 512), BF), pltpu.VMEM((1, 3, 128, 1024), BF),
            pltpu.VMEM((1, 256, 512), BF), pltpu.VMEM((1, 128, 1024), BF),
            *sems, dma((1, 8)), dma((1, 8)), dma((14,)), dma((8, 2)), dma((2,)),
            dma((12,)),
        ],
        compiler_params=pltpu.CompilerParams(
            collective_id=2, has_side_effects=True, vmem_limit_bytes=63 * MIB
        ),
    )(*args)


def leave_kernel(*refs):
    n = 8
    srcs, gex, dsts, rows = refs[:n], refs[n], refs[n + 1 : 2 * n + 1], refs[2 * n + 1]
    bufs, sin, sout = refs[2 * n + 2 : 3 * n + 2], refs[3 * n + 2], refs[3 * n + 3]
    ins = [pltpu.make_async_copy(s, v, sin.at[i]) for i, (s, v) in enumerate(zip(srcs, bufs))]
    outs = [pltpu.make_async_copy(v, d, sout.at[i]) for i, (v, d) in enumerate(zip(bufs, dsts))]
    for cp in ins:
        cp.start()
    rows[...] = jnp.transpose(jnp.concatenate([gex[...]] * 4, axis=0))[0:8]
    for a, b in zip(ins, outs):
        a.wait()
        b.start()
    for cp in outs:
        cp.wait()


def run_leave(arrays, gex):
    shapes = [jax.ShapeDtypeStruct(a.shape, a.dtype) for a in arrays]
    return pl.pallas_call(
        leave_kernel,
        out_shape=(*shapes, jax.ShapeDtypeStruct((8, 128), F32)),
        in_specs=[ANY] * 8 + [VM],
        out_specs=(ANY,) * 8 + (VM,),
        scratch_shapes=[
            *(pltpu.VMEM(a.shape, a.dtype) for a in arrays),
            pltpu.SemaphoreType.DMA((8,)), pltpu.SemaphoreType.DMA((8,)),
        ],
        compiler_params=pltpu.CompilerParams(vmem_limit_bytes=63 * MIB),
    )(*arrays, gex)


def fused_device(
    tokens, cotangent, lengths, expert_ids, slot_ids, w_qkv, w_out, gain_one, w_in, w_down,
    w_expert_in, w_expert_out, w_mix, gain_two,
):
    table = jnp.where(slot_ids >= 0, expert_ids * CAP + slot_ids, -1).astype(F32)
    small = jnp.concatenate([w_mix.T, gain_one[None], gain_two[None]], axis=0)
    qkv, lse, att, s2, n1, wmix, pack_all, wi_all, wd_all, g_all, nt_all = run_enter(
        lengths, tokens, cotangent, table.reshape(1, 384),
        w_qkv, w_out, small, w_in, w_expert_in, w_down, w_expert_out,
    )
    gsum, gl, *rest = run_ff(nt_all, wmix.reshape(1024, 128), g_all, wi_all, wd_all)
    block, gtok, gqkv, gwo, gex, gdd, gde, gwi, gwe = run_back(
        lengths, tokens, s2, n1, qkv, lse, att, gsum, gl, g_all, nt_all, pack_all, *rest
    )
    *big, rows = run_leave((block, gtok, gqkv, gwo, gwi, gdd, gwe, gde), gex)
    block, gtok, gqkv, gwo, gwi, gdd, gwe, gde = big
    return (
        block, gtok, gqkv, gwo, rows[2, 0:32], gwi, gdd, gwe, gde, rows[0:2, 0:32].T, rows[3, 0:32],
    )


def solution(mesh):
    placed = (
        P(("dp", "fsdp"), None),
        P(("dp", "fsdp"), None),
        P(("dp", "fsdp")),
        P(("dp", "fsdp")),
        P(("dp", "fsdp")),
        P(("dp", "fsdp"), None),
        P(("dp", "fsdp"), None),
        P(("dp", "fsdp")),
        P(("dp", "fsdp"), None),
        P(("dp", "fsdp"), None),
        P(None, ("dp", "fsdp"), None),
        P(None, ("dp", "fsdp"), None),
        P(("dp", "fsdp"), None),
        P(("dp", "fsdp")),
    )
    fused = (mesh.shape["dp"], mesh.shape["fsdp"]) == (8, 4)
    return jax.shard_map(
        fused_device if fused else per_device,
        mesh=mesh,
        in_specs=placed,
        out_specs=(
            P(("dp", "fsdp"), None),
            P(("dp", "fsdp"), None),
            P(("dp", "fsdp"), None),
            P(("dp", "fsdp"), None),
            P(("dp", "fsdp")),
            P(("dp", "fsdp"), None),
            P(("dp", "fsdp"), None),
            P(None, ("dp", "fsdp"), None),
            P(None, ("dp", "fsdp"), None),
            P(("dp", "fsdp"), None),
            P(("dp", "fsdp")),
        ),
        check_vma=False,
    )
```
